256 devices in a mesh: pool: 32 (over x, z), tp: 8 (over y, core).
Axes of the slice: x: 4, y: 4, z: 8, core: 2. Of those that a mesh axis runs over, the one named last changes fastest.
Arguments:
- hidden_rows: bfloat16 [512, 16384], P('pool', 'tp'), may hold values from -6 to 6
- queries: bfloat16 [512, 16384], P('pool', 'tp'), may hold values from -64 to 64
- cache_keys: bfloat16 [512, 128, 1024], P('pool', None, 'tp'), may hold values from -64 to 64
- cache_values: bfloat16 [512, 128, 1024], P('pool', None, 'tp'), may hold values from -6 to 6
- new_keys: bfloat16 [512, 1024], P('pool', 'tp'), may hold values from -6 to 6
- new_values: bfloat16 [512, 1024], P('pool', 'tp'), may hold values from -6 to 6
- lengths: int32 [512], P('pool'), may hold values from 2 to 128, as said below
- norm_gain: bfloat16 [16384], P('tp'), may hold values from 0.099609375 to 1.8984375
- w_gate: bfloat16 [16384, 28672], P('tp', 'pool'), may hold values from -0.046875 to 0.046875
- w_up: bfloat16 [16384, 28672], P('tp', 'pool'), may hold values from -0.046875 to 0.046875
- w_down: bfloat16 [28672, 16384], P('pool', 'tp'), may hold values from -0.03125 to 0.03125
Outputs:
- layer_out: bfloat16 [512, 16384], P('pool', 'tp')
The draws below stay inside these ranges and needn't reach their ends.
Inputs may be any that keep to these rules, and one draw needn't show every extreme that they name: `lengths`: every draw has a request with all 128 slots live.
All inputs are finite; a program needn't handle non-finite values.
Results may differ from the reference program's by a relative error of at most 0.007.
Values may be sent and summed in bfloat16 or wider, within the bound.
No kernel may reach another device: no remote copies, remote signals or barrier semaphores. Data moves between devices by JAX's collectives and lax.ppermute only.
A program may use at most 64 MiB of HBM per device.

```python
import jax
import jax.numpy as jnp
from jax import lax

REQ_DEV = 16
CTX = 128
D = 16384
HEADS = 128
KV_HEADS = 8
HEAD_DIM = 128
REQ = 512
FF = 28672


def draw_queries(key, part):
    key = jax.random.fold_in(key, 11)
    base = 0.5 * jnp.clip(jax.random.normal(key, (REQ, HEADS, HEAD_DIM), jnp.float32), -6.0, 6.0)
    return base.reshape(REQ, HEADS * HEAD_DIM).astype(jnp.bfloat16)


def draw_cache_keys(key, part):
    key = jax.random.fold_in(key, 23)
    base = jnp.clip(jax.random.normal(key, (REQ, CTX, KV_HEADS, HEAD_DIM), jnp.float32), -6.0, 6.0)
    return base.reshape(REQ, CTX, KV_HEADS * HEAD_DIM).astype(jnp.bfloat16)


def draw_lengths(key, part):
    key = jax.random.fold_in(key, 37)
    first, second = jax.random.split(key)
    raw = jax.random.randint(first, (REQ,), 0, 1 << 20, jnp.int32)
    level = jax.random.randint(second, (REQ // REQ_DEV,), 0, 3, jnp.int32)
    caps = jnp.where(level == 0, CTX // 4, jnp.where(level == 1, CTX // 2, CTX))
    caps = jnp.maximum(jnp.repeat(caps, REQ_DEV), 2)
    lengths = 2 + raw % (caps - 1)
    return lengths.at[0].set(CTX).astype(jnp.int32)


def levels(rng, shape, cuts, least, top_value):
    level = 1.0
    for axis_at, blocks in cuts:
        steps = jax.random.uniform(jax.random.fold_in(jax.random.fold_in(rng, 6), axis_at), (blocks,), jnp.float32, least / len(cuts), top_value / len(cuts))
        level = level * jnp.repeat(jnp.exp(steps), shape[axis_at] // blocks).reshape((-1,) + (1,) * (len(shape) - 1 - axis_at))
    return level


def scatter_about(key, extent, spread, limit, cuts=(), kind=jnp.bfloat16):
    values = spread * jax.random.normal(key, extent, jnp.float32)
    if cuts:
        values = values * levels(key, extent, cuts, -0.22, 0.18)
    return jnp.clip(values, -limit, limit).astype(kind)


def setup_inputs(seed: int = 0) -> dict:
    streams_of = jax.random.split(jax.random.key(seed), 12)
    hidden_rows = scatter_about(streams_of[0], (REQ, D), 1.0, 6.0, ((0, 32), (1, 8)))
    queries = draw_queries(jax.random.fold_in(streams_of[11], 71), 0)
    cache_keys = draw_cache_keys(jax.random.fold_in(streams_of[11], 71), 0)
    cache_values = scatter_about(streams_of[3], (REQ, CTX, KV_HEADS * HEAD_DIM), 1.0, 6.0, ((0, 32), (2, 8)))
    new_keys = scatter_about(streams_of[4], (REQ, KV_HEADS * HEAD_DIM), 1.0, 6.0, ((0, 32), (1, 8)))
    new_values = scatter_about(streams_of[5], (REQ, KV_HEADS * HEAD_DIM), 1.0, 6.0, ((0, 32), (1, 8)))
    lengths = draw_lengths(jax.random.fold_in(streams_of[11], 71), 0)
    norm_gain = jnp.clip(1.0 + 0.18 * jax.random.normal(streams_of[7], (D,), jnp.float32), 0.099609375, 1.8984375).astype(jnp.bfloat16)
    w_gate = scatter_about(streams_of[8], (D, FF), D ** -0.5, 0.046875, ((0, 8), (1, 32)))
    w_up = scatter_about(streams_of[9], (D, FF), D ** -0.5, 0.046875, ((0, 8), (1, 32)))
    w_down = scatter_about(streams_of[10], (FF, D), FF ** -0.5, 0.03125, ((0, 32), (1, 8)))
    return {"hidden_rows": hidden_rows, "queries": queries, "cache_keys": cache_keys, "cache_values": cache_values, "new_keys": new_keys, "new_values": new_values, "lengths": lengths, "norm_gain": norm_gain, "w_gate": w_gate, "w_up": w_up, "w_down": w_down}


def attend(queries, cache_keys, cache_values, new_keys, new_values, lengths):
    rows = queries.shape[0]
    ctx = cache_keys.shape[1]
    groups = cache_keys.shape[2] // HEAD_DIM
    per = queries.shape[1] // HEAD_DIM // groups
    scale = HEAD_DIM ** (-0.5)
    qq = queries.reshape(rows, groups, per, HEAD_DIM).astype(jnp.float32)
    keys = cache_keys.reshape(rows, ctx, groups, HEAD_DIM).astype(jnp.float32)
    vals = cache_values.reshape(rows, ctx, groups, HEAD_DIM).astype(jnp.float32)
    own_key = new_keys.reshape(rows, groups, HEAD_DIM).astype(jnp.float32)
    own_val = new_values.reshape(rows, groups, HEAD_DIM).astype(jnp.float32)
    scores = jnp.einsum('rgjd,rcgd->rgjc', qq, keys) * scale
    own = jnp.einsum('rgjd,rgd->rgj', qq, own_key) * scale
    live = (jnp.arange(ctx, dtype=jnp.int32)[None, :] < lengths[:, None])[:, None, None, :]
    scores = jnp.where(live, scores, jnp.float32(-1e+30))
    top = jnp.maximum(lax.optimization_barrier(jnp.max(scores, axis=-1)), own)
    weights = jnp.where(live, jnp.exp(scores - top[..., None]), jnp.float32(0.0))
    own_weight = jnp.exp(own - top)
    total = lax.optimization_barrier(jnp.sum(weights, axis=-1)) + own_weight
    low = weights.astype(jnp.bfloat16).astype(jnp.float32)
    own_low = own_weight.astype(jnp.bfloat16).astype(jnp.float32)
    mixed = jnp.einsum('rgjc,rcgd->rgjd', low, vals) + own_low[..., None] * own_val[:, :, None, :]
    return (mixed / total[..., None]).reshape(rows, groups * per * HEAD_DIM)

def reference(hidden_rows, queries, cache_keys, cache_values, new_keys, new_values, lengths, norm_gain, w_gate, w_up, w_down):
    readout = attend(queries, cache_keys, cache_values, new_keys, new_values, lengths)
    stream = hidden_rows.astype(jnp.float32) + readout
    meansq = lax.optimization_barrier(jnp.mean(stream * stream, axis=1))
    normed = (stream * jax.lax.rsqrt(meansq + 1e-05)[:, None] * norm_gain.astype(jnp.float32)[None, :]).astype(jnp.bfloat16)
    gate = jnp.dot(normed, w_gate, preferred_element_type=jnp.float32)
    up = jnp.dot(normed, w_up, preferred_element_type=jnp.float32)
    hidden = (jax.nn.silu(gate) * up).astype(jnp.bfloat16)
    ffn = jnp.dot(hidden, w_down, preferred_element_type=jnp.float32)
    return (stream + ffn).astype(jnp.bfloat16)
```

```python
import jax
import jax.numpy as jnp
from jax import lax
from jax.sharding import Mesh
from jax.sharding import PartitionSpec as P

D = 16384
HEAD_DIM = 128
NX, NZ, NT = 4, 8, 8
CHUNKS = ((0, 1, -1, 2), (-2, 3, -3, 4))
TP = ("y", "core")


def attend_local(queries, cache_keys, cache_values, new_keys, new_values, lengths):
    rows = queries.shape[0]
    ctx = cache_keys.shape[1]
    groups = cache_keys.shape[2] // HEAD_DIM
    per = queries.shape[1] // HEAD_DIM // groups
    scale = HEAD_DIM ** (-0.5)
    query_heads = queries.reshape(rows, groups, per, HEAD_DIM)
    keys = cache_keys.reshape(rows, ctx, groups, HEAD_DIM)
    values = cache_values.reshape(rows, ctx, groups, HEAD_DIM)
    own_key = new_keys.reshape(rows, groups, HEAD_DIM)
    own_val = new_values.reshape(rows, groups, HEAD_DIM).astype(jnp.float32)
    scores = (
        jnp.einsum("rgjd,rcgd->rgjc", query_heads, keys, preferred_element_type=jnp.float32) * scale
    )
    own = (
        jnp.einsum("rgjd,rgd->rgj", query_heads, own_key, preferred_element_type=jnp.float32)
        * scale
    )
    live = (jnp.arange(ctx, dtype=jnp.int32)[None, :] < lengths[:, None])[:, None, None, :]
    scores = jnp.where(live, scores, jnp.float32(-1e30))
    top = jnp.maximum(jnp.max(scores, axis=-1), own)
    weights = jnp.where(live, jnp.exp(scores - top[..., None]), jnp.float32(0.0))
    own_weight = jnp.exp(own - top)
    total = jnp.sum(weights, axis=-1) + own_weight
    low = weights.astype(jnp.bfloat16)
    own_low = own_weight.astype(jnp.bfloat16).astype(jnp.float32)
    mixed = jnp.einsum("rgjc,rcgd->rgjd", low, values, preferred_element_type=jnp.float32)
    mixed = mixed + own_low[..., None] * own_val[:, :, None, :]
    return (mixed / total[..., None]).reshape(rows, groups * per * HEAD_DIM)


def shift(v, axis, by, n):
    return lax.ppermute(v, axis, [(i, (i + by) % n) for i in range(n)])


def gather(v, axis, n):
    return lax.all_to_all(jnp.broadcast_to(v[None], (n,) + v.shape), axis, 0, 0)


def shards(
    hidden_rows,
    queries,
    cache_keys,
    cache_values,
    new_keys,
    new_values,
    lengths,
    norm_gain,
    w_gate,
    w_up,
    w_down,
):
    f32, bf16 = jnp.float32, jnp.bfloat16
    rows, feats = hidden_rows.shape
    width = w_gate.shape[1]
    readout = attend_local(queries, cache_keys, cache_values, new_keys, new_values, lengths)
    stream = hidden_rows.astype(f32) + readout
    gain = norm_gain.astype(f32)
    scaled = (stream * gain[None, :]).astype(bf16)
    inv_gain2 = 1.0 / (gain * gain)

    own = gather(scaled, "x", NX)
    pieces = {0: own}
    right = left = own
    for step in range(1, NZ // 2 + 1):
        left = shift(left, "z", -1, NZ)
        pieces[step] = left
        if step < NZ // 2:
            right = shift(right, "z", 1, NZ)
            pieces[-step] = right

    back = {}
    for chunk in CHUNKS:
        part = jnp.stack([pieces[j] for j in chunk], axis=1).reshape(-1, feats)
        total = part.shape[0]
        wide = part.astype(f32)
        squares = jnp.sum(wide * wide * inv_gain2[None, :], axis=1)
        high = squares.astype(bf16)
        low = (squares - high.astype(f32)).astype(bf16)
        marks = jnp.stack([high, low], axis=1)
        marks = jnp.pad(marks, ((0, 0), (0, 126)))
        gate = jnp.dot(part, w_gate, preferred_element_type=f32).astype(bf16)
        up = jnp.dot(part, w_up, preferred_element_type=f32).astype(bf16)
        sums = jnp.concatenate([gate, up, marks], axis=1).reshape(NT, total // NT, -1)
        sums = lax.all_to_all(sums, TP, 0, 0)
        sums = jnp.sum(sums.astype(f32), axis=0)
        meansq = (sums[:, 2 * width] + sums[:, 2 * width + 1]) / D
        inv = lax.rsqrt(meansq + 1e-05)[:, None]
        hidden = (jax.nn.silu(sums[:, :width] * inv) * (sums[:, width : 2 * width] * inv)).astype(bf16)
        hidden = gather(hidden, TP, NT).reshape(total, width)
        terms = jnp.dot(hidden, w_down, preferred_element_type=f32).astype(bf16)
        terms = lax.all_to_all(terms.reshape(NX, total // NX, feats), "x", 0, 0)
        terms = jnp.sum(terms.astype(f32), axis=0).astype(bf16).reshape(len(chunk), rows, feats)
        for i, j in enumerate(chunk):
            back[j] = shift(terms[i], "z", j, NZ) if j else terms[i]
    ffn = sum(v.astype(f32) for v in back.values())
    return (stream + ffn).astype(bf16)


def solution(mesh):
    fine = Mesh(mesh.devices.reshape(NX, NZ, 4, 2), ("x", "z", "y", "core"))
    pool = ("x", "z")
    placed = (
        P(pool, TP),
        P(pool, TP),
        P(pool, None, TP),
        P(pool, None, TP),
        P(pool, TP),
        P(pool, TP),
        P(pool),
        P(TP),
        P(TP, pool),
        P(TP, pool),
        P(pool, TP),
    )
    return jax.shard_map(shards, mesh=fine, in_specs=placed, out_specs=P(pool, TP), check_vma=False)
```

```python
import functools

import jax
import jax.numpy as jnp
from jax import lax
from jax.experimental import pallas as pl
from jax.experimental.pallas import tpu as pltpu
from jax.sharding import Mesh
from jax.sharding import PartitionSpec as P

D = 16384
HEAD_DIM = 128
NX, NZ, NY, NC = 4, 8, 4, 2
TP = ("y", "core")
MARKS = 128
MIB = 1 << 20


def attend_local(queries, cache_keys, cache_values, new_keys, new_values, lengths):
    rows = queries.shape[0]
    ctx = cache_keys.shape[1]
    groups = cache_keys.shape[2] // HEAD_DIM
    per = queries.shape[1] // HEAD_DIM // groups
    scale = HEAD_DIM ** (-0.5)
    query_heads = queries.reshape(rows, groups, per, HEAD_DIM)
    keys = cache_keys.reshape(rows, ctx, groups, HEAD_DIM)
    values = cache_values.reshape(rows, ctx, groups, HEAD_DIM)
    own_key = new_keys.reshape(rows, groups, HEAD_DIM)
    own_val = new_values.reshape(rows, groups, HEAD_DIM).astype(jnp.float32)
    scores = (
        jnp.einsum("rgjd,rcgd->rgjc", query_heads, keys, preferred_element_type=jnp.float32) * scale
    )
    own = (
        jnp.einsum("rgjd,rgd->rgj", query_heads, own_key, preferred_element_type=jnp.float32)
        * scale
    )
    live = (jnp.arange(ctx, dtype=jnp.int32)[None, :] < lengths[:, None])[:, None, None, :]
    scores = jnp.where(live, scores, jnp.float32(-1e30))
    top = jnp.maximum(jnp.max(scores, axis=-1), own)
    weights = jnp.where(live, jnp.exp(scores - top[..., None]), jnp.float32(0.0))
    own_weight = jnp.exp(own - top)
    total = jnp.sum(weights, axis=-1) + own_weight
    low = weights.astype(jnp.bfloat16)
    own_low = own_weight.astype(jnp.bfloat16).astype(jnp.float32)
    mixed = jnp.einsum("rgjc,rcgd->rgjd", low, values, preferred_element_type=jnp.float32)
    mixed = mixed + own_low[..., None] * own_val[:, :, None, :]
    return (mixed / total[..., None]).reshape(rows, groups * per * HEAD_DIM)


def shift(v, axis, by, n):
    return lax.ppermute(v, axis, [(i, (i + by) % n) for i in range(n)])


def rows_at(start, count):
    return pl.ds(pl.multiple_of(start, count), count)


def call(kernel, outs, args, kinds, scratch=(), flops=0, moved=0, limit=16 * MIB):
    spaces = {"s": pltpu.SMEM, "v": pltpu.VMEM, "h": pl.ANY}
    single = not isinstance(outs, (list, tuple))
    whole = [outs] if single else list(outs)
    got = pl.pallas_call(
        kernel,
        out_shape=whole,
        in_specs=[pl.BlockSpec(memory_space=spaces[k]) for k in kinds],
        out_specs=[pl.BlockSpec(memory_space=pltpu.VMEM)] * len(whole),
        scratch_shapes=list(scratch),
        compiler_params=pltpu.CompilerParams(vmem_limit_bytes=limit),
        cost_estimate=pl.CostEstimate(flops=flops, bytes_accessed=moved, transcendentals=0),
    )(*args)
    return got[0] if single else got


def shape(*dims, kind=jnp.bfloat16):
    return jax.ShapeDtypeStruct(dims, kind)


def first_matmul(rows, width, *refs):
    idx, rest = refs[0], refs[1:]
    along_z, rest = rest[:NZ], rest[NZ:]
    along_x, rest = rest[:NX], rest[NX:]
    inv_gain2, w_gate, w_up, keep, send, part, weights, sems = rest
    half = part.shape[1] // 2
    mine_x, mine_z, core = idx[0], idx[1], idx[3]
    copies = [
        pltpu.make_async_copy(w_gate, weights.at[:, pl.ds(0, width)], sems.at[0]),
        pltpu.make_async_copy(w_up, weights.at[:, pl.ds(width, width)], sems.at[1]),
    ]
    for copy in copies:
        copy.start()
    block = NX * rows
    for j in range(NZ):
        z = lax.rem(mine_z - j + NZ + NZ // 2 * core, NZ)
        for k in range(NX):
            x = lax.rem(mine_x - k + NX, NX)
            part[rows_at(z * block + x * rows, rows), pl.ds(0, half)] = along_z[j][pl.ds(k * rows, rows), :]
    for k in range(NX):
        x = lax.rem(mine_x - k + NX, NX)
        for z in range(NZ):
            at = lax.rem(z + NZ // 2 * core, NZ)
            part[rows_at(at * block + x * rows, rows), pl.ds(half, half)] = along_x[k][pl.ds(z * rows, rows), :]
    total = part.shape[0]
    top = total // 2
    step = 64
    lane = lax.broadcasted_iota(jnp.int32, (step, MARKS), 1)

    def squares(i, out, base):
        wide = part[rows_at(base + i * step, step), :].astype(jnp.float32)
        sums = jnp.sum(wide * wide * inv_gain2[...], axis=1, keepdims=True)
        high = sums.astype(jnp.bfloat16).astype(jnp.float32)
        marks = jnp.where(lane == 0, high, jnp.where(lane == 1, sums - high, 0.0))
        out[rows_at(i * step, step), pl.ds(2 * width, MARKS)] = marks.astype(jnp.bfloat16)

    pl.loop(0, top // step)(lambda i: squares(i, keep, 0))
    pl.loop(0, top // step)(lambda i: squares(i, send, top))
    copies[0].wait()
    copies[1].wait()

    @pl.loop(0, 2 * width // 256)
    def _(t):
        cols = pl.ds(pl.multiple_of(t * 256, 256), 256)
        terms = jnp.dot(part[...], weights[:, cols], preferred_element_type=jnp.float32)
        keep[:, cols] = terms[:top].astype(jnp.bfloat16)
        send[:, cols] = terms[top:].astype(jnp.bfloat16)


def core_sum(block, idx, keep, came, own, *outs):
    mine = idx[2]

    def summed(y):
        at = rows_at(y * block, block)
        return keep[at, :].astype(jnp.float32) + came[at, :].astype(jnp.float32)

    own[...] = summed(mine)
    for k, out in enumerate(outs, 1):
        out[...] = summed(lax.rem(mine + k, NY)).astype(jnp.bfloat16)


def activate(width, own, one, two, three, hidden):
    sums = own[...] + one[...].astype(jnp.float32) + two[...].astype(jnp.float32) + three[...].astype(jnp.float32)
    meansq = jnp.sum(sums[:, 2 * width :], axis=1, keepdims=True) / D
    inv = lax.rsqrt(meansq + 1e-05)
    gate = sums[:, :width] * inv
    up = sums[:, width : 2 * width] * inv
    hidden[...] = (gate / (1.0 + jnp.exp(-gate)) * up).astype(jnp.bfloat16)


def second_matmul(rows, *refs):
    idx, rest = refs[0], refs[1:]
    same, rest = rest[:NY], rest[NY:]
    other, rest = rest[:NY], rest[NY:]
    w_down, rest = rest[0], rest[1:]
    by_z, rest = rest[:NZ], rest[NZ:]
    by_x, rest = rest[:NX], rest[NX:]
    hidden, weights, terms, sem = rest
    mine_x, mine_z, mine_y, core = idx[0], idx[1], idx[2], idx[3]
    copy = pltpu.make_async_copy(w_down, weights, sem)
    copy.start()
    block = NX * rows
    for k in range(NY):
        y = lax.rem(mine_y - k + NY, NY)
        hidden[rows_at((NY * core + y) * block, block), :] = same[k][...]
        hidden[rows_at((NY * (1 - core) + y) * block, block), :] = other[k][...]
    copy.wait()
    feats = weights.shape[1]

    @pl.loop(0, feats // 256)
    def _(t):
        cols = pl.ds(pl.multiple_of(t * 256, 256), 256)
        terms[:, cols] = jnp.dot(hidden[...], weights[:, cols], preferred_element_type=jnp.float32).astype(jnp.bfloat16)

    half = feats // 2
    for j in range(NZ):
        z = lax.rem(mine_z + j, NZ)
        by_z[j][...] = terms[rows_at(z * block, block), pl.ds(0, half)]
    for k in range(NX):
        x = lax.rem(mine_x + k, NX)
        for z in range(NZ):
            by_x[k][pl.ds(z * rows, rows), :] = terms[rows_at(z * block + x * rows, rows), pl.ds(half, half)]


def z_sum(rows, idx, own, up, down, mine, *outs):
    at_x = idx[0]

    def summed(x):
        at = rows_at(x * rows, rows)
        return own[at, :].astype(jnp.float32) + up[at, :].astype(jnp.float32) + down[at, :].astype(jnp.float32)

    mine[...] = summed(at_x)
    for k, out in enumerate(outs, 1):
        out[...] = summed(lax.rem(at_x + k, NX)).astype(jnp.bfloat16)


def shards(
    hidden_rows,
    queries,
    cache_keys,
    cache_values,
    new_keys,
    new_values,
    lengths,
    norm_gain,
    w_gate,
    w_up,
    w_down,
):
    f32, bf16 = jnp.float32, jnp.bfloat16
    rows, feats = hidden_rows.shape
    width = w_gate.shape[1]
    half = feats // 2
    total = rows * NX * NZ
    block = rows * NX
    wide = 2 * width + MARKS
    idx = jnp.stack([lax.axis_index(a) for a in ("x", "z", "y", "core")]).astype(jnp.int32)
    readout = attend_local(queries, cache_keys, cache_values, new_keys, new_values, lengths)
    stream = hidden_rows.astype(f32) + readout
    gain = norm_gain.astype(f32)
    scaled = (stream * gain[None, :]).astype(bf16)
    inv_gain2 = (1.0 / (gain * gain))[None, :]

    left, right = scaled[:, :half], scaled[:, half:]
    wait_z = lax.all_to_all(jnp.broadcast_to(right[None], (NZ,) + right.shape), "z", 0, 0)
    own = jnp.concatenate([left] + [shift(left, "x", k, NX) for k in range(1, NX)], axis=0)
    along_z = {0: own}
    up = down = own
    for step in range(1, NZ // 2 + 1):
        up = shift(up, "z", 1, NZ)
        along_z[step] = up
        if step < NZ // 2:
            down = shift(down, "z", -1, NZ)
            along_z[NZ - step] = down
    right = wait_z.reshape(NZ * rows, half)
    along_x = [right] + [shift(right, "x", k, NX) for k in range(1, NX)]

    keep, send = call(
        functools.partial(first_matmul, rows, width),
        [shape(total // 2, wide)] * 2,
        [idx] + [along_z[j] for j in range(NZ)] + along_x + [inv_gain2, w_gate, w_up],
        "s" + "v" * (NZ + NX + 1) + "hh",
        scratch=[
            pltpu.VMEM((total, feats), bf16),
            pltpu.VMEM((feats, 2 * width), bf16),
            pltpu.SemaphoreType.DMA((2,)),
        ],
        flops=4 * total * feats * width,
        moved=4 * feats * width,
        limit=28 * MIB,
    )
    came = shift(send, "core", 1, NC)
    own, *parts = call(
        functools.partial(core_sum, block),
        [shape(block, wide, kind=f32)] + [shape(block, wide)] * (NY - 1),
        [idx, keep, came],
        "svv",
        moved=4 * total * wide,
    )
    parts = [shift(v, "y", k, NY) for k, v in enumerate(parts, 1)]
    hidden = call(functools.partial(activate, width), shape(block, width), [own] + parts, "vvvv", moved=10 * block * wide)
    same = [hidden] + [shift(hidden, "y", k, NY) for k in range(1, NY)]
    other = [shift(v, "core", 1, NC) for v in same]
    blocks = call(
        functools.partial(second_matmul, rows),
        [shape(block, half)] * NZ + [shape(NZ * rows, half)] * NX,
        [idx] + same + other + [w_down],
        "s" + "v" * 2 * NY + "h",
        scratch=[
            pltpu.VMEM((total, width), bf16),
            pltpu.VMEM((width, feats), bf16),
            pltpu.VMEM((total, feats), bf16),
            pltpu.SemaphoreType.DMA(()),
        ],
        flops=2 * total * feats * width,
        moved=2 * feats * width + 2 * total * feats,
        limit=24 * MIB,
    )
    by_z, by_x = blocks[:NZ], blocks[NZ:]

    def add(a, b):
        return (a.astype(f32) + b.astype(f32)).astype(bf16)

    got_x = [shift(by_x[k], "x", k, NX) for k in range(1, NX)]
    up, down = by_z[NZ // 2], by_z[NZ // 2 + 1]
    for step in range(NZ // 2, 0, -1):
        up = shift(up, "z", 1, NZ)
        if step > 1:
            up = add(up, by_z[step - 1])
            down = shift(down, "z", -1, NZ)
            if step > 2:
                down = add(down, by_z[NZ - step + 2])
    sum_x = sum(v.astype(f32) for v in got_x) + by_x[0].astype(f32)
    got_z = lax.all_to_all(sum_x.astype(bf16).reshape(NZ, rows, half), "z", 0, 0)
    mine, *parts = call(
        functools.partial(z_sum, rows),
        [shape(rows, half, kind=f32)] + [shape(rows, half)] * (NX - 1),
        [idx, by_z[0], up, down],
        "svvv",
        moved=8 * block * half,
    )
    parts = [shift(v, "x", k, NX) for k, v in enumerate(parts, 1)]
    left = stream[:, :half] + mine + sum(v.astype(f32) for v in parts)
    right = stream[:, half:] + jnp.sum(got_z.astype(f32), axis=0)
    return jnp.concatenate([left, right], axis=1).astype(bf16)


def solution(mesh):
    fine = Mesh(mesh.devices.reshape(NX, NZ, NY, NC), ("x", "z", "y", "core"))
    pool = ("x", "z")
    placed = (
        P(pool, TP),
        P(pool, TP),
        P(pool, None, TP),
        P(pool, None, TP),
        P(pool, TP),
        P(pool, TP),
        P(pool),
        P(TP),
        P(TP, pool),
        P(TP, pool),
        P(pool, TP),
    )
    return jax.shard_map(shards, mesh=fine, in_specs=placed, out_specs=P(pool, TP), check_vma=False)
```

```python
import functools

import jax
import jax.numpy as jnp
from jax import lax
from jax.experimental import pallas as pl
from jax.experimental.pallas import tpu as pltpu
from jax.sharding import Mesh
from jax.sharding import PartitionSpec as P

D = 16384
HEAD_DIM = 128
NX, NZ, NY, NC = 4, 8, 4, 2
TP = ("y", "core")
MARKS = 128
MIB = 1 << 20
PARTS = 2


def shift(v, axis, by, n):
    return lax.ppermute(v, axis, [(i, (i + by) % n) for i in range(n)])


def rows_at(start, count):
    return pl.ds(pl.multiple_of(start, count), count)


def call(kernel, outs, args, kinds, scratch=(), flops=0, moved=0, limit=16 * MIB):
    spaces = {"s": pltpu.SMEM, "v": pltpu.VMEM, "h": pltpu.HBM}
    single = not isinstance(outs, (list, tuple))
    whole = [outs] if single else list(outs)
    got = pl.pallas_call(
        kernel,
        out_shape=whole,
        in_specs=[pl.BlockSpec(memory_space=spaces[k]) for k in kinds],
        out_specs=[pl.BlockSpec(memory_space=pltpu.VMEM)] * len(whole),
        scratch_shapes=list(scratch),
        compiler_params=pltpu.CompilerParams(vmem_limit_bytes=limit),
        cost_estimate=pl.CostEstimate(flops=flops, bytes_accessed=moved, transcendentals=0),
    )(*args)
    return got[0] if single else got


def shape(*dims, kind=jnp.bfloat16):
    return jax.ShapeDtypeStruct(dims, kind)


def start_rows(scale, lengths, hidden, queries, keys, values, own_keys, own_values, gain, stream, inv_gain2, *rest):
    outs, (heads, mixed) = rest[:PARTS], rest[PARTS:]
    rows, feats = hidden.shape
    per = feats // HEAD_DIM
    ctx = keys.shape[1]
    f32, bf16 = jnp.float32, jnp.bfloat16
    wide = queries[...].astype(f32)
    for h in range(per):
        heads[pl.ds(h, rows, stride=per), :] = wide[:, h * HEAD_DIM : (h + 1) * HEAD_DIM]
    slot = lax.broadcasted_iota(jnp.int32, (per, ctx), 1)
    own_keys = own_keys[...].astype(f32)
    own_values = own_values[...].astype(f32)
    for r in range(rows):
        mine = heads[pl.ds(r * per, per), :]
        live = slot < lengths[r]
        score = lax.dot_general(
            mine.astype(bf16), keys[r], (((1,), (1,)), ((), ())), preferred_element_type=f32
        )
        score = jnp.where(live, score * scale, -1e30)
        own = jnp.sum(mine * own_keys[r : r + 1, :], axis=1, keepdims=True) * scale
        top = jnp.maximum(jnp.max(score, axis=1, keepdims=True), own)
        weight = jnp.where(live, jnp.exp(score - top), 0.0)
        own_weight = jnp.exp(own - top)
        total = jnp.sum(weight, axis=1, keepdims=True) + own_weight
        read = jnp.dot(weight.astype(bf16), values[r], preferred_element_type=f32)
        read = read + own_weight.astype(bf16).astype(f32) * own_values[r : r + 1, :]
        mixed[pl.ds(r * per, per), :] = read / total
    scales = gain[...].astype(f32)
    inv_gain2[...] = 1.0 / (scales * scales)
    count = rows // PARTS
    for h in range(per):
        cols = slice(h * HEAD_DIM, (h + 1) * HEAD_DIM)
        got = hidden[:, cols].astype(f32) + mixed[pl.ds(h, rows, stride=per), :]
        stream[:, cols] = got
        scaled = got * scales[:, cols]
        for p, out in enumerate(outs):
            piece = scaled[p * count : (p + 1) * count, :].astype(bf16)
            for z in range(NZ):
                out[z, :, cols] = piece


def fetch_weights(width, _, w_gate, w_up, w_down, both, down, sems):
    copies = [
        pltpu.make_async_copy(w_gate, both.at[:, pl.ds(0, width)], sems.at[0]),
        pltpu.make_async_copy(w_up, both.at[:, pl.ds(width, width)], sems.at[1]),
        pltpu.make_async_copy(w_down, down, sems.at[2]),
    ]
    for copy in copies:
        copy.start()
    for copy in copies:
        copy.wait()


def first_matmul(width, idx, *refs):
    along_x, (inv_gain2, weights, keep, send, part) = refs[:NX], refs[NX:]
    core = idx[3]
    block = along_x[0].shape[0]
    for k in range(NX):
        at = lax.rem(k + NX // NC * core, NX)
        part[rows_at(at * block, block), :] = along_x[k][...]
    top = part.shape[0] // 2
    lane = lax.broadcasted_iota(jnp.int32, (block, MARKS), 1)
    for i in range(NX):
        wide = part[pl.ds(i * block, block), :].astype(jnp.float32)
        sums = jnp.sum(wide * wide * inv_gain2[...], axis=1, keepdims=True)
        high = sums.astype(jnp.bfloat16).astype(jnp.float32)
        marks = jnp.where(lane == 0, high, jnp.where(lane == 1, sums - high, 0.0))
        out = keep if i * block < top else send
        out[pl.ds(i * block % top, block), pl.ds(2 * width, MARKS)] = marks.astype(jnp.bfloat16)

    @pl.loop(0, 2 * width // 256)
    def _(t):
        cols = pl.ds(pl.multiple_of(t * 256, 256), 256)
        terms = jnp.dot(part[...], weights[:, cols], preferred_element_type=jnp.float32)
        keep[:, cols] = terms[:top].astype(jnp.bfloat16)
        send[:, cols] = terms[top:].astype(jnp.bfloat16)


def core_sum(block, idx, keep, came, own, *outs):
    mine = idx[2]

    def summed(y):
        at = rows_at(y * block, block)
        return keep[at, :].astype(jnp.float32) + came[at, :].astype(jnp.float32)

    own[...] = summed(mine)
    for k, out in enumerate(outs, 1):
        out[...] = summed(lax.rem(mine + k, NY)).astype(jnp.bfloat16)


def activate(width, own, one, two, three, hidden):
    sums = own[...] + one[...].astype(jnp.float32) + two[...].astype(jnp.float32) + three[...].astype(jnp.float32)
    meansq = jnp.sum(sums[:, 2 * width :], axis=1, keepdims=True) / D
    inv = lax.rsqrt(meansq + 1e-05)
    gate = sums[:, :width] * inv
    up = sums[:, width : 2 * width] * inv
    made = (gate / (1.0 + jnp.exp(-gate)) * up).astype(jnp.bfloat16)
    for t in range(hidden.shape[0]):
        hidden[t] = made


def second_matmul(came, weights, *refs):
    by_x, (hidden, terms) = refs[:NX], refs[NX:]
    block = came.shape[1]
    for y in range(NY):
        for core in range(NC):
            hidden[pl.ds((core * NY + y) * block, block), :] = came[y * NC + core]

    @pl.loop(0, weights.shape[1] // 256)
    def _(t):
        cols = pl.ds(pl.multiple_of(t * 256, 256), 256)
        terms[:, cols] = jnp.dot(hidden[...], weights[:, cols], preferred_element_type=jnp.float32).astype(jnp.bfloat16)

    size = by_x[0].shape[0]
    for k in range(NX):
        by_x[k][...] = terms[pl.ds((NX - k) % NX * size, size), :]


def x_sum(one, two, three, four, out):
    total = one[...].astype(jnp.float32)
    for ref in (two, three, four):
        total = total + ref[...].astype(jnp.float32)
    out[...] = total.astype(jnp.bfloat16)


def finish(stream, *refs):
    parts, out = refs[:-1], refs[-1]
    count = parts[0].shape[1]
    sums = []
    for part in parts:
        total = part[0].astype(jnp.float32)
        for z in range(1, NZ):
            total = total + part[z].astype(jnp.float32)
        sums.append(total)
    out[...] = (stream[...] + jnp.concatenate(sums, axis=0)).astype(jnp.bfloat16)


def shards(
    hidden_rows,
    queries,
    cache_keys,
    cache_values,
    new_keys,
    new_values,
    lengths,
    norm_gain,
    w_gate,
    w_up,
    w_down,
):
    f32, bf16 = jnp.float32, jnp.bfloat16
    rows, feats = hidden_rows.shape
    width = w_gate.shape[1]
    count = rows // PARTS
    total = count * NX * NZ
    block = total // (NY * NC)
    wide = 2 * width + MARKS
    per = feats // HEAD_DIM
    idx = jnp.stack([lax.axis_index(a) for a in ("x", "z", "y", "core")]).astype(jnp.int32)
    stream, inv_gain2, *scaled = call(
        functools.partial(start_rows, HEAD_DIM ** (-0.5)),
        [shape(rows, feats, kind=f32), shape(1, feats, kind=f32)] + [shape(NZ, count, feats)] * PARTS,
        [lengths, hidden_rows, queries, cache_keys, cache_values, new_keys, new_values, norm_gain[None]],
        "s" + "v" * 7,
        scratch=[pltpu.VMEM((rows * per, HEAD_DIM), f32)] * 2,
        moved=4 * cache_keys.size,
    )

    along_z = [lax.all_to_all(v, "z", 0, 0).reshape(NZ * count, feats) for v in scaled]
    along_x = [[v] + [shift(v, "x", k, NX) for k in range(1, NX)] for v in along_z]
    both, down = call(
        functools.partial(fetch_weights, width),
        [shape(feats, 2 * width), shape(width, feats)],
        [along_z[0], w_gate, w_up, w_down],
        "hhhh",
        scratch=[pltpu.SemaphoreType.DMA((3,))],
        moved=12 * feats * width,
        limit=12 * MIB,
    )

    ends = []
    for part in along_x:
        keep, send = call(
            functools.partial(first_matmul, width),
            [shape(total // 2, wide)] * 2,
            [idx] + part + [inv_gain2, both],
            "s" + "v" * (NX + 2),
            scratch=[pltpu.VMEM((total, feats), bf16)],
            flops=4 * total * feats * width,
            moved=4 * feats * width,
        )
        came = shift(send, "core", 1, NC)
        own, *pieces = call(
            functools.partial(core_sum, block),
            [shape(block, wide, kind=f32)] + [shape(block, wide)] * (NY - 1),
            [idx, keep, came],
            "svv",
            moved=4 * total * wide,
        )
        pieces = [shift(v, "y", k, NY) for k, v in enumerate(pieces, 1)]
        hidden = call(
            functools.partial(activate, width),
            shape(NY * NC, block, width),
            [own] + pieces,
            "vvvv",
            moved=10 * block * wide,
        )
        hidden = lax.all_to_all(hidden, TP, 0, 0)
        by_x = call(
            second_matmul,
            [shape(NZ * count, feats)] * NX,
            [hidden, down],
            "vv",
            scratch=[pltpu.VMEM((total, width), bf16), pltpu.VMEM((total, feats), bf16)],
            flops=2 * total * feats * width,
            moved=2 * feats * width,
        )
        got = [by_x[0]] + [shift(by_x[k], "x", k, NX) for k in range(1, NX)]
        summed = call(x_sum, shape(NZ * count, feats), got, "vvvv", moved=10 * count * NZ * feats)
        ends.append(lax.all_to_all(summed.reshape(NZ, count, feats), "z", 0, 0))
    return call(finish, shape(rows, feats), [stream] + ends, "v" * (1 + PARTS), moved=40 * rows * feats)


def solution(mesh):
    fine = Mesh(mesh.devices.reshape(NX, NZ, NY, NC), ("x", "z", "y", "core"))
    pool = ("x", "z")
    placed = (
        P(pool, TP),
        P(pool, TP),
        P(pool, None, TP),
        P(pool, None, TP),
        P(pool, TP),
        P(pool, TP),
        P(pool),
        P(TP),
        P(TP, pool),
        P(TP, pool),
        P(pool, TP),
    )
    return jax.shard_map(shards, mesh=fine, in_specs=placed, out_specs=P(pool, TP), check_vma=False)
```

```python
import functools

import jax
import jax.numpy as jnp
from jax import lax
from jax.experimental import pallas as pl
from jax.experimental.pallas import tpu as pltpu
from jax.sharding import Mesh
from jax.sharding import PartitionSpec as P

D = 16384
HEAD_DIM = 128
NX, NZ, NY, NC = 4, 8, 4, 2
TP = ("y", "core")
MARKS = 128
MIB = 1 << 20
ORDER = (0, -1, 1, -2, 2, -3, 3, 4)
EARLY = 5


def shift(v, axis, by, n):
    return lax.ppermute(v, axis, [(i, (i + by) % n) for i in range(n)])


def rows_at(start, count):
    return pl.ds(pl.multiple_of(start, count), count)


def call(kernel, outs, args, kinds, scratch=(), flops=0, moved=0, limit=16 * MIB):
    spaces = {"s": pltpu.SMEM, "v": pltpu.VMEM, "h": pltpu.HBM}
    single = not isinstance(outs, (list, tuple))
    whole = [outs] if single else list(outs)
    got = pl.pallas_call(
        kernel,
        out_shape=whole,
        in_specs=[pl.BlockSpec(memory_space=spaces[k]) for k in kinds],
        out_specs=[pl.BlockSpec(memory_space=pltpu.VMEM)] * len(whole),
        scratch_shapes=list(scratch),
        compiler_params=pltpu.CompilerParams(vmem_limit_bytes=limit),
        cost_estimate=pl.CostEstimate(flops=flops, bytes_accessed=moved, transcendentals=0),
    )(*args)
    return got[0] if single else got


def shape(*dims, kind=jnp.bfloat16):
    return jax.ShapeDtypeStruct(dims, kind)


def copy_in(pairs, sems):
    copies = [pltpu.make_async_copy(src, dst, sems.at[i]) for i, (src, dst) in enumerate(pairs)]
    for copy in copies:
        copy.start()
    for copy in copies:
        copy.wait()


def start_rows(scale, lengths_in, hidden_in, queries_in, keys_in, values_in, own_keys_in, own_values_in, gain_in, *rest):
    stream, inv_gain2, out, lengths, hidden, queries, keys, values, own_keys, own_values, gain, heads, mixed, sems = rest
    copy_in(
        [
            (lengths_in, lengths),
            (queries_in, queries),
            (keys_in, keys),
            (values_in, values),
            (own_keys_in, own_keys),
            (own_values_in, own_values),
            (hidden_in, hidden),
            (gain_in, gain),
        ],
        sems,
    )
    rows, feats = hidden.shape
    per = feats // HEAD_DIM
    ctx = keys.shape[1]
    f32, bf16 = jnp.float32, jnp.bfloat16
    wide = queries[...].astype(f32)
    for h in range(per):
        heads[pl.ds(h, rows, stride=per), :] = wide[:, h * HEAD_DIM : (h + 1) * HEAD_DIM]
    slot = lax.broadcasted_iota(jnp.int32, (per, ctx), 1)
    keys_new = own_keys[...].astype(f32)
    values_new = own_values[...].astype(f32)
    for r in range(rows):
        mine = heads[pl.ds(r * per, per), :]
        live = slot < lengths[r]
        score = lax.dot_general(
            mine.astype(bf16), keys[r], (((1,), (1,)), ((), ())), preferred_element_type=f32
        )
        score = jnp.where(live, score * scale, -1e30)
        own = jnp.sum(mine * keys_new[r : r + 1, :], axis=1, keepdims=True) * scale
        top = jnp.maximum(jnp.max(score, axis=1, keepdims=True), own)
        weight = jnp.where(live, jnp.exp(score - top), 0.0)
        own_weight = jnp.exp(own - top)
        total = jnp.sum(weight, axis=1, keepdims=True) + own_weight
        read = jnp.dot(weight.astype(bf16), values[r], preferred_element_type=f32)
        read = read + own_weight.astype(bf16).astype(f32) * values_new[r : r + 1, :]
        mixed[pl.ds(r * per, per), :] = read / total
    scales = gain[...].astype(f32)
    inv_gain2[...] = 1.0 / (scales * scales)
    for h in range(per):
        cols = slice(h * HEAD_DIM, (h + 1) * HEAD_DIM)
        got = hidden[:, cols].astype(f32) + mixed[pl.ds(h, rows, stride=per), :]
        stream[:, cols] = got
        out[:, cols] = (got * scales[:, cols]).astype(bf16)


def join(*refs):
    parts, out = refs[:-1], refs[-1]
    size = parts[0].shape[0]
    for k, part in enumerate(parts):
        out[pl.ds(k * size, size), :] = part[...]


def first_matmul(width, idx, *refs):
    pieces, (inv_gain2, w_gate, w_up, keep, send, part) = refs[:-6], refs[-6:]
    core = idx[3]
    top = keep.shape[0]
    at = 0
    spare = []
    for piece in pieces:
        half = piece.shape[0] // 2 if piece.shape[0] == 64 else piece.shape[0]
        if half < piece.shape[0]:
            part[pl.ds(at, half), :] = piece[rows_at(core * half, half), :]
            part[pl.ds(top + at, half), :] = piece[rows_at((1 - core) * half, half), :]
            at += half
        else:
            spare.append(piece)
    if spare:
        first, second = spare
        half = first.shape[0]
        low = jnp.where(core == 0, first[...], second[...])
        high = jnp.where(core == 0, second[...], first[...])
        part[pl.ds(at, half), :] = low
        part[pl.ds(top + at, half), :] = high
    step = 32
    lane = lax.broadcasted_iota(jnp.int32, (step, MARKS), 1)
    for i in range(2 * top // step):
        wide = part[pl.ds(i * step, step), :].astype(jnp.float32)
        sums = jnp.sum(wide * wide * inv_gain2[...], axis=1, keepdims=True)
        high = sums.astype(jnp.bfloat16).astype(jnp.float32)
        marks = jnp.where(lane == 0, high, jnp.where(lane == 1, sums - high, 0.0))
        out = keep if i * step < top else send
        out[pl.ds(i * step % top, step), pl.ds(2 * width, MARKS)] = marks.astype(jnp.bfloat16)

    def tile(weights, base, start, size):
        terms = jnp.dot(part[...], weights[:, pl.ds(start, size)], preferred_element_type=jnp.float32)
        keep[:, pl.ds(base + start, size)] = terms[:top].astype(jnp.bfloat16)
        send[:, pl.ds(base + start, size)] = terms[top:].astype(jnp.bfloat16)

    for weights, base in ((w_gate, 0), (w_up, width)):
        whole = width // 256
        pl.loop(0, whole)(lambda t, w=weights, b=base: tile(w, b, pl.multiple_of(t * 256, 256), 256))
        if width % 256:
            tile(weights, base, whole * 256, width % 256)


def halves(up, down, _, up_half, down_half):
    size = up_half.shape[0]
    up_half[...] = up[pl.ds(0, size), :]
    down_half[...] = down[pl.ds(size, size), :]


def core_sum(block, idx, keep, keep_late, came, came_late, own, *rest):
    outs, total = rest[:-1], rest[-1]
    mine = idx[2]
    first = keep.shape[0]
    total[pl.ds(0, first), :] = keep[...].astype(jnp.float32) + came[...].astype(jnp.float32)
    total[pl.ds(first, keep_late.shape[0]), :] = keep_late[...].astype(jnp.float32) + came_late[...].astype(jnp.float32)
    own[...] = total[rows_at(mine * block, block), :]
    for k, out in enumerate(outs, 1):
        out[...] = total[rows_at(lax.rem(mine + k, NY) * block, block), :].astype(jnp.bfloat16)


def activate(width, own, one, two, three, hidden):
    sums = own[...] + one[...].astype(jnp.float32) + two[...].astype(jnp.float32) + three[...].astype(jnp.float32)
    meansq = jnp.sum(sums[:, 2 * width :], axis=1, keepdims=True) / D
    inv = lax.rsqrt(meansq + 1e-05)
    gate = sums[:, :width] * inv
    up = sums[:, width : 2 * width] * inv
    hidden[...] = (gate / (1.0 + jnp.exp(-gate)) * up).astype(jnp.bfloat16)


def second_matmul(first, last, idx, *refs):
    same, refs = refs[:NY], refs[NY:]
    other, refs = refs[:NY], refs[NY:]
    weights, outs, (hidden, terms) = refs[0], refs[1:-2], refs[-2:]
    mine, core = idx[2], idx[3]
    block = same[0].shape[0]
    half = block // 2
    for k in range(NY):
        at = lax.rem(mine - k + NY, NY) * 2 * block
        for i in range(2):
            hidden[rows_at(at + i * block + core * half, half), :] = same[k][pl.ds(i * half, half), :]
            hidden[rows_at(at + i * block + (1 - core) * half, half), :] = other[k][pl.ds(i * half, half), :]

    @pl.loop(0, weights.shape[1] // 256)
    def _(t):
        cols = pl.ds(pl.multiple_of(t * 256, 256), 256)
        some = hidden[pl.ds(first * block, (last - first) * block), :]
        terms[:, cols] = jnp.dot(some, weights[:, cols], preferred_element_type=jnp.float32).astype(jnp.bfloat16)

    at = 0
    for out in outs:
        size = out.shape[0]
        out[...] = terms[pl.ds(at, size), :]
        at += size


def add_half(up_came, down_came, up_own, down_own, up, down):
    f32, bf16 = jnp.float32, jnp.bfloat16
    size = up_came.shape[0]
    low, high = pl.ds(0, size), pl.ds(size, size)
    up[low, :] = (up_came[...].astype(f32) + up_own[low, :].astype(f32)).astype(bf16)
    up[high, :] = up_own[high, :]
    down[low, :] = down_own[low, :]
    down[high, :] = (down_came[...].astype(f32) + down_own[high, :].astype(f32)).astype(bf16)


def add_whole(up_came, down_came, up_own, down_own, up, down):
    f32, bf16 = jnp.float32, jnp.bfloat16
    up[...] = (up_came[...].astype(f32) + up_own[...].astype(f32)).astype(bf16)
    down[...] = (down_came[...].astype(f32) + down_own[...].astype(f32)).astype(bf16)


def z_sum(own, up, down, mine, *outs):
    rows = mine.shape[0]

    def summed(k):
        at = pl.ds(k * rows, rows)
        return own[at, :].astype(jnp.float32) + up[at, :].astype(jnp.float32) + down[at, :].astype(jnp.float32)

    mine[...] = summed(0)
    for k, out in enumerate(outs, 1):
        out[...] = summed(k).astype(jnp.bfloat16)


def finish(stream, mine, one, two, three, out):
    total = stream[...] + mine[...]
    for ref in (one, two, three):
        total = total + ref[...].astype(jnp.float32)
    out[...] = total.astype(jnp.bfloat16)


def shards(
    hidden_rows,
    queries,
    cache_keys,
    cache_values,
    new_keys,
    new_values,
    lengths,
    norm_gain,
    w_gate,
    w_up,
    w_down,
):
    f32, bf16 = jnp.float32, jnp.bfloat16
    rows, feats = hidden_rows.shape
    width = w_gate.shape[1]
    piece = rows * NX
    total = piece * NZ
    block = total // (NY * NC)
    wide = 2 * width + MARKS
    per = feats // HEAD_DIM
    idx = jnp.stack([lax.axis_index(a) for a in ("x", "z", "y", "core")]).astype(jnp.int32)
    given = [lengths, hidden_rows, queries, cache_keys, cache_values, new_keys, new_values, norm_gain[None]]
    stream, inv_gain2, scaled = call(
        functools.partial(start_rows, HEAD_DIM ** (-0.5)),
        [shape(rows, feats, kind=f32), shape(1, feats, kind=f32), shape(rows, feats)],
        given,
        "h" * 8,
        scratch=[pltpu.SMEM(lengths.shape, jnp.int32)]
        + [pltpu.VMEM(v.shape, v.dtype) for v in given[1:]]
        + [pltpu.VMEM((rows * per, HEAD_DIM), f32)] * 2
        + [pltpu.SemaphoreType.DMA((8,))],
        moved=4 * cache_keys.size,
        limit=60 * MIB,
    )

    own = call(
        join,
        shape(piece, feats),
        [scaled] + [shift(scaled, "x", k, NX) for k in range(1, NX)],
        "v" * NX,
        moved=4 * piece * feats,
    )
    pieces = {0: own}
    up = down = own
    for step in range(1, NZ // 2):
        up = shift(up, "z", 1, NZ)
        down = shift(down, "z", -1, NZ)
        pieces[-step], pieces[step] = up, down

    def project(some):
        size = sum(v.shape[0] for v in some)
        return call(
            functools.partial(first_matmul, width),
            [shape(size // 2, wide)] * 2,
            [idx] + some + [inv_gain2, w_gate, w_up],
            "s" + "v" * (len(some) + 3),
            scratch=[pltpu.VMEM((size, feats), bf16)],
            flops=4 * size * feats * width,
            moved=4 * feats * width,
        )

    keep, send = project([pieces[j] for j in ORDER[:EARLY]])
    came = shift(send, "core", 1, NC)
    up, down = call(halves, [shape(piece // 2, feats)] * 2, [up, down, keep], "vvh", moved=4 * piece * feats)
    up = shift(up, "z", 1, NZ)
    down = shift(down, "z", -1, NZ)
    keep_late, send_late = project([pieces[j] for j in ORDER[EARLY:-1]] + [up, down])
    came_late = shift(send_late, "core", 1, NC)
    own, *parts = call(
        functools.partial(core_sum, block),
        [shape(block, wide, kind=f32)] + [shape(block, wide)] * (NY - 1),
        [idx, keep, keep_late, came, came_late],
        "svvvv",
        scratch=[pltpu.VMEM((total // 2, wide), f32)],
        moved=4 * total * wide,
    )
    parts = [shift(v, "y", k, NY) for k, v in enumerate(parts, 1)]
    hidden = call(functools.partial(activate, width), shape(block, width), [own] + parts, "vvvv", moved=10 * block * wide)
    same = [hidden] + [shift(hidden, "y", k, NY) for k in range(1, NY)]
    other = [shift(v, "core", 1, NC) for v in same]

    def expand(first, last, sizes):
        return call(
            functools.partial(second_matmul, first, last),
            [shape(size, feats) for size in sizes],
            [idx] + same + other + [w_down],
            "s" + "v" * (2 * NY + 1),
            scratch=[pltpu.VMEM((total, width), bf16), pltpu.VMEM(((last - first) * piece, feats), bf16)],
            flops=2 * (last - first) * piece * feats * width,
            moved=2 * feats * width,
        )

    far = expand(EARLY, NZ, [piece, piece, piece // 2, piece // 2])
    near = expand(0, EARLY, [piece] * EARLY)
    terms = dict(zip(ORDER, near + far[:2]))

    up, down = far[2], far[3]
    for step in range(NZ // 2 - 1, 0, -1):
        up = shift(up, "z", -1, NZ)
        down = shift(down, "z", 1, NZ)
        up, down = call(
            add_half if step == NZ // 2 - 1 else add_whole,
            [shape(piece, feats)] * 2,
            [up, down, terms[-step], terms[step]],
            "vvvv",
            moved=12 * piece * feats,
        )
    up = shift(up, "z", -1, NZ)
    down = shift(down, "z", 1, NZ)
    mine, *parts = call(
        z_sum,
        [shape(rows, feats, kind=f32)] + [shape(rows, feats)] * (NX - 1),
        [terms[0], up, down],
        "vvv",
        moved=8 * piece * feats,
    )
    parts = [shift(v, "x", -k, NX) for k, v in enumerate(parts, 1)]
    return call(finish, shape(rows, feats), [stream, mine] + parts, "v" * 5, moved=20 * rows * feats)


def solution(mesh):
    fine = Mesh(mesh.devices.reshape(NX, NZ, NY, NC), ("x", "z", "y", "core"))
    pool = ("x", "z")
    placed = (
        P(pool, TP),
        P(pool, TP),
        P(pool, None, TP),
        P(pool, None, TP),
        P(pool, TP),
        P(pool, TP),
        P(pool),
        P(TP),
        P(TP, pool),
        P(TP, pool),
        P(pool, TP),
    )
    return jax.shard_map(shards, mesh=fine, in_specs=placed, out_specs=P(pool, TP), check_vma=False)
```

```python
import functools

import jax
import jax.numpy as jnp
from jax import lax
from jax.experimental import pallas as pl
from jax.experimental.pallas import tpu as pltpu
from jax.sharding import Mesh
from jax.sharding import PartitionSpec as P

D = 16384
HEAD_DIM = 128
NX, NZ, NY, NC = 4, 8, 4, 2
TP = ("y", "core")
MARKS = 128
MIB = 1 << 20
ORDER = (0, -1, 1, -2, 2, -3, 3, 4)
EARLY = 5


def shift(v, axis, by, n):
    return lax.ppermute(v, axis, [(i, (i + by) % n) for i in range(n)])


def rows_at(start, count):
    return pl.ds(pl.multiple_of(start, count), count)


def call(kernel, outs, args, kinds, scratch=(), flops=0, moved=0, limit=16 * MIB):
    spaces = {"s": pltpu.SMEM, "v": pltpu.VMEM, "h": pltpu.HBM}
    single = not isinstance(outs, (list, tuple))
    whole = [outs] if single else list(outs)
    got = pl.pallas_call(
        kernel,
        out_shape=whole,
        in_specs=[pl.BlockSpec(memory_space=spaces[k]) for k in kinds],
        out_specs=[pl.BlockSpec(memory_space=pltpu.VMEM)] * len(whole),
        scratch_shapes=list(scratch),
        compiler_params=pltpu.CompilerParams(vmem_limit_bytes=limit),
        cost_estimate=pl.CostEstimate(flops=flops, bytes_accessed=moved, transcendentals=0),
    )(*args)
    return got[0] if single else got


def shape(*dims, kind=jnp.bfloat16):
    return jax.ShapeDtypeStruct(dims, kind)


def copy_in(pairs, sems):
    copies = [pltpu.make_async_copy(src, dst, sems.at[i]) for i, (src, dst) in enumerate(pairs)]
    for copy in copies:
        copy.start()
    for copy in copies:
        copy.wait()


def copy_in(pairs, sems):
    copies = [pltpu.make_async_copy(src, dst, sems.at[i]) for i, (src, dst) in enumerate(pairs)]
    for copy in copies:
        copy.start()
    for copy in copies:
        copy.wait()


def start_rows(scale, lengths_in, hidden_in, queries_in, keys_in, values_in, own_keys_in, own_values_in, gain_in, *rest):
    stream, inv_gain2, out, lengths, hidden, queries, keys, values, own_keys, own_values, gain, heads, work, low, sems = rest
    copy_in(
        [
            (queries_in, queries),
            (lengths_in, lengths),
            (keys_in, keys),
            (values_in, values),
            (own_keys_in, own_keys),
            (own_values_in, own_values),
            (hidden_in, hidden),
            (gain_in, gain),
        ],
        sems,
    )
    rows, feats = hidden.shape
    per = feats // HEAD_DIM
    ctx = keys.shape[1]
    f32, bf16 = jnp.float32, jnp.bfloat16
    wide = queries[...].astype(f32)
    for h in range(per):
        heads[pl.ds(h, rows, stride=per), :] = wide[:, h * HEAD_DIM : (h + 1) * HEAD_DIM]
    slot = lax.broadcasted_iota(jnp.int32, (per, ctx), 1)

    def spread(ref):
        each = ref[...].astype(f32)
        return jnp.concatenate(
            [jnp.broadcast_to(each[r : r + 1, :], (per, HEAD_DIM)) for r in range(rows)], axis=0
        )

    for r in range(rows):
        score = lax.dot_general(
            heads[pl.ds(r * per, per), :].astype(bf16),
            keys[r],
            (((1,), (1,)), ((), ())),
            preferred_element_type=f32,
        )
        work[pl.ds(r * per, per), :] = jnp.where(slot < lengths[r], score * scale, -1e30)
    own = jnp.sum(heads[...] * spread(own_keys), axis=1, keepdims=True) * scale
    score = work[...]
    top = jnp.maximum(jnp.max(score, axis=1, keepdims=True), own)
    weight = jnp.exp(score - top)
    own_weight = jnp.exp(own - top)
    total = jnp.sum(weight, axis=1, keepdims=True) + own_weight
    low[...] = weight.astype(bf16)
    for r in range(rows):
        work[pl.ds(r * per, per), :] = jnp.dot(low[pl.ds(r * per, per), :], values[r], preferred_element_type=f32)
    work[...] = (work[...] + own_weight.astype(bf16).astype(f32) * spread(own_values)) / total
    scales = gain[...].astype(f32)
    inv_gain2[...] = 1.0 / (scales * scales)
    for h in range(per):
        cols = slice(h * HEAD_DIM, (h + 1) * HEAD_DIM)
        got = hidden[:, cols].astype(f32) + work[pl.ds(h, rows, stride=per), :]
        stream[:, cols] = got
        out[:, cols] = (got * scales[h : h + 1, :]).astype(bf16)


def join(first, second, *refs):
    out = refs[-1]
    size = first.shape[0]
    out[pl.ds(0, size), :] = first[...]
    out[pl.ds(size, size), :] = second[...]


def fetch_first(width, _, w_gate, w_up, both, sems):
    copy_in([(w_gate, both.at[:, pl.ds(0, width)]), (w_up, both.at[:, pl.ds(width, width)])], sems)


def first_matmul(width, idx, *refs):
    pieces, (inv_gain2, weights, keep, send, part) = refs[:-5], refs[-5:]
    core = idx[3]
    top = keep.shape[0]
    half = pieces[0].shape[0]
    for i, piece in enumerate(pieces):
        away = lax.rem(i + core, NC)
        part[rows_at(away * top + i // 2 * half, half), :] = piece[...]
    step = 32
    lane = lax.broadcasted_iota(jnp.int32, (step, MARKS), 1)
    for i in range(2 * top // step):
        sums = 0.0
        for h in range(part.shape[1] // HEAD_DIM):
            wide = part[pl.ds(i * step, step), pl.ds(h * HEAD_DIM, HEAD_DIM)].astype(jnp.float32)
            sums = sums + wide * wide * inv_gain2[pl.ds(h, 1), :]
        sums = jnp.sum(sums, axis=1, keepdims=True)
        high = sums.astype(jnp.bfloat16).astype(jnp.float32)
        marks = jnp.where(lane == 0, high, jnp.where(lane == 1, sums - high, 0.0))
        out = keep if i * step < top else send
        out[pl.ds(i * step % top, step), pl.ds(2 * width, MARKS)] = marks.astype(jnp.bfloat16)

    @pl.loop(0, 2 * width // 256)
    def _(t):
        cols = pl.ds(pl.multiple_of(t * 256, 256), 256)
        terms = jnp.dot(part[...], weights[:, cols], preferred_element_type=jnp.float32)
        keep[:, cols] = terms[:top].astype(jnp.bfloat16)
        send[:, cols] = terms[top:].astype(jnp.bfloat16)


def core_sum(block, idx, keep, keep_late, came, came_late, own, *rest):
    outs, total = rest[:-1], rest[-1]
    mine = idx[2]
    first = keep.shape[0]
    total[pl.ds(0, first), :] = keep[...].astype(jnp.float32) + came[...].astype(jnp.float32)
    total[pl.ds(first, keep_late.shape[0]), :] = keep_late[...].astype(jnp.float32) + came_late[...].astype(jnp.float32)
    own[...] = total[rows_at(mine * block, block), :]
    for k, out in enumerate(outs, 1):
        out[...] = total[rows_at(lax.rem(mine + k, NY) * block, block), :].astype(jnp.bfloat16)


def activate(width, own, one, two, three, hidden):
    sums = own[...] + one[...].astype(jnp.float32) + two[...].astype(jnp.float32) + three[...].astype(jnp.float32)
    meansq = jnp.sum(sums[:, 2 * width :], axis=1, keepdims=True) / D
    inv = lax.rsqrt(meansq + 1e-05)
    gate = sums[:, :width] * inv
    up = sums[:, width : 2 * width] * inv
    hidden[...] = (gate / (1.0 + jnp.exp(-gate)) * up).astype(jnp.bfloat16)


def second_matmul(first, last, idx, *refs):
    same, refs = refs[:NY], refs[NY:]
    other, refs = refs[:NY], refs[NY:]
    weights, outs, (hidden, terms) = refs[0], refs[1:-2], refs[-2:]
    mine, core = idx[2], idx[3]
    block = same[0].shape[0]
    half = block // 2
    for k in range(NY):
        at = lax.rem(mine - k + NY, NY) * 2 * block
        for i in range(2):
            hidden[rows_at(at + i * block + core * half, half), :] = same[k][pl.ds(i * half, half), :]
            hidden[rows_at(at + i * block + (1 - core) * half, half), :] = other[k][pl.ds(i * half, half), :]

    @pl.loop(0, weights.shape[1] // 256)
    def _(t):
        cols = pl.ds(pl.multiple_of(t * 256, 256), 256)
        some = hidden[pl.ds(first * block, (last - first) * block), :]
        terms[:, cols] = jnp.dot(some, weights[:, cols], preferred_element_type=jnp.float32).astype(jnp.bfloat16)

    at = 0
    for out in outs:
        size = out.shape[0]
        out[...] = terms[pl.ds(at, size), :]
        at += size


def add(came, own, out):
    out[...] = (came[...].astype(jnp.float32) + own[...].astype(jnp.float32)).astype(jnp.bfloat16)


def z_sum(own, one, two, *outs):
    rows = outs[0].shape[0]
    for k, out in enumerate(outs):
        at = pl.ds(k * rows, rows)
        total = own[at, :].astype(jnp.float32) + one[at, :].astype(jnp.float32) + two[at, :].astype(jnp.float32)
        out[...] = total.astype(out.dtype)


def finish(stream, mine, one, two, three, out):
    total = stream[...] + mine[...]
    for ref in (one, two, three):
        total = total + ref[...].astype(jnp.float32)
    out[...] = total.astype(jnp.bfloat16)


def shards(
    hidden_rows,
    queries,
    cache_keys,
    cache_values,
    new_keys,
    new_values,
    lengths,
    norm_gain,
    w_gate,
    w_up,
    w_down,
):
    f32, bf16 = jnp.float32, jnp.bfloat16
    rows, feats = hidden_rows.shape
    width = w_gate.shape[1]
    piece = rows * NX
    total = piece * NZ
    block = total // (NY * NC)
    wide = 2 * width + MARKS
    per = feats // HEAD_DIM
    idx = jnp.stack([lax.axis_index(a) for a in ("x", "z", "y", "core")]).astype(jnp.int32)
    given = [lengths, hidden_rows, queries, cache_keys, cache_values, new_keys, new_values, norm_gain.reshape(per, HEAD_DIM)]
    stream, inv_gain2, scaled = call(
        functools.partial(start_rows, HEAD_DIM ** (-0.5)),
        [shape(rows, feats, kind=f32), shape(per, HEAD_DIM, kind=f32), shape(rows, feats)],
        given,
        "h" * 8,
        scratch=[pltpu.SMEM(lengths.shape, jnp.int32)]
        + [pltpu.VMEM(v.shape, v.dtype) for v in given[1:]]
        + [pltpu.VMEM((rows * per, HEAD_DIM), f32)] * 2
        + [pltpu.VMEM((rows * per, HEAD_DIM), bf16)]
        + [pltpu.SemaphoreType.DMA((8,))],
        moved=4 * cache_keys.size,
        limit=60 * MIB,
    )

    from_x = [scaled] + [shift(scaled, "x", k, NX) for k in range(1, NX)]
    both = call(
        functools.partial(fetch_first, width),
        shape(feats, 2 * width),
        [scaled, w_gate, w_up],
        "hhh",
        scratch=[pltpu.SemaphoreType.DMA((2,))],
        moved=8 * feats * width,
        limit=12 * MIB,
    )
    low = call(join, shape(piece // 2, feats), from_x[:2], "vv", moved=2 * piece * feats)
    high = call(join, shape(piece // 2, feats), from_x[2:] + [both], "vvh", moved=2 * piece * feats)
    pieces = {0: [low, high]}
    for step in range(1, NZ // 2):
        pieces[-step] = [shift(v, "z", 1, NZ) for v in pieces[1 - step]]
        pieces[step] = [shift(v, "z", -1, NZ) for v in pieces[step - 1]]
    pieces[NZ // 2] = [
        shift(pieces[1 - NZ // 2][0], "z", 1, NZ),
        shift(pieces[NZ // 2 - 1][1], "z", -1, NZ),
    ]

    def project(some):
        size = len(some) * piece
        return call(
            functools.partial(first_matmul, width),
            [shape(size // 2, wide)] * 2,
            [idx] + [v for j in some for v in pieces[j]] + [inv_gain2, both],
            "s" + "v" * (2 * len(some) + 2),
            scratch=[pltpu.VMEM((size, feats), bf16)],
            flops=4 * size * feats * width,
            moved=4 * feats * width,
        )

    keep, send = project(ORDER[:EARLY])
    came = shift(send, "core", 1, NC)
    keep_late, send_late = project(ORDER[EARLY:])
    came_late = shift(send_late, "core", 1, NC)
    own, *parts = call(
        functools.partial(core_sum, block),
        [shape(block, wide, kind=f32)] + [shape(block, wide)] * (NY - 1),
        [idx, keep, keep_late, came, came_late],
        "svvvv",
        scratch=[pltpu.VMEM((total // 2, wide), f32)],
        moved=4 * total * wide,
    )
    parts = [shift(v, "y", k, NY) for k, v in enumerate(parts, 1)]
    hidden = call(functools.partial(activate, width), shape(block, width), [own] + parts, "vvvv", moved=10 * block * wide)
    same = [hidden] + [shift(hidden, "y", k, NY) for k in range(1, NY)]
    other = [shift(v, "core", 1, NC) for v in same]

    def expand(first, last):
        got = call(
            functools.partial(second_matmul, first, last),
            [shape(piece // 2, feats)] * (2 * (last - first)),
            [idx] + same + other + [w_down],
            "s" + "v" * (2 * NY + 1),
            scratch=[pltpu.VMEM((total, width), bf16), pltpu.VMEM(((last - first) * piece, feats), bf16)],
            flops=2 * (last - first) * piece * feats * width,
            moved=2 * feats * width,
        )
        return {j: got[2 * i : 2 * i + 2] for i, j in enumerate(ORDER[first:last])}

    terms = {**expand(EARLY, NZ), **expand(0, EARLY)}

    def chain(half, way, steps):
        got = terms[way * steps if steps < NZ // 2 else steps][half]
        for step in range(steps, 1, -1):
            got = shift(got, "z", way, NZ)
            own = terms[way * (step - 1)][half]
            got = call(add, shape(piece // 2, feats), [got, own], "vv", moved=6 * piece * feats // 2)
        return shift(got, "z", way, NZ)

    far = NZ // 2
    low = [chain(0, -1, far), chain(0, 1, far - 1)]
    high = [chain(1, 1, far), chain(1, -1, far - 1)]
    mine, one = call(
        z_sum, [shape(rows, feats, kind=f32), shape(rows, feats)], [terms[0][0]] + low, "vvv", moved=4 * piece * feats
    )
    two, three = call(z_sum, [shape(rows, feats)] * 2, [terms[0][1]] + high, "vvv", moved=4 * piece * feats)
    parts = [shift(v, "x", -k, NX) for k, v in enumerate([one, two, three], 1)]
    return call(finish, shape(rows, feats), [stream, mine] + parts, "v" * 5, moved=20 * rows * feats)


def solution(mesh):
    fine = Mesh(mesh.devices.reshape(NX, NZ, NY, NC), ("x", "z", "y", "core"))
    pool = ("x", "z")
    placed = (
        P(pool, TP),
        P(pool, TP),
        P(pool, None, TP),
        P(pool, None, TP),
        P(pool, TP),
        P(pool, TP),
        P(pool),
        P(TP),
        P(TP, pool),
        P(TP, pool),
        P(pool, TP),
    )
    return jax.shard_map(shards, mesh=fine, in_specs=placed, out_specs=P(pool, TP), check_vma=False)
```

```python
import functools

import jax
import jax.numpy as jnp
from jax import lax
from jax.experimental import pallas as pl
from jax.experimental.pallas import tpu as pltpu
from jax.sharding import Mesh
from jax.sharding import PartitionSpec as P

D = 16384
HEAD_DIM = 128
NX, NZ, NY, NC = 4, 8, 4, 2
TP = ("y", "core")
MARKS = 128
MIB = 1 << 20
ORDER = (0, -1, 1, -2, 2, -3, 3, 4)
EARLY = 5


def shift(v, axis, by, n):
    return lax.ppermute(v, axis, [(i, (i + by) % n) for i in range(n)])


def rows_at(start, count):
    return pl.ds(pl.multiple_of(start, count), count)


def call(kernel, outs, args, kinds, scratch=(), flops=0, moved=0, limit=16 * MIB, alias=None):
    spaces = {"s": pltpu.SMEM, "v": pltpu.VMEM, "h": pltpu.HBM}
    single = not isinstance(outs, (list, tuple))
    whole = [outs] if single else list(outs)
    got = pl.pallas_call(
        kernel,
        out_shape=whole,
        in_specs=[pl.BlockSpec(memory_space=spaces[k]) for k in kinds],
        out_specs=[pl.BlockSpec(memory_space=pltpu.VMEM)] * len(whole),
        scratch_shapes=list(scratch),
        input_output_aliases=alias or {},
        compiler_params=pltpu.CompilerParams(vmem_limit_bytes=limit),
        cost_estimate=pl.CostEstimate(flops=flops, bytes_accessed=moved, transcendentals=0),
    )(*args)
    return got[0] if single else got


def shape(*dims, kind=jnp.bfloat16):
    return jax.ShapeDtypeStruct(dims, kind)


def copy_in(pairs, sems):
    copies = [pltpu.make_async_copy(src, dst, sems.at[i]) for i, (src, dst) in enumerate(pairs)]
    for copy in copies:
        copy.start()
    for copy in copies:
        copy.wait()


def copy_in(pairs, sems):
    copies = [pltpu.make_async_copy(src, dst, sems.at[i]) for i, (src, dst) in enumerate(pairs)]
    for copy in copies:
        copy.start()
    for copy in copies:
        copy.wait()


def start_rows(scale, lengths_in, hidden_in, queries_in, keys_in, values_in, own_keys_in, own_values_in, gain_in, *rest):
    stream, inv_gain2, out, lengths, hidden, queries, keys, values, own_keys, own_values, gain, heads, work, low, sems = rest
    copy_in(
        [
            (queries_in, queries),
            (lengths_in, lengths),
            (keys_in, keys),
            (values_in, values),
            (own_keys_in, own_keys),
            (own_values_in, own_values),
            (hidden_in, hidden),
            (gain_in, gain),
        ],
        sems,
    )
    rows, feats = hidden.shape
    per = feats // HEAD_DIM
    ctx = keys.shape[1]
    f32, bf16 = jnp.float32, jnp.bfloat16
    wide = queries[...].astype(f32)
    for h in range(per):
        heads[pl.ds(h, rows, stride=per), :] = wide[:, h * HEAD_DIM : (h + 1) * HEAD_DIM]
    slot = lax.broadcasted_iota(jnp.int32, (per, ctx), 1)

    def spread(ref):
        each = ref[...].astype(f32)
        return jnp.concatenate(
            [jnp.broadcast_to(each[r : r + 1, :], (per, HEAD_DIM)) for r in range(rows)], axis=0
        )

    for r in range(rows):
        score = lax.dot_general(
            heads[pl.ds(r * per, per), :].astype(bf16),
            keys[r],
            (((1,), (1,)), ((), ())),
            preferred_element_type=f32,
        )
        work[pl.ds(r * per, per), :] = jnp.where(slot < lengths[r], score * scale, -1e30)
    own = jnp.sum(heads[...] * spread(own_keys), axis=1, keepdims=True) * scale
    score = work[...]
    top = jnp.maximum(jnp.max(score, axis=1, keepdims=True), own)
    weight = jnp.exp(score - top)
    own_weight = jnp.exp(own - top)
    total = jnp.sum(weight, axis=1, keepdims=True) + own_weight
    low[...] = weight.astype(bf16)
    for r in range(rows):
        work[pl.ds(r * per, per), :] = jnp.dot(low[pl.ds(r * per, per), :], values[r], preferred_element_type=f32)
    work[...] = (work[...] + own_weight.astype(bf16).astype(f32) * spread(own_values)) / total
    scales = gain[...].astype(f32)
    inv_gain2[...] = 1.0 / (scales * scales)
    for h in range(per):
        cols = slice(h * HEAD_DIM, (h + 1) * HEAD_DIM)
        got = hidden[:, cols].astype(f32) + work[pl.ds(h, rows, stride=per), :]
        stream[:, cols] = got
        out[:, cols] = (got * scales[h : h + 1, :]).astype(bf16)


def join(*refs):
    parts, out = refs[:-1], refs[-1]
    size = parts[0].shape[0]
    for k, part in enumerate(parts):
        out[pl.ds(k * size, size), :] = part[...]


def place(core, pieces, part):
    top = part.shape[0] // 2
    at = 0
    spare = []
    for piece in pieces:
        half = piece.shape[0] // 2
        if piece.shape[0] < pieces[0].shape[0]:
            spare.append(piece)
            continue
        part[pl.ds(at, half), :] = piece[rows_at(core * half, half), :]
        part[pl.ds(top + at, half), :] = piece[rows_at((1 - core) * half, half), :]
        at += half
    for i, piece in enumerate(spare):
        half = piece.shape[0]
        part[rows_at(lax.rem(core + i, NC) * top + at, half), :] = piece[...]


def squares(width, part, inv_gain2, keep, send):
    top = part.shape[0] // 2
    step = 32
    lane = lax.broadcasted_iota(jnp.int32, (step, MARKS), 1)
    for i in range(2 * top // step):
        sums = 0.0
        for h in range(part.shape[1] // HEAD_DIM):
            wide = part[pl.ds(i * step, step), pl.ds(h * HEAD_DIM, HEAD_DIM)].astype(jnp.float32)
            sums = sums + wide * wide * inv_gain2[pl.ds(h, 1), :]
        sums = jnp.sum(sums, axis=1, keepdims=True)
        high = sums.astype(jnp.bfloat16).astype(jnp.float32)
        marks = jnp.where(lane == 0, high, jnp.where(lane == 1, sums - high, 0.0))
        out = keep if i * step < top else send
        out[pl.ds(i * step % top, step), pl.ds(2 * width, MARKS)] = marks.astype(jnp.bfloat16)


def project(weights, base, part, keep, send):
    top, width = part.shape[0] // 2, weights.shape[1]

    def tile(start, size):
        terms = jnp.dot(part[...], weights[:, pl.ds(start, size)], preferred_element_type=jnp.float32)
        keep[:, pl.ds(base + start, size)] = terms[:top].astype(jnp.bfloat16)
        send[:, pl.ds(base + start, size)] = terms[top:].astype(jnp.bfloat16)

    pl.loop(0, width // 256)(lambda t: tile(pl.multiple_of(t * 256, 256), 256))
    if width % 256:
        tile(width // 256 * 256, width % 256)


def gate_matmul(width, idx, *refs):
    pieces, (inv_gain2, w_gate, keep, send, part, done) = refs[:-6], refs[-6:]
    place(idx[3], pieces, part)
    squares(width, part, inv_gain2, keep, send)
    project(w_gate, 0, part, keep, send)
    done[...] = jnp.zeros_like(done)


def up_matmul(width, part, w_up, keep_in, send_in, keep, send):
    project(w_up, width, part, keep, send)


def both_matmul(width, idx, *refs):
    pieces, (inv_gain2, w_gate, w_up, keep, send, part) = refs[:-6], refs[-6:]
    place(idx[3], pieces, part)
    squares(width, part, inv_gain2, keep, send)
    project(w_gate, 0, part, keep, send)
    project(w_up, width, part, keep, send)


def halves(up, down, _, up_half, down_half):
    size = up_half.shape[0]
    up_half[...] = up[pl.ds(0, size), :]
    down_half[...] = down[pl.ds(size, size), :]


def core_sum(block, idx, keep, keep_late, came, came_late, own, *rest):
    outs, total = rest[:-1], rest[-1]
    mine = idx[2]
    first = keep.shape[0]
    total[pl.ds(0, first), :] = keep[...].astype(jnp.float32) + came[...].astype(jnp.float32)
    total[pl.ds(first, keep_late.shape[0]), :] = keep_late[...].astype(jnp.float32) + came_late[...].astype(jnp.float32)
    own[...] = total[rows_at(mine * block, block), :]
    for k, out in enumerate(outs, 1):
        out[...] = total[rows_at(lax.rem(mine + k, NY) * block, block), :].astype(jnp.bfloat16)


def activate(width, own, one, two, three, hidden):
    sums = own[...] + one[...].astype(jnp.float32) + two[...].astype(jnp.float32) + three[...].astype(jnp.float32)
    meansq = jnp.sum(sums[:, 2 * width :], axis=1, keepdims=True) / D
    inv = lax.rsqrt(meansq + 1e-05)
    gate = sums[:, :width] * inv
    up = sums[:, width : 2 * width] * inv
    hidden[...] = (gate / (1.0 + jnp.exp(-gate)) * up).astype(jnp.bfloat16)


def second_matmul(first, last, idx, *refs):
    same, refs = refs[:NY], refs[NY:]
    other, refs = refs[:NY], refs[NY:]
    weights, outs, (hidden, terms) = refs[0], refs[1:-2], refs[-2:]
    mine, core = idx[2], idx[3]
    block = same[0].shape[0]
    half = block // 2
    for k in range(NY):
        at = lax.rem(mine - k + NY, NY) * 2 * block
        for i in range(2):
            hidden[rows_at(at + i * block + core * half, half), :] = same[k][pl.ds(i * half, half), :]
            hidden[rows_at(at + i * block + (1 - core) * half, half), :] = other[k][pl.ds(i * half, half), :]

    @pl.loop(0, weights.shape[1] // 256)
    def _(t):
        cols = pl.ds(pl.multiple_of(t * 256, 256), 256)
        some = hidden[pl.ds(first * block, (last - first) * block), :]
        terms[:, cols] = jnp.dot(some, weights[:, cols], preferred_element_type=jnp.float32).astype(jnp.bfloat16)

    at = 0
    for out in outs:
        size = out.shape[0]
        out[...] = terms[pl.ds(at, size), :]
        at += size


def add(came, own, out):
    out[...] = (came[...].astype(jnp.float32) + own[...].astype(jnp.float32)).astype(jnp.bfloat16)


def z_sum(own, one, two, *outs):
    rows = outs[0].shape[0]
    for k, out in enumerate(outs):
        at = pl.ds(k * rows, rows)
        total = own[at, :].astype(jnp.float32) + one[at, :].astype(jnp.float32) + two[at, :].astype(jnp.float32)
        out[...] = total.astype(out.dtype)


def finish(stream, mine, one, two, three, out):
    total = stream[...] + mine[...]
    for ref in (one, two, three):
        total = total + ref[...].astype(jnp.float32)
    out[...] = total.astype(jnp.bfloat16)


def shards(
    hidden_rows,
    queries,
    cache_keys,
    cache_values,
    new_keys,
    new_values,
    lengths,
    norm_gain,
    w_gate,
    w_up,
    w_down,
):
    f32, bf16 = jnp.float32, jnp.bfloat16
    rows, feats = hidden_rows.shape
    width = w_gate.shape[1]
    piece = rows * NX
    total = piece * NZ
    block = total // (NY * NC)
    wide = 2 * width + MARKS
    per = feats // HEAD_DIM
    idx = jnp.stack([lax.axis_index(a) for a in ("x", "z", "y", "core")]).astype(jnp.int32)
    given = [lengths, hidden_rows, queries, cache_keys, cache_values, new_keys, new_values, norm_gain.reshape(per, HEAD_DIM)]
    stream, inv_gain2, scaled = call(
        functools.partial(start_rows, HEAD_DIM ** (-0.5)),
        [shape(rows, feats, kind=f32), shape(per, HEAD_DIM, kind=f32), shape(rows, feats)],
        given,
        "h" * 8,
        scratch=[pltpu.SMEM(lengths.shape, jnp.int32)]
        + [pltpu.VMEM(v.shape, v.dtype) for v in given[1:]]
        + [pltpu.VMEM((rows * per, HEAD_DIM), f32)] * 2
        + [pltpu.VMEM((rows * per, HEAD_DIM), bf16)]
        + [pltpu.SemaphoreType.DMA((8,))],
        moved=4 * cache_keys.size,
        limit=60 * MIB,
    )

    own = call(
        join,
        shape(piece, feats),
        [scaled] + [shift(scaled, "x", k, NX) for k in range(1, NX)],
        "v" * NX,
        moved=4 * piece * feats,
    )
    pieces = {0: own}
    up = down = own
    for step in range(1, NZ // 2):
        up = shift(up, "z", 1, NZ)
        down = shift(down, "z", -1, NZ)
        pieces[-step], pieces[step] = up, down

    some = [pieces[j] for j in ORDER[:EARLY]]
    size = EARLY * piece
    keep, send, part, done = call(
        functools.partial(gate_matmul, width),
        [shape(size // 2, wide)] * 2 + [shape(size, feats), shape(8, 128, kind=f32)],
        [idx] + some + [inv_gain2, w_gate],
        "s" + "v" * (EARLY + 2),
        flops=2 * size * feats * width,
        moved=2 * feats * width,
    )
    up, down = call(halves, [shape(piece // 2, feats)] * 2, [up, down, done], "vvh", moved=4 * piece * feats)
    up = shift(up, "z", 1, NZ)
    down = shift(down, "z", -1, NZ)
    keep, send = call(
        functools.partial(up_matmul, width),
        [shape(size // 2, wide)] * 2,
        [part, w_up, keep, send],
        "vvvv",
        flops=2 * size * feats * width,
        moved=2 * feats * width,
        alias={2: 0, 3: 1},
    )
    came = shift(send, "core", 1, NC)
    some = [pieces[j] for j in ORDER[EARLY:-1]] + [up, down]
    size = (NZ - EARLY) * piece
    keep_late, send_late = call(
        functools.partial(both_matmul, width),
        [shape(size // 2, wide)] * 2,
        [idx] + some + [inv_gain2, w_gate, w_up],
        "s" + "v" * (len(some) + 3),
        scratch=[pltpu.VMEM((size, feats), bf16)],
        flops=4 * size * feats * width,
        moved=4 * feats * width,
    )
    came_late = shift(send_late, "core", 1, NC)
    own, *parts = call(
        functools.partial(core_sum, block),
        [shape(block, wide, kind=f32)] + [shape(block, wide)] * (NY - 1),
        [idx, keep, keep_late, came, came_late],
        "svvvv",
        scratch=[pltpu.VMEM((total // 2, wide), f32)],
        moved=4 * total * wide,
    )
    parts = [shift(v, "y", k, NY) for k, v in enumerate(parts, 1)]
    hidden = call(functools.partial(activate, width), shape(block, width), [own] + parts, "vvvv", moved=10 * block * wide)
    same = [hidden] + [shift(hidden, "y", k, NY) for k in range(1, NY)]
    other = [shift(v, "core", 1, NC) for v in same]

    def expand(first, last):
        got = call(
            functools.partial(second_matmul, first, last),
            [shape(piece // 2, feats)] * (2 * (last - first)),
            [idx] + same + other + [w_down],
            "s" + "v" * (2 * NY + 1),
            scratch=[pltpu.VMEM((total, width), bf16), pltpu.VMEM(((last - first) * piece, feats), bf16)],
            flops=2 * (last - first) * piece * feats * width,
            moved=2 * feats * width,
        )
        return {j: got[2 * i : 2 * i + 2] for i, j in enumerate(ORDER[first:last])}

    terms = {**expand(EARLY, NZ), **expand(0, EARLY)}

    def chain(half, way, steps):
        got = terms[way * steps if steps < NZ // 2 else steps][half]
        for step in range(steps, 1, -1):
            got = shift(got, "z", way, NZ)
            own = terms[way * (step - 1)][half]
            got = call(add, shape(piece // 2, feats), [got, own], "vv", moved=6 * piece * feats // 2)
        return shift(got, "z", way, NZ)

    far = NZ // 2
    low = [chain(0, -1, far), chain(0, 1, far - 1)]
    high = [chain(1, 1, far), chain(1, -1, far - 1)]
    mine, one = call(
        z_sum, [shape(rows, feats, kind=f32), shape(rows, feats)], [terms[0][0]] + low, "vvv", moved=4 * piece * feats
    )
    two, three = call(z_sum, [shape(rows, feats)] * 2, [terms[0][1]] + high, "vvv", moved=4 * piece * feats)
    parts = [shift(v, "x", -k, NX) for k, v in enumerate([one, two, three], 1)]
    return call(finish, shape(rows, feats), [stream, mine] + parts, "v" * 5, moved=20 * rows * feats)


def solution(mesh):
    fine = Mesh(mesh.devices.reshape(NX, NZ, NY, NC), ("x", "z", "y", "core"))
    pool = ("x", "z")
    placed = (
        P(pool, TP),
        P(pool, TP),
        P(pool, None, TP),
        P(pool, None, TP),
        P(pool, TP),
        P(pool, TP),
        P(pool),
        P(TP),
        P(TP, pool),
        P(TP, pool),
        P(pool, TP),
    )
    return jax.shard_map(shards, mesh=fine, in_specs=placed, out_specs=P(pool, TP), check_vma=False)
```

```python
import functools

import jax
import jax.numpy as jnp
from jax import lax
from jax.experimental import pallas as pl
from jax.experimental.pallas import tpu as pltpu
from jax.sharding import Mesh
from jax.sharding import PartitionSpec as P

D = 16384
HEAD_DIM = 128
NX, NZ, NY, NC = 4, 8, 4, 2
TP = ("y", "core")
MARKS = 128
MIB = 1 << 20
ORDER = (0, -1, 1, -2, 2, -3, 3, 4)
EARLY = 4
FAR = 5
AWAY = (2, 1, 3)


def shift(v, axis, by, n):
    return lax.ppermute(v, axis, [(i, (i + by) % n) for i in range(n)])


def rows_at(start, count):
    return pl.ds(pl.multiple_of(start, count), count)


def call(kernel, outs, args, kinds, scratch=(), flops=0, moved=0, limit=16 * MIB, alias=None):
    spaces = {"s": pltpu.SMEM, "v": pltpu.VMEM, "h": pltpu.HBM}
    single = not isinstance(outs, (list, tuple))
    whole = [outs] if single else list(outs)
    got = pl.pallas_call(
        kernel,
        out_shape=whole,
        in_specs=[pl.BlockSpec(memory_space=spaces[k]) for k in kinds],
        out_specs=[pl.BlockSpec(memory_space=pltpu.VMEM)] * len(whole),
        scratch_shapes=list(scratch),
        input_output_aliases=alias or {},
        compiler_params=pltpu.CompilerParams(vmem_limit_bytes=limit),
        cost_estimate=pl.CostEstimate(flops=flops, bytes_accessed=moved, transcendentals=0),
    )(*args)
    return got[0] if single else got


def shape(*dims, kind=jnp.bfloat16):
    return jax.ShapeDtypeStruct(dims, kind)


def copy_in(pairs, sems):
    copies = [pltpu.make_async_copy(src, dst, sems.at[i]) for i, (src, dst) in enumerate(pairs)]
    for copy in copies:
        copy.start()
    for copy in copies:
        copy.wait()


def copy_in(pairs, sems):
    copies = [pltpu.make_async_copy(src, dst, sems.at[i]) for i, (src, dst) in enumerate(pairs)]
    for copy in copies:
        copy.start()
    for copy in copies:
        copy.wait()


def start_rows(scale, lengths_in, hidden_in, queries_in, keys_in, values_in, own_keys_in, own_values_in, gain_in, *rest):
    stream, inv_gain2, out, lengths, hidden, queries, keys, values, own_keys, own_values, gain, heads, work, low, sems = rest
    copy_in(
        [
            (queries_in, queries),
            (lengths_in, lengths),
            (keys_in, keys),
            (values_in, values),
            (own_keys_in, own_keys),
            (own_values_in, own_values),
            (hidden_in, hidden),
            (gain_in, gain),
        ],
        sems,
    )
    rows, feats = hidden.shape
    per = feats // HEAD_DIM
    ctx = keys.shape[1]
    f32, bf16 = jnp.float32, jnp.bfloat16
    wide = queries[...].astype(f32)
    for h in range(per):
        heads[pl.ds(h, rows, stride=per), :] = wide[:, h * HEAD_DIM : (h + 1) * HEAD_DIM]
    slot = lax.broadcasted_iota(jnp.int32, (per, ctx), 1)

    def spread(ref):
        each = ref[...].astype(f32)
        return jnp.concatenate(
            [jnp.broadcast_to(each[r : r + 1, :], (per, HEAD_DIM)) for r in range(rows)], axis=0
        )

    for r in range(rows):
        score = lax.dot_general(
            heads[pl.ds(r * per, per), :].astype(bf16),
            keys[r],
            (((1,), (1,)), ((), ())),
            preferred_element_type=f32,
        )
        work[pl.ds(r * per, per), :] = jnp.where(slot < lengths[r], score * scale, -1e30)
    own = jnp.sum(heads[...] * spread(own_keys), axis=1, keepdims=True) * scale
    score = work[...]
    top = jnp.maximum(jnp.max(score, axis=1, keepdims=True), own)
    weight = jnp.exp(score - top)
    own_weight = jnp.exp(own - top)
    total = jnp.sum(weight, axis=1, keepdims=True) + own_weight
    low[...] = weight.astype(bf16)
    for r in range(rows):
        work[pl.ds(r * per, per), :] = jnp.dot(low[pl.ds(r * per, per), :], values[r], preferred_element_type=f32)
    work[...] = (work[...] + own_weight.astype(bf16).astype(f32) * spread(own_values)) / total
    scales = gain[...].astype(f32)
    inv_gain2[...] = 1.0 / (scales * scales)
    for h in range(per):
        cols = slice(h * HEAD_DIM, (h + 1) * HEAD_DIM)
        got = hidden[:, cols].astype(f32) + work[pl.ds(h, rows, stride=per), :]
        stream[:, cols] = got
        out[:, cols] = (got * scales[h : h + 1, :]).astype(bf16)


def seat(own, out):
    out[pl.ds(0, own.shape[0]), :] = own[...]


def join(first, *refs):
    parts, out = refs[:-1], refs[-1]
    size = parts[0].shape[0]
    for k, part in enumerate(parts, 1):
        out[pl.ds(k * size, size), :] = part[...]


def place(core, pieces, part):
    top = part.shape[0] // 2
    at = 0
    spare = []
    for piece in pieces:
        half = piece.shape[0] // 2
        if piece.shape[0] < pieces[0].shape[0]:
            spare.append(piece)
            continue
        part[pl.ds(at, half), :] = piece[rows_at(core * half, half), :]
        part[pl.ds(top + at, half), :] = piece[rows_at((1 - core) * half, half), :]
        at += half
    for i, piece in enumerate(spare):
        half = piece.shape[0]
        part[rows_at(lax.rem(core + i, NC) * top + at, half), :] = piece[...]


def squares(width, part, inv_gain2, keep, send):
    top = part.shape[0] // 2
    step = 32
    lane = lax.broadcasted_iota(jnp.int32, (step, MARKS), 1)
    for i in range(2 * top // step):
        sums = 0.0
        for h in range(part.shape[1] // HEAD_DIM):
            wide = part[pl.ds(i * step, step), pl.ds(h * HEAD_DIM, HEAD_DIM)].astype(jnp.float32)
            sums = sums + wide * wide * inv_gain2[pl.ds(h, 1), :]
        sums = jnp.sum(sums, axis=1, keepdims=True)
        high = sums.astype(jnp.bfloat16).astype(jnp.float32)
        marks = jnp.where(lane == 0, high, jnp.where(lane == 1, sums - high, 0.0))
        out = keep if i * step < top else send
        out[pl.ds(i * step % top, step), pl.ds(2 * width, MARKS)] = marks.astype(jnp.bfloat16)


def project(weights, base, part, keep, send):
    top, width = part.shape[0] // 2, weights.shape[1]

    def tile(start, size):
        terms = jnp.dot(part[...], weights[:, pl.ds(start, size)], preferred_element_type=jnp.float32)
        keep[:, pl.ds(base + start, size)] = terms[:top].astype(jnp.bfloat16)
        send[:, pl.ds(base + start, size)] = terms[top:].astype(jnp.bfloat16)

    pl.loop(0, width // 256)(lambda t: tile(pl.multiple_of(t * 256, 256), 256))
    if width % 256:
        tile(width // 256 * 256, width % 256)


def gate_matmul(width, idx, *refs):
    pieces, (_, inv_gain2, w_gate, keep, send, part, done) = refs[:-7], refs[-7:]
    place(idx[3], pieces, part)
    squares(width, part, inv_gain2, keep, send)
    project(w_gate, 0, part, keep, send)
    done[...] = jnp.zeros_like(done)


def up_matmul(width, _, part, w_up, keep_in, send_in, keep, send):
    project(w_up, width, part, keep, send)


def halves(up, down, _, up_half, down_half):
    size = up_half.shape[0]
    up_half[...] = up[pl.ds(0, size), :]
    down_half[...] = down[pl.ds(size, size), :]


def core_sum(block, idx, keep, came, own, *outs):
    mine = idx[2]

    def summed(y):
        at = rows_at(y * block, block)
        return keep[at, :].astype(jnp.float32) + came[at, :].astype(jnp.float32)

    own[...] = summed(mine)
    for k, out in enumerate(outs, 1):
        out[...] = summed(lax.rem(mine + k, NY)).astype(jnp.bfloat16)


def activate(width, *refs):
    parts, hidden = refs[:-1], refs[-1]
    block = parts[0].shape[0]
    for i in range(2):
        own, one, two, three = parts[i * NY : (i + 1) * NY]
        sums = own[...] + one[...].astype(jnp.float32) + two[...].astype(jnp.float32) + three[...].astype(jnp.float32)
        meansq = jnp.sum(sums[:, 2 * width :], axis=1, keepdims=True) / D
        inv = lax.rsqrt(meansq + 1e-05)
        gate = sums[:, :width] * inv
        up = sums[:, width : 2 * width] * inv
        hidden[pl.ds(i * block, block), :] = (gate / (1.0 + jnp.exp(-gate)) * up).astype(jnp.bfloat16)


def second_matmul(first, last, idx, *refs):
    same, refs = refs[:NY], refs[NY:]
    other, refs = refs[:NY], refs[NY:]
    weights, outs, (hidden, terms) = refs[0], refs[1:-2], refs[-2:]
    mine, core = idx[2], idx[3]
    block = same[0].shape[0]
    half = block // 2
    for k in range(NY):
        y = lax.rem(mine - k + NY, NY)
        for i in range(2):
            at = (i * NY + y) * block
            hidden[rows_at(at + core * half, half), :] = same[k][pl.ds(i * half, half), :]
            hidden[rows_at(at + (1 - core) * half, half), :] = other[k][pl.ds(i * half, half), :]

    @pl.loop(0, weights.shape[1] // 256)
    def _(t):
        cols = pl.ds(pl.multiple_of(t * 256, 256), 256)
        some = hidden[pl.ds(first * block, (last - first) * block), :]
        terms[:, cols] = jnp.dot(some, weights[:, cols], preferred_element_type=jnp.float32).astype(jnp.bfloat16)

    at = 0
    for out in outs:
        size = out.shape[0]
        out[...] = terms[pl.ds(at, size), :]
        at += size


def add(came, own, *refs):
    out = refs[-1]
    out[...] = (came[...].astype(jnp.float32) + own[...].astype(jnp.float32)).astype(jnp.bfloat16)


def z_sum(own, one, two, *outs):
    rows = outs[0].shape[0]
    for k, out in enumerate(outs):
        at = pl.ds(k * rows, rows)
        total = own[at, :].astype(jnp.float32) + one[at, :].astype(jnp.float32) + two[at, :].astype(jnp.float32)
        out[...] = total.astype(out.dtype)


def finish(stream, mine, one, two, three, out):
    total = stream[...] + mine[...]
    for ref in (one, two, three):
        total = total + ref[...].astype(jnp.float32)
    out[...] = total.astype(jnp.bfloat16)


def shards(
    hidden_rows,
    queries,
    cache_keys,
    cache_values,
    new_keys,
    new_values,
    lengths,
    norm_gain,
    w_gate,
    w_up,
    w_down,
):
    f32, bf16 = jnp.float32, jnp.bfloat16
    rows, feats = hidden_rows.shape
    width = w_gate.shape[1]
    piece = rows * NX
    total = piece * NZ
    block = total // (NY * NC)
    wide = 2 * width + MARKS
    per = feats // HEAD_DIM
    idx = jnp.stack([lax.axis_index(a) for a in ("x", "z", "y", "core")]).astype(jnp.int32)
    given = [lengths, hidden_rows, queries, cache_keys, cache_values, new_keys, new_values, norm_gain.reshape(per, HEAD_DIM)]
    stream, inv_gain2, scaled = call(
        functools.partial(start_rows, HEAD_DIM ** (-0.5)),
        [shape(rows, feats, kind=f32), shape(per, HEAD_DIM, kind=f32), shape(rows, feats)],
        given,
        "h" * 8,
        scratch=[pltpu.SMEM(lengths.shape, jnp.int32)]
        + [pltpu.VMEM(v.shape, v.dtype) for v in given[1:]]
        + [pltpu.VMEM((rows * per, HEAD_DIM), f32)] * 2
        + [pltpu.VMEM((rows * per, HEAD_DIM), bf16)]
        + [pltpu.SemaphoreType.DMA((8,))],
        moved=4 * cache_keys.size,
        limit=60 * MIB,
    )

    own = call(seat, shape(piece, feats), [scaled], "v", moved=2 * rows * feats)
    from_x = {k: shift(scaled, "x", k, NX) for k in AWAY}
    own = call(
        join,
        shape(piece, feats),
        [own] + [from_x[k] for k in range(1, NX)],
        "v" * NX,
        moved=4 * piece * feats,
        alias={0: 0},
    )
    pieces = {0: own}
    up = down = own
    for step in range(1, NZ // 2):
        up = shift(up, "z", 1, NZ)
        down = shift(down, "z", -1, NZ)
        pieces[-step], pieces[step] = up, down

    def gates(some, after):
        size = sum(v.shape[0] for v in some)
        return call(
            functools.partial(gate_matmul, width),
            [shape(size // 2, wide)] * 2 + [shape(size, feats), shape(8, 128, kind=f32)],
            [idx] + some + [after, inv_gain2, w_gate],
            "s" + "v" * len(some) + "hvv",
            flops=2 * size * feats * width,
            moved=2 * feats * width,
        )

    def ups(keep, send, part, after):
        return call(
            functools.partial(up_matmul, width),
            [shape(*keep.shape)] * 2,
            [after, part, w_up, keep, send],
            "hvvvv",
            flops=2 * part.size * width,
            moved=2 * feats * width,
            alias={3: 0, 4: 1},
        )

    keep, send, part, done = gates([pieces[j] for j in ORDER[:EARLY]], pieces[2])
    up, down = call(halves, [shape(piece // 2, feats)] * 2, [up, down, done], "vvh", moved=4 * piece * feats)
    keep, send = ups(keep, send, part, up)
    up = shift(up, "z", 1, NZ)
    down = shift(down, "z", -1, NZ)

    def across(keep, send):
        came = shift(send, "core", 1, NC)
        own, *parts = call(
            functools.partial(core_sum, block // 2),
            [shape(block // 2, wide, kind=f32)] + [shape(block // 2, wide)] * (NY - 1),
            [idx, keep, came],
            "svv",
            moved=2 * total * wide,
        )
        got = {k: shift(parts[k - 1], "y", k, NY) for k in AWAY}
        return [own] + [got[k] for k in range(1, NY)]

    early = across(keep, send)
    keep, send, part, _ = gates([pieces[j] for j in ORDER[EARLY:-1]] + [up, down], early[0])
    keep, send = ups(keep, send, part, early[2])
    late = across(keep, send)
    hidden = call(functools.partial(activate, width), shape(block, width), early + late, "v" * 2 * NY, moved=10 * block * wide)
    same = {0: hidden, **{k: shift(hidden, "y", k, NY) for k in AWAY}}
    other = {k: shift(v, "core", 1, NC) for k, v in same.items()}
    same, other = ([v[k] for k in range(NY)] for v in (same, other))

    def expand(first, last):
        got = call(
            functools.partial(second_matmul, first, last),
            [shape(piece // 2, feats)] * (2 * (last - first)),
            [idx] + same + other + [w_down],
            "s" + "v" * (2 * NY + 1),
            scratch=[pltpu.VMEM((total, width), bf16), pltpu.VMEM(((last - first) * piece, feats), bf16)],
            flops=2 * (last - first) * piece * feats * width,
            moved=2 * feats * width,
        )
        return {j: got[2 * i : 2 * i + 2] for i, j in enumerate(ORDER[first:last])}

    terms = {**expand(FAR, NZ), **expand(0, FAR)}

    def chain(half, way, steps):
        got = terms[way * steps if steps < NZ // 2 else steps][half]
        for step in range(steps, 1, -1):
            got = shift(got, "z", way, NZ)
            own = terms[way * (step - 1)][half]
            after = [terms[0][0]] if step == steps else []
            got = call(add, shape(piece // 2, feats), [got, own] + after, "vvh"[: 2 + len(after)], moved=3 * piece * feats)
        return shift(got, "z", way, NZ)

    far = NZ // 2
    low = [chain(0, -1, far), chain(0, 1, far - 1)]
    high = [chain(1, 1, far), chain(1, -1, far - 1)]
    mine, one = call(
        z_sum, [shape(rows, feats, kind=f32), shape(rows, feats)], [terms[0][0]] + low, "vvv", moved=4 * piece * feats
    )
    two, three = call(z_sum, [shape(rows, feats)] * 2, [terms[0][1]] + high, "vvv", moved=4 * piece * feats)
    sent = {1: one, 2: two, 3: three}
    parts = {k: shift(sent[k], "x", -k, NX) for k in AWAY}
    return call(finish, shape(rows, feats), [stream, mine] + [parts[k] for k in range(1, NX)], "v" * 5, moved=20 * rows * feats)


def solution(mesh):
    fine = Mesh(mesh.devices.reshape(NX, NZ, NY, NC), ("x", "z", "y", "core"))
    pool = ("x", "z")
    placed = (
        P(pool, TP),
        P(pool, TP),
        P(pool, None, TP),
        P(pool, None, TP),
        P(pool, TP),
        P(pool, TP),
        P(pool),
        P(TP),
        P(TP, pool),
        P(TP, pool),
        P(pool, TP),
    )
    return jax.shard_map(shards, mesh=fine, in_specs=placed, out_specs=P(pool, TP), check_vma=False)
```

```python
import functools

import jax
import jax.numpy as jnp
from jax import lax
from jax.experimental import pallas as pl
from jax.experimental.pallas import tpu as pltpu
from jax.sharding import Mesh
from jax.sharding import PartitionSpec as P

D = 16384
HEAD_DIM = 128
NX, NZ, NY, NC = 4, 8, 4, 2
TP = ("y", "core")
MARKS = 128
MIB = 1 << 20
ORDER = (0, -1, 1, -2, 2, -3, 3, 4)
EARLY = 4
FAR = 5
AWAY = (2, 1, 3)


def shift(v, axis, by, n):
    return lax.ppermute(v, axis, [(i, (i + by) % n) for i in range(n)])


def rows_at(start, count):
    return pl.ds(pl.multiple_of(start, count), count)


def call(kernel, outs, args, kinds, scratch=(), flops=0, moved=0, limit=16 * MIB, alias=None):
    spaces = {"s": pltpu.SMEM, "v": pltpu.VMEM, "h": pltpu.HBM}
    single = not isinstance(outs, (list, tuple))
    whole = [outs] if single else list(outs)
    got = pl.pallas_call(
        kernel,
        out_shape=whole,
        in_specs=[pl.BlockSpec(memory_space=spaces[k]) for k in kinds],
        out_specs=[pl.BlockSpec(memory_space=pltpu.VMEM)] * len(whole),
        scratch_shapes=list(scratch),
        input_output_aliases=alias or {},
        compiler_params=pltpu.CompilerParams(vmem_limit_bytes=limit),
        cost_estimate=pl.CostEstimate(flops=flops, bytes_accessed=moved, transcendentals=0),
    )(*args)
    return got[0] if single else got


def shape(*dims, kind=jnp.bfloat16):
    return jax.ShapeDtypeStruct(dims, kind)


def copy_in(pairs, sems):
    copies = [pltpu.make_async_copy(src, dst, sems.at[i]) for i, (src, dst) in enumerate(pairs)]
    for copy in copies:
        copy.start()
    for copy in copies:
        copy.wait()


def copy_in(pairs, sems):
    copies = [pltpu.make_async_copy(src, dst, sems.at[i]) for i, (src, dst) in enumerate(pairs)]
    for copy in copies:
        copy.start()
    for copy in copies:
        copy.wait()


def start_rows(scale, lengths_in, hidden_in, queries_in, keys_in, values_in, own_keys_in, own_values_in, gain_in, *rest):
    stream, inv_gain2, out, lengths, hidden, queries, keys, values, own_keys, own_values, gain, heads, work, low, sems = rest
    copy_in(
        [
            (queries_in, queries),
            (lengths_in, lengths),
            (keys_in, keys),
            (values_in, values),
            (own_keys_in, own_keys),
            (own_values_in, own_values),
            (hidden_in, hidden),
            (gain_in, gain),
        ],
        sems,
    )
    rows, feats = hidden.shape
    per = feats // HEAD_DIM
    ctx = keys.shape[1]
    f32, bf16 = jnp.float32, jnp.bfloat16
    wide = queries[...].astype(f32)
    for h in range(per):
        heads[pl.ds(h, rows, stride=per), :] = wide[:, h * HEAD_DIM : (h + 1) * HEAD_DIM]
    slot = lax.broadcasted_iota(jnp.int32, (per, ctx), 1)

    def spread(ref):
        each = ref[...].astype(f32)
        return jnp.concatenate(
            [jnp.broadcast_to(each[r : r + 1, :], (per, HEAD_DIM)) for r in range(rows)], axis=0
        )

    for r in range(rows):
        score = lax.dot_general(
            heads[pl.ds(r * per, per), :].astype(bf16),
            keys[r],
            (((1,), (1,)), ((), ())),
            preferred_element_type=f32,
        )
        work[pl.ds(r * per, per), :] = jnp.where(slot < lengths[r], score * scale, -1e30)
    own = jnp.sum(heads[...] * spread(own_keys), axis=1, keepdims=True) * scale
    score = work[...]
    top = jnp.maximum(jnp.max(score, axis=1, keepdims=True), own)
    weight = jnp.exp(score - top)
    own_weight = jnp.exp(own - top)
    total = jnp.sum(weight, axis=1, keepdims=True) + own_weight
    low[...] = weight.astype(bf16)
    for r in range(rows):
        work[pl.ds(r * per, per), :] = jnp.dot(low[pl.ds(r * per, per), :], values[r], preferred_element_type=f32)
    work[...] = (work[...] + own_weight.astype(bf16).astype(f32) * spread(own_values)) / total
    scales = gain[...].astype(f32)
    inv_gain2[...] = 1.0 / (scales * scales)
    for h in range(per):
        cols = slice(h * HEAD_DIM, (h + 1) * HEAD_DIM)
        got = hidden[:, cols].astype(f32) + work[pl.ds(h, rows, stride=per), :]
        stream[:, cols] = got
        out[:, cols] = (got * scales[h : h + 1, :]).astype(bf16)


def seat(own, out):
    out[pl.ds(0, own.shape[0]), :] = own[...]


def join(first, *refs):
    parts, out = refs[:-1], refs[-1]
    size = parts[0].shape[0]
    for k, part in enumerate(parts, 1):
        out[pl.ds(k * size, size), :] = part[...]


def place(core, pieces, part):
    top = part.shape[0] // 2
    at = 0
    spare = []
    for piece in pieces:
        half = piece.shape[0] // 2
        if piece.shape[0] < pieces[0].shape[0]:
            spare.append(piece)
            continue
        part[pl.ds(at, half), :] = piece[rows_at(core * half, half), :]
        part[pl.ds(top + at, half), :] = piece[rows_at((1 - core) * half, half), :]
        at += half
    for i, piece in enumerate(spare):
        half = piece.shape[0]
        part[rows_at(lax.rem(core + i, NC) * top + at, half), :] = piece[...]


def squares(width, part, inv_gain2, keep, send):
    top = part.shape[0] // 2
    step = 32
    lane = lax.broadcasted_iota(jnp.int32, (step, MARKS), 1)
    for i in range(2 * top // step):
        sums = 0.0
        for h in range(part.shape[1] // HEAD_DIM):
            wide = part[pl.ds(i * step, step), pl.ds(h * HEAD_DIM, HEAD_DIM)].astype(jnp.float32)
            sums = sums + wide * wide * inv_gain2[pl.ds(h, 1), :]
        sums = jnp.sum(sums, axis=1, keepdims=True)
        high = sums.astype(jnp.bfloat16).astype(jnp.float32)
        marks = jnp.where(lane == 0, high, jnp.where(lane == 1, sums - high, 0.0))
        out = keep if i * step < top else send
        out[pl.ds(i * step % top, step), pl.ds(2 * width, MARKS)] = marks.astype(jnp.bfloat16)


def project(weights, base, part, keep, send):
    top, width = part.shape[0] // 2, weights.shape[1]

    def tile(start, size):
        terms = jnp.dot(part[...], weights[:, pl.ds(start, size)], preferred_element_type=jnp.float32)
        keep[:, pl.ds(base + start, size)] = terms[:top].astype(jnp.bfloat16)
        send[:, pl.ds(base + start, size)] = terms[top:].astype(jnp.bfloat16)

    pl.loop(0, width // 256)(lambda t: tile(pl.multiple_of(t * 256, 256), 256))
    if width % 256:
        tile(width // 256 * 256, width % 256)


def gate_matmul(width, idx, *refs):
    pieces, (_, inv_gain2, w_gate, keep, send, part, done) = refs[:-7], refs[-7:]
    place(idx[3], pieces, part)
    squares(width, part, inv_gain2, keep, send)
    project(w_gate, 0, part, keep, send)
    done[...] = jnp.zeros_like(done)


def up_matmul(width, _, part, w_up, keep_in, send_in, keep, send):
    project(w_up, width, part, keep, send)


def halves(up, down, _, up_half, down_half):
    size = up_half.shape[0]
    up_half[...] = up[pl.ds(0, size), :]
    down_half[...] = down[pl.ds(size, size), :]


def core_sum(block, idx, keep, came, own, *outs):
    mine = idx[2]

    def summed(y):
        at = rows_at(y * block, block)
        return keep[at, :].astype(jnp.float32) + came[at, :].astype(jnp.float32)

    own[...] = summed(mine)
    for k, out in enumerate(outs, 1):
        out[...] = summed(lax.rem(mine + k, NY)).astype(jnp.bfloat16)


def activate(width, *refs):
    parts, hidden = refs[:-1], refs[-1]
    block = parts[0].shape[0]
    for i in range(2):
        own, one, two, three = parts[i * NY : (i + 1) * NY]
        sums = own[...] + one[...].astype(jnp.float32) + two[...].astype(jnp.float32) + three[...].astype(jnp.float32)
        meansq = jnp.sum(sums[:, 2 * width :], axis=1, keepdims=True) / D
        inv = lax.rsqrt(meansq + 1e-05)
        gate = sums[:, :width] * inv
        up = sums[:, width : 2 * width] * inv
        hidden[pl.ds(i * block, block), :] = (gate / (1.0 + jnp.exp(-gate)) * up).astype(jnp.bfloat16)


def second_matmul(first, last, idx, *refs):
    same, refs = refs[:NY], refs[NY:]
    other, refs = refs[:NY], refs[NY:]
    weights, outs, hidden = refs[0], refs[1:-1], refs[-1]
    mine, core = idx[2], idx[3]
    block = same[0].shape[0]
    half = block // 2
    groups = range(first // NY, 2)
    for k in range(NY):
        y = lax.rem(mine - k + NY, NY)
        for i in groups:
            at = ((i - groups[0]) * NY + y) * block
            hidden[rows_at(at + core * half, half), :] = same[k][pl.ds(i * half, half), :]
            hidden[rows_at(at + (1 - core) * half, half), :] = other[k][pl.ds(i * half, half), :]
    some = pl.ds((first - groups[0] * NY) * block, (last - first) * block)

    @pl.loop(0, weights.shape[1] // 256)
    def _(t):
        cols = pl.ds(pl.multiple_of(t * 256, 256), 256)
        terms = jnp.dot(hidden[some, :], weights[:, cols], preferred_element_type=jnp.float32).astype(jnp.bfloat16)
        for i, out in enumerate(outs):
            out[:, cols] = terms[i * half : (i + 1) * half]


def add(came, own, *refs):
    out = refs[-1]
    out[...] = (came[...].astype(jnp.float32) + own[...].astype(jnp.float32)).astype(jnp.bfloat16)


def z_sum(own, one, two, *outs):
    rows = outs[0].shape[0]
    for k, out in enumerate(outs):
        at = pl.ds(k * rows, rows)
        total = own[at, :].astype(jnp.float32) + one[at, :].astype(jnp.float32) + two[at, :].astype(jnp.float32)
        out[...] = total.astype(out.dtype)


def finish(stream, mine, one, two, three, out):
    total = stream[...] + mine[...]
    for ref in (one, two, three):
        total = total + ref[...].astype(jnp.float32)
    out[...] = total.astype(jnp.bfloat16)


def shards(
    hidden_rows,
    queries,
    cache_keys,
    cache_values,
    new_keys,
    new_values,
    lengths,
    norm_gain,
    w_gate,
    w_up,
    w_down,
):
    f32, bf16 = jnp.float32, jnp.bfloat16
    rows, feats = hidden_rows.shape
    width = w_gate.shape[1]
    piece = rows * NX
    total = piece * NZ
    block = total // (NY * NC)
    wide = 2 * width + MARKS
    per = feats // HEAD_DIM
    idx = jnp.stack([lax.axis_index(a) for a in ("x", "z", "y", "core")]).astype(jnp.int32)
    given = [lengths, hidden_rows, queries, cache_keys, cache_values, new_keys, new_values, norm_gain.reshape(per, HEAD_DIM)]
    stream, inv_gain2, scaled = call(
        functools.partial(start_rows, HEAD_DIM ** (-0.5)),
        [shape(rows, feats, kind=f32), shape(per, HEAD_DIM, kind=f32), shape(rows, feats)],
        given,
        "h" * 8,
        scratch=[pltpu.SMEM(lengths.shape, jnp.int32)]
        + [pltpu.VMEM(v.shape, v.dtype) for v in given[1:]]
        + [pltpu.VMEM((rows * per, HEAD_DIM), f32)] * 2
        + [pltpu.VMEM((rows * per, HEAD_DIM), bf16)]
        + [pltpu.SemaphoreType.DMA((8,))],
        moved=4 * cache_keys.size,
        limit=60 * MIB,
    )

    own = call(seat, shape(piece, feats), [scaled], "v", moved=2 * rows * feats)
    from_x = {k: shift(scaled, "x", k, NX) for k in AWAY}
    own = call(
        join,
        shape(piece, feats),
        [own] + [from_x[k] for k in range(1, NX)],
        "v" * NX,
        moved=4 * piece * feats,
        alias={0: 0},
    )
    pieces = {0: own}
    up = down = own
    for step in range(1, NZ // 2):
        up = shift(up, "z", 1, NZ)
        down = shift(down, "z", -1, NZ)
        pieces[-step], pieces[step] = up, down

    def gates(some, after):
        size = sum(v.shape[0] for v in some)
        return call(
            functools.partial(gate_matmul, width),
            [shape(size // 2, wide)] * 2 + [shape(size, feats), shape(8, 128, kind=f32)],
            [idx] + some + [after, inv_gain2, w_gate],
            "s" + "v" * len(some) + "hvv",
            flops=2 * size * feats * width,
            moved=2 * feats * width,
        )

    def ups(keep, send, part, after):
        return call(
            functools.partial(up_matmul, width),
            [shape(*keep.shape)] * 2,
            [after, part, w_up, keep, send],
            "hvvvv",
            flops=2 * part.size * width,
            moved=2 * feats * width,
            alias={3: 0, 4: 1},
        )

    keep, send, part, done = gates([pieces[j] for j in ORDER[:EARLY]], pieces[2])
    up, down = call(halves, [shape(piece // 2, feats)] * 2, [up, down, done], "vvh", moved=4 * piece * feats)
    keep, send = ups(keep, send, part, up)
    up = shift(up, "z", 1, NZ)
    down = shift(down, "z", -1, NZ)

    def across(keep, send):
        came = shift(send, "core", 1, NC)
        own, *parts = call(
            functools.partial(core_sum, block // 2),
            [shape(block // 2, wide, kind=f32)] + [shape(block // 2, wide)] * (NY - 1),
            [idx, keep, came],
            "svv",
            moved=2 * total * wide,
        )
        got = {k: shift(parts[k - 1], "y", k, NY) for k in AWAY}
        return [own] + [got[k] for k in range(1, NY)]

    early = across(keep, send)
    keep, send, part, _ = gates([pieces[j] for j in ORDER[EARLY:-1]] + [up, down], idx)
    keep, send = ups(keep, send, part, idx)
    late = across(keep, send)
    hidden = call(functools.partial(activate, width), shape(block, width), early + late, "v" * 2 * NY, moved=10 * block * wide)
    same = {0: hidden, **{k: shift(hidden, "y", k, NY) for k in AWAY}}
    other = {k: shift(v, "core", 1, NC) for k, v in same.items()}
    same, other = ([v[k] for k in range(NY)] for v in (same, other))

    def expand(first, last):
        got = call(
            functools.partial(second_matmul, first, last),
            [shape(piece // 2, feats)] * (2 * (last - first)),
            [idx] + same + other + [w_down],
            "s" + "v" * (2 * NY + 1),
            scratch=[pltpu.VMEM((total - first // NY * NY * piece, width), bf16)],
            flops=2 * (last - first) * piece * feats * width,
            moved=2 * feats * width,
        )
        return {j: got[2 * i : 2 * i + 2] for i, j in enumerate(ORDER[first:last])}

    terms = {**expand(FAR, NZ), **expand(0, FAR)}

    def chain(half, way, steps):
        got = terms[way * steps if steps < NZ // 2 else steps][half]
        for step in range(steps, 1, -1):
            got = shift(got, "z", way, NZ)
            own = terms[way * (step - 1)][half]
            after = [terms[0][0]] if step == steps else []
            got = call(add, shape(piece // 2, feats), [got, own] + after, "vvh"[: 2 + len(after)], moved=3 * piece * feats)
        return shift(got, "z", way, NZ)

    far = NZ // 2
    low = [chain(0, -1, far), chain(0, 1, far - 1)]
    high = [chain(1, 1, far), chain(1, -1, far - 1)]
    mine, one = call(
        z_sum, [shape(rows, feats, kind=f32), shape(rows, feats)], [terms[0][0]] + low, "vvv", moved=4 * piece * feats
    )
    two, three = call(z_sum, [shape(rows, feats)] * 2, [terms[0][1]] + high, "vvv", moved=4 * piece * feats)
    sent = {1: one, 2: two, 3: three}
    parts = {k: shift(sent[k], "x", -k, NX) for k in AWAY}
    return call(finish, shape(rows, feats), [stream, mine] + [parts[k] for k in range(1, NX)], "v" * 5, moved=20 * rows * feats)


def solution(mesh):
    fine = Mesh(mesh.devices.reshape(NX, NZ, NY, NC), ("x", "z", "y", "core"))
    pool = ("x", "z")
    placed = (
        P(pool, TP),
        P(pool, TP),
        P(pool, None, TP),
        P(pool, None, TP),
        P(pool, TP),
        P(pool, TP),
        P(pool),
        P(TP),
        P(TP, pool),
        P(TP, pool),
        P(pool, TP),
    )
    return jax.shard_map(shards, mesh=fine, in_specs=placed, out_specs=P(pool, TP), check_vma=False)
```

```python
import functools

import jax
import jax.numpy as jnp
from jax import lax
from jax.experimental import pallas as pl
from jax.experimental.pallas import tpu as pltpu
from jax.sharding import Mesh
from jax.sharding import PartitionSpec as P

D = 16384
HEAD_DIM = 128
NX, NZ, NY, NC = 4, 8, 4, 2
TP = ("y", "core")
MARKS = 128
MIB = 1 << 20
ORDER = (0, -1, 1, -2, 2, -3, 3, 4)
EARLY = 4
FAR = 5
AWAY = (2, 1, 3)


def shift(v, axis, by, n):
    return lax.ppermute(v, axis, [(i, (i + by) % n) for i in range(n)])


def rows_at(start, count):
    return pl.ds(pl.multiple_of(start, count), count)


def call(kernel, outs, args, kinds, scratch=(), flops=0, moved=0, limit=16 * MIB, alias=None):
    spaces = {"s": pltpu.SMEM, "v": pltpu.VMEM, "h": pltpu.HBM}
    single = not isinstance(outs, (list, tuple))
    whole = [outs] if single else list(outs)
    got = pl.pallas_call(
        kernel,
        out_shape=whole,
        in_specs=[pl.BlockSpec(memory_space=spaces[k]) for k in kinds],
        out_specs=[pl.BlockSpec(memory_space=pltpu.VMEM)] * len(whole),
        scratch_shapes=list(scratch),
        input_output_aliases=alias or {},
        compiler_params=pltpu.CompilerParams(vmem_limit_bytes=limit),
        cost_estimate=pl.CostEstimate(flops=flops, bytes_accessed=moved, transcendentals=0),
    )(*args)
    return got[0] if single else got


def shape(*dims, kind=jnp.bfloat16):
    return jax.ShapeDtypeStruct(dims, kind)


def copy_in(pairs, sems):
    copies = [pltpu.make_async_copy(src, dst, sems.at[i]) for i, (src, dst) in enumerate(pairs)]
    for copy in copies:
        copy.start()
    for copy in copies:
        copy.wait()


def copy_in(pairs, sems):
    copies = [pltpu.make_async_copy(src, dst, sems.at[i]) for i, (src, dst) in enumerate(pairs)]
    for copy in copies:
        copy.start()
    for copy in copies:
        copy.wait()


def start_rows(scale, lengths_in, hidden_in, queries_in, keys_in, values_in, own_keys_in, own_values_in, gain_in, *rest):
    stream, inv_gain2, out, lengths, hidden, queries, keys, values, own_keys, own_values, gain, heads, work, low, sems = rest
    copy_in(
        [
            (queries_in, queries),
            (lengths_in, lengths),
            (keys_in, keys),
            (values_in, values),
            (own_keys_in, own_keys),
            (own_values_in, own_values),
            (hidden_in, hidden),
            (gain_in, gain),
        ],
        sems,
    )
    rows, feats = hidden.shape
    per = feats // HEAD_DIM
    ctx = keys.shape[1]
    f32, bf16 = jnp.float32, jnp.bfloat16
    wide = queries[...].astype(f32)
    for h in range(per):
        heads[pl.ds(h, rows, stride=per), :] = wide[:, h * HEAD_DIM : (h + 1) * HEAD_DIM]
    slot = lax.broadcasted_iota(jnp.int32, (per, ctx), 1)

    def spread(ref):
        each = ref[...].astype(f32)
        return jnp.concatenate(
            [jnp.broadcast_to(each[r : r + 1, :], (per, HEAD_DIM)) for r in range(rows)], axis=0
        )

    for r in range(rows):
        score = lax.dot_general(
            heads[pl.ds(r * per, per), :].astype(bf16),
            keys[r],
            (((1,), (1,)), ((), ())),
            preferred_element_type=f32,
        )
        work[pl.ds(r * per, per), :] = jnp.where(slot < lengths[r], score * scale, -1e30)
    own = jnp.sum(heads[...] * spread(own_keys), axis=1, keepdims=True) * scale
    score = work[...]
    top = jnp.maximum(jnp.max(score, axis=1, keepdims=True), own)
    weight = jnp.exp(score - top)
    own_weight = jnp.exp(own - top)
    total = jnp.sum(weight, axis=1, keepdims=True) + own_weight
    low[...] = weight.astype(bf16)
    for r in range(rows):
        work[pl.ds(r * per, per), :] = jnp.dot(low[pl.ds(r * per, per), :], values[r], preferred_element_type=f32)
    work[...] = (work[...] + own_weight.astype(bf16).astype(f32) * spread(own_values)) / total
    scales = gain[...].astype(f32)
    inv_gain2[...] = 1.0 / (scales * scales)
    for h in range(per):
        cols = slice(h * HEAD_DIM, (h + 1) * HEAD_DIM)
        got = hidden[:, cols].astype(f32) + work[pl.ds(h, rows, stride=per), :]
        stream[:, cols] = got
        out[:, cols] = (got * scales[h : h + 1, :]).astype(bf16)


def seat(own, out):
    out[pl.ds(0, own.shape[0]), :] = own[...]


def join(first, *refs):
    parts, out = refs[:-1], refs[-1]
    size = parts[0].shape[0]
    for k, part in enumerate(parts, 1):
        out[pl.ds(k * size, size), :] = part[...]


def place(core, pieces, part):
    top = part.shape[0] // 2
    for i, piece in enumerate(pieces):
        half = piece.shape[0] // 2
        at = i * half
        part[pl.ds(at, half), :] = piece[rows_at(core * half, half), :]
        part[pl.ds(top + at, half), :] = piece[rows_at((1 - core) * half, half), :]


def squares(width, part, inv_gain2, keep, send, row):
    top = part.shape[0] // 2
    step = 32
    lane = lax.broadcasted_iota(jnp.int32, (step, MARKS), 1)
    for i in range(2 * top // step):
        sums = 0.0
        for h in range(part.shape[1] // HEAD_DIM):
            wide = part[pl.ds(i * step, step), pl.ds(h * HEAD_DIM, HEAD_DIM)].astype(jnp.float32)
            sums = sums + wide * wide * inv_gain2[pl.ds(h, 1), :]
        sums = jnp.sum(sums, axis=1, keepdims=True)
        high = sums.astype(jnp.bfloat16).astype(jnp.float32)
        marks = jnp.where(lane == 0, high, jnp.where(lane == 1, sums - high, 0.0))
        out = keep if i * step < top else send
        out[pl.ds(row + i * step % top, step), pl.ds(2 * width, MARKS)] = marks.astype(jnp.bfloat16)


def project(weights, base, part, keep, send, row):
    top, width = part.shape[0] // 2, weights.shape[1]
    to = pl.ds(row, top)

    def tile(start, size):
        terms = jnp.dot(part[...], weights[:, pl.ds(start, size)], preferred_element_type=jnp.float32)
        keep[to, pl.ds(base + start, size)] = terms[:top].astype(jnp.bfloat16)
        send[to, pl.ds(base + start, size)] = terms[top:].astype(jnp.bfloat16)

    pl.loop(0, width // 256)(lambda t: tile(pl.multiple_of(t * 256, 256), 256))
    if width % 256:
        tile(width // 256 * 256, width % 256)


def gate_matmul(width, idx, *refs):
    pieces, (_, inv_gain2, w_gate, keep, send, part, done) = refs[:-7], refs[-7:]
    place(idx[3], pieces, part)
    squares(width, part, inv_gain2, keep, send, 0)
    project(w_gate, 0, part, keep, send, 0)
    done[...] = jnp.zeros_like(done)


def up_matmul(width, _, part, w_up, keep_in, send_in, keep, send):
    project(w_up, width, part, keep, send, 0)


def middle_matmul(width, idx, *refs):
    pieces, (_, inv_gain2, w_gate, w_up, keep, send, _, part) = refs[:-8], refs[-8:]
    place(idx[3], pieces, part)
    squares(width, part, inv_gain2, keep, send, 0)
    project(w_gate, 0, part, keep, send, 0)
    project(w_up, width, part, keep, send, 0)


def last_matmul(width, idx, low, high, inv_gain2, w_gate, w_up, keep_in, send_in, keep, send, part):
    core = idx[3]
    half = low.shape[0]
    part[rows_at(core * half, half), :] = low[...]
    part[rows_at((1 - core) * half, half), :] = high[...]
    row = keep.shape[0] - half
    squares(width, part, inv_gain2, keep, send, row)
    project(w_gate, 0, part, keep, send, row)
    project(w_up, width, part, keep, send, row)


def halves(up, down, _, up_half, down_half):
    size = up_half.shape[0]
    up_half[...] = up[pl.ds(0, size), :]
    down_half[...] = down[pl.ds(size, size), :]


def core_sum(block, idx, keep, came, own, *outs):
    mine = idx[2]

    def summed(y):
        at = rows_at(y * block, block)
        return keep[at, :].astype(jnp.float32) + came[at, :].astype(jnp.float32)

    own[...] = summed(mine)
    for k, out in enumerate(outs, 1):
        out[...] = summed(lax.rem(mine + k, NY)).astype(jnp.bfloat16)


def activate(width, *refs):
    parts, hidden = refs[:-1], refs[-1]
    block = parts[0].shape[0]
    for i in range(2):
        own, one, two, three = parts[i * NY : (i + 1) * NY]
        sums = own[...] + one[...].astype(jnp.float32) + two[...].astype(jnp.float32) + three[...].astype(jnp.float32)
        meansq = jnp.sum(sums[:, 2 * width :], axis=1, keepdims=True) / D
        inv = lax.rsqrt(meansq + 1e-05)
        gate = sums[:, :width] * inv
        up = sums[:, width : 2 * width] * inv
        hidden[pl.ds(i * block, block), :] = (gate / (1.0 + jnp.exp(-gate)) * up).astype(jnp.bfloat16)


def second_matmul(first, last, idx, *refs):
    same, refs = refs[:NY], refs[NY:]
    other, refs = refs[:NY], refs[NY:]
    weights, outs, hidden = refs[0], refs[1:-1], refs[-1]
    mine, core = idx[2], idx[3]
    block = same[0].shape[0]
    half = block // 2
    groups = range(first // NY, 2)
    for k in range(NY):
        y = lax.rem(mine - k + NY, NY)
        for i in groups:
            at = ((i - groups[0]) * NY + y) * block
            hidden[rows_at(at + core * half, half), :] = same[k][pl.ds(i * half, half), :]
            hidden[rows_at(at + (1 - core) * half, half), :] = other[k][pl.ds(i * half, half), :]
    some = pl.ds((first - groups[0] * NY) * block, (last - first) * block)

    @pl.loop(0, weights.shape[1] // 256)
    def _(t):
        cols = pl.ds(pl.multiple_of(t * 256, 256), 256)
        terms = jnp.dot(hidden[some, :], weights[:, cols], preferred_element_type=jnp.float32).astype(jnp.bfloat16)
        for i, out in enumerate(outs):
            out[:, cols] = terms[i * half : (i + 1) * half]


def add(came, own, *refs):
    out = refs[-1]
    out[...] = (came[...].astype(jnp.float32) + own[...].astype(jnp.float32)).astype(jnp.bfloat16)


def z_sum(own, one, two, *outs):
    rows = outs[0].shape[0]
    for k, out in enumerate(outs):
        at = pl.ds(k * rows, rows)
        total = own[at, :].astype(jnp.float32) + one[at, :].astype(jnp.float32) + two[at, :].astype(jnp.float32)
        out[...] = total.astype(out.dtype)


def finish(stream, mine, one, two, three, out):
    total = stream[...] + mine[...]
    for ref in (one, two, three):
        total = total + ref[...].astype(jnp.float32)
    out[...] = total.astype(jnp.bfloat16)


def shards(
    hidden_rows,
    queries,
    cache_keys,
    cache_values,
    new_keys,
    new_values,
    lengths,
    norm_gain,
    w_gate,
    w_up,
    w_down,
):
    f32, bf16 = jnp.float32, jnp.bfloat16
    rows, feats = hidden_rows.shape
    width = w_gate.shape[1]
    piece = rows * NX
    total = piece * NZ
    block = total // (NY * NC)
    wide = 2 * width + MARKS
    per = feats // HEAD_DIM
    idx = jnp.stack([lax.axis_index(a) for a in ("x", "z", "y", "core")]).astype(jnp.int32)
    given = [lengths, hidden_rows, queries, cache_keys, cache_values, new_keys, new_values, norm_gain.reshape(per, HEAD_DIM)]
    stream, inv_gain2, scaled = call(
        functools.partial(start_rows, HEAD_DIM ** (-0.5)),
        [shape(rows, feats, kind=f32), shape(per, HEAD_DIM, kind=f32), shape(rows, feats)],
        given,
        "h" * 8,
        scratch=[pltpu.SMEM(lengths.shape, jnp.int32)]
        + [pltpu.VMEM(v.shape, v.dtype) for v in given[1:]]
        + [pltpu.VMEM((rows * per, HEAD_DIM), f32)] * 2
        + [pltpu.VMEM((rows * per, HEAD_DIM), bf16)]
        + [pltpu.SemaphoreType.DMA((8,))],
        moved=4 * cache_keys.size,
        limit=60 * MIB,
    )

    own = call(seat, shape(piece, feats), [scaled], "v", moved=2 * rows * feats)
    from_x = {k: shift(scaled, "x", k, NX) for k in AWAY}
    own = call(
        join,
        shape(piece, feats),
        [own] + [from_x[k] for k in range(1, NX)],
        "v" * NX,
        moved=4 * piece * feats,
        alias={0: 0},
    )
    pieces = {0: own}
    up = down = own
    for step in range(1, NZ // 2):
        up = shift(up, "z", 1, NZ)
        down = shift(down, "z", -1, NZ)
        pieces[-step], pieces[step] = up, down

    def gates(some, after):
        size = sum(v.shape[0] for v in some)
        return call(
            functools.partial(gate_matmul, width),
            [shape(size // 2, wide)] * 2 + [shape(size, feats), shape(8, 128, kind=f32)],
            [idx] + some + [after, inv_gain2, w_gate],
            "s" + "v" * len(some) + "hvv",
            flops=2 * size * feats * width,
            moved=2 * feats * width,
        )

    def ups(keep, send, part, after):
        return call(
            functools.partial(up_matmul, width),
            [shape(*keep.shape)] * 2,
            [after, part, w_up, keep, send],
            "hvvvv",
            flops=2 * part.size * width,
            moved=2 * feats * width,
            alias={3: 0, 4: 1},
        )

    keep, send, part, done = gates([pieces[j] for j in ORDER[:EARLY]], pieces[2])
    up, down = call(halves, [shape(piece // 2, feats)] * 2, [up, down, done], "vvh", moved=4 * piece * feats)
    late = [pieces[j] for j in ORDER[EARLY:-1]]
    size = (NZ - EARLY) * piece
    keep, send = ups(keep, send, part, up)
    later, send_later, send = call(
        functools.partial(middle_matmul, width),
        [shape(size // 2, wide)] * 2 + [shape(*send.shape)],
        [idx] + late + [send, inv_gain2, w_gate, w_up],
        "s" + "v" * (len(late) + 4),
        scratch=[pltpu.VMEM((size - piece, feats), bf16)],
        flops=4 * (size - piece) * feats * width,
        moved=4 * feats * width,
        alias={1 + len(late): 2},
    )
    up = shift(up, "z", 1, NZ)
    down = shift(down, "z", -1, NZ)

    def across(keep, send):
        came = shift(send, "core", 1, NC)
        own, *parts = call(
            functools.partial(core_sum, block // 2),
            [shape(block // 2, wide, kind=f32)] + [shape(block // 2, wide)] * (NY - 1),
            [idx, keep, came],
            "svv",
            moved=2 * total * wide,
        )
        got = {k: shift(parts[k - 1], "y", k, NY) for k in AWAY}
        return [own] + [got[k] for k in range(1, NY)]

    early = across(keep, send)
    later, send_later = call(
        functools.partial(last_matmul, width),
        [shape(size // 2, wide)] * 2,
        [idx, up, down, inv_gain2, w_gate, w_up, later, send_later],
        "svvvvvvv",
        scratch=[pltpu.VMEM((piece, feats), bf16)],
        flops=4 * piece * feats * width,
        moved=4 * feats * width,
        alias={6: 0, 7: 1},
    )
    late = across(later, send_later)
    hidden = call(functools.partial(activate, width), shape(block, width), early + late, "v" * 2 * NY, moved=10 * block * wide)
    same = {0: hidden, **{k: shift(hidden, "y", k, NY) for k in AWAY}}
    other = {k: shift(v, "core", 1, NC) for k, v in same.items()}
    same, other = ([v[k] for k in range(NY)] for v in (same, other))

    def expand(first, last):
        got = call(
            functools.partial(second_matmul, first, last),
            [shape(piece // 2, feats)] * (2 * (last - first)),
            [idx] + same + other + [w_down],
            "s" + "v" * (2 * NY + 1),
            scratch=[pltpu.VMEM((total - first // NY * NY * piece, width), bf16)],
            flops=2 * (last - first) * piece * feats * width,
            moved=2 * feats * width,
        )
        return {j: got[2 * i : 2 * i + 2] for i, j in enumerate(ORDER[first:last])}

    terms = {**expand(FAR, NZ), **expand(0, FAR)}

    def chain(half, way, steps):
        got = terms[way * steps if steps < NZ // 2 else steps][half]
        for step in range(steps, 1, -1):
            got = shift(got, "z", way, NZ)
            own = terms[way * (step - 1)][half]
            after = [terms[0][0]] if step == steps else []
            got = call(add, shape(piece // 2, feats), [got, own] + after, "vvh"[: 2 + len(after)], moved=3 * piece * feats)
        return shift(got, "z", way, NZ)

    far = NZ // 2
    low = [chain(0, -1, far), chain(0, 1, far - 1)]
    high = [chain(1, 1, far), chain(1, -1, far - 1)]
    mine, one = call(
        z_sum, [shape(rows, feats, kind=f32), shape(rows, feats)], [terms[0][0]] + low, "vvv", moved=4 * piece * feats
    )
    two, three = call(z_sum, [shape(rows, feats)] * 2, [terms[0][1]] + high, "vvv", moved=4 * piece * feats)
    sent = {1: one, 2: two, 3: three}
    parts = {k: shift(sent[k], "x", -k, NX) for k in AWAY}
    return call(finish, shape(rows, feats), [stream, mine] + [parts[k] for k in range(1, NX)], "v" * 5, moved=20 * rows * feats)


def solution(mesh):
    fine = Mesh(mesh.devices.reshape(NX, NZ, NY, NC), ("x", "z", "y", "core"))
    pool = ("x", "z")
    placed = (
        P(pool, TP),
        P(pool, TP),
        P(pool, None, TP),
        P(pool, None, TP),
        P(pool, TP),
        P(pool, TP),
        P(pool),
        P(TP),
        P(TP, pool),
        P(TP, pool),
        P(pool, TP),
    )
    return jax.shard_map(shards, mesh=fine, in_specs=placed, out_specs=P(pool, TP), check_vma=False)
```

```python
import functools

import jax
import jax.numpy as jnp
from jax import lax
from jax.experimental import pallas as pl
from jax.experimental.pallas import tpu as pltpu
from jax.sharding import Mesh
from jax.sharding import PartitionSpec as P

D = 16384
HEAD_DIM = 128
NX, NZ, NY, NC = 4, 8, 4, 2
TP = ("y", "core")
MARKS = 128
MIB = 1 << 20
ORDER = (0, -1, 1, -2, 2, -3, 3, 4)
EARLY = 4
AWAY = (2, 1, 3)


def shift(v, axis, by, n):
    return lax.ppermute(v, axis, [(i, (i + by) % n) for i in range(n)])


def rows_at(start, count):
    return pl.ds(pl.multiple_of(start, count), count)


def call(kernel, outs, args, kinds, scratch=(), flops=0, moved=0, limit=16 * MIB, alias=None):
    spaces = {"s": pltpu.SMEM, "v": pltpu.VMEM, "h": pltpu.HBM}
    single = not isinstance(outs, (list, tuple))
    whole = [outs] if single else list(outs)
    got = pl.pallas_call(
        kernel,
        out_shape=whole,
        in_specs=[pl.BlockSpec(memory_space=spaces[k]) for k in kinds],
        out_specs=[pl.BlockSpec(memory_space=pltpu.VMEM)] * len(whole),
        scratch_shapes=list(scratch),
        input_output_aliases=alias or {},
        compiler_params=pltpu.CompilerParams(vmem_limit_bytes=limit),
        cost_estimate=pl.CostEstimate(flops=flops, bytes_accessed=moved, transcendentals=0),
    )(*args)
    return got[0] if single else got


def shape(*dims, kind=jnp.bfloat16):
    return jax.ShapeDtypeStruct(dims, kind)


def copy_in(pairs, sems):
    copies = [pltpu.make_async_copy(src, dst, sems.at[i]) for i, (src, dst) in enumerate(pairs)]
    for copy in copies:
        copy.start()
    for copy in copies:
        copy.wait()


def copy_in(pairs, sems):
    copies = [pltpu.make_async_copy(src, dst, sems.at[i]) for i, (src, dst) in enumerate(pairs)]
    for copy in copies:
        copy.start()
    for copy in copies:
        copy.wait()


def start_rows(scale, lengths_in, hidden_in, queries_in, keys_in, values_in, own_keys_in, own_values_in, gain_in, *rest):
    stream, inv_gain2, out, lengths, hidden, queries, keys, values, own_keys, own_values, gain, heads, work, low, sems = rest
    copy_in(
        [
            (queries_in, queries),
            (lengths_in, lengths),
            (keys_in, keys),
            (values_in, values),
            (own_keys_in, own_keys),
            (own_values_in, own_values),
            (hidden_in, hidden),
            (gain_in, gain),
        ],
        sems,
    )
    rows, feats = hidden.shape
    per = feats // HEAD_DIM
    ctx = keys.shape[1]
    f32, bf16 = jnp.float32, jnp.bfloat16
    wide = queries[...].astype(f32)
    for h in range(per):
        heads[pl.ds(h, rows, stride=per), :] = wide[:, h * HEAD_DIM : (h + 1) * HEAD_DIM]
    slot = lax.broadcasted_iota(jnp.int32, (per, ctx), 1)

    def spread(ref):
        each = ref[...].astype(f32)
        return jnp.concatenate(
            [jnp.broadcast_to(each[r : r + 1, :], (per, HEAD_DIM)) for r in range(rows)], axis=0
        )

    for r in range(rows):
        score = lax.dot_general(
            heads[pl.ds(r * per, per), :].astype(bf16),
            keys[r],
            (((1,), (1,)), ((), ())),
            preferred_element_type=f32,
        )
        work[pl.ds(r * per, per), :] = jnp.where(slot < lengths[r], score * scale, -1e30)
    own = jnp.sum(heads[...] * spread(own_keys), axis=1, keepdims=True) * scale
    score = work[...]
    top = jnp.maximum(jnp.max(score, axis=1, keepdims=True), own)
    weight = jnp.exp(score - top)
    own_weight = jnp.exp(own - top)
    total = jnp.sum(weight, axis=1, keepdims=True) + own_weight
    low[...] = weight.astype(bf16)
    for r in range(rows):
        work[pl.ds(r * per, per), :] = jnp.dot(low[pl.ds(r * per, per), :], values[r], preferred_element_type=f32)
    work[...] = (work[...] + own_weight.astype(bf16).astype(f32) * spread(own_values)) / total
    scales = gain[...].astype(f32)
    inv_gain2[...] = 1.0 / (scales * scales)
    for h in range(per):
        cols = slice(h * HEAD_DIM, (h + 1) * HEAD_DIM)
        got = hidden[:, cols].astype(f32) + work[pl.ds(h, rows, stride=per), :]
        stream[:, cols] = got
        out[:, cols] = (got * scales[h : h + 1, :]).astype(bf16)


def seat(own, inv_gain2, out, kept):
    out[pl.ds(0, own.shape[0]), :] = own[...]
    kept[...] = inv_gain2[...]


def join(first, *refs):
    parts, out = refs[:-1], refs[-1]
    size = parts[0].shape[0]
    for k, part in enumerate(parts, 1):
        out[pl.ds(k * size, size), :] = part[...]


def place(core, pieces, part):
    top = part.shape[0] // 2
    for i, piece in enumerate(pieces):
        half = piece.shape[0] // 2
        at = i * half
        part[pl.ds(at, half), :] = piece[rows_at(core * half, half), :]
        part[pl.ds(top + at, half), :] = piece[rows_at((1 - core) * half, half), :]


def squares(width, part, inv_gain2, keep, send, row):
    top = part.shape[0] // 2
    step = 32
    lane = lax.broadcasted_iota(jnp.int32, (step, MARKS), 1)
    for i in range(2 * top // step):
        sums = 0.0
        for h in range(part.shape[1] // HEAD_DIM):
            wide = part[pl.ds(i * step, step), pl.ds(h * HEAD_DIM, HEAD_DIM)].astype(jnp.float32)
            sums = sums + wide * wide * inv_gain2[pl.ds(h, 1), :]
        sums = jnp.sum(sums, axis=1, keepdims=True)
        high = sums.astype(jnp.bfloat16).astype(jnp.float32)
        marks = jnp.where(lane == 0, high, jnp.where(lane == 1, sums - high, 0.0))
        out = keep if i * step < top else send
        out[pl.ds(row + i * step % top, step), pl.ds(2 * width, MARKS)] = marks.astype(jnp.bfloat16)


def project(weights, base, part, keep, send, row):
    top, width = part.shape[0] // 2, weights.shape[1]
    to = pl.ds(row, top)

    def tile(start, size):
        terms = jnp.dot(part[...], weights[:, pl.ds(start, size)], preferred_element_type=jnp.float32)
        keep[to, pl.ds(base + start, size)] = terms[:top].astype(jnp.bfloat16)
        send[to, pl.ds(base + start, size)] = terms[top:].astype(jnp.bfloat16)

    pl.loop(0, width // 256)(lambda t: tile(pl.multiple_of(t * 256, 256), 256))
    if width % 256:
        tile(width // 256 * 256, width % 256)


def gate_matmul(width, idx, *refs):
    pieces, (_, inv_gain2, w_gate, keep, send, part, done) = refs[:-7], refs[-7:]
    place(idx[3], pieces, part)
    squares(width, part, inv_gain2, keep, send, 0)
    project(w_gate, 0, part, keep, send, 0)
    done[...] = jnp.zeros_like(done)


def up_matmul(width, _, part, w_up, keep_in, send_in, keep, send):
    project(w_up, width, part, keep, send, 0)


def middle_matmul(width, idx, *refs):
    pieces, (_, inv_gain2, w_gate, w_up, keep, send, _, part) = refs[:-8], refs[-8:]
    place(idx[3], pieces, part)
    squares(width, part, inv_gain2, keep, send, 0)
    project(w_gate, 0, part, keep, send, 0)
    project(w_up, width, part, keep, send, 0)


def last_matmul(width, idx, low, high, inv_gain2, w_gate, w_up, keep_in, send_in, keep, send, part):
    core = idx[3]
    half = low.shape[0]
    part[rows_at(core * half, half), :] = low[...]
    part[rows_at((1 - core) * half, half), :] = high[...]
    row = keep.shape[0] - half
    squares(width, part, inv_gain2, keep, send, row)
    project(w_gate, 0, part, keep, send, row)
    project(w_up, width, part, keep, send, row)


def halves(up, down, _, up_half, down_half):
    size = up_half.shape[0]
    up_half[...] = up[pl.ds(0, size), :]
    down_half[...] = down[pl.ds(size, size), :]


def core_sum(block, idx, keep, came, own, *outs):
    mine = idx[2]

    def summed(y):
        at = rows_at(y * block, block)
        return keep[at, :].astype(jnp.float32) + came[at, :].astype(jnp.float32)

    own[...] = summed(mine)
    for k, out in enumerate(outs, 1):
        out[...] = summed(lax.rem(mine + k, NY)).astype(jnp.bfloat16)


def activate(width, *refs):
    parts, hidden = refs[:-1], refs[-1]
    block = parts[0].shape[0]
    for i in range(2):
        own, one, two, three = parts[i * NY : (i + 1) * NY]
        sums = own[...] + one[...].astype(jnp.float32) + two[...].astype(jnp.float32) + three[...].astype(jnp.float32)
        meansq = jnp.sum(sums[:, 2 * width :], axis=1, keepdims=True) / D
        inv = lax.rsqrt(meansq + 1e-05)
        gate = sums[:, :width] * inv
        up = sums[:, width : 2 * width] * inv
        hidden[pl.ds(i * block, block), :] = (gate / (1.0 + jnp.exp(-gate)) * up).astype(jnp.bfloat16)


def second_matmul(groups, ranges, idx, *refs):
    same, refs = refs[:NY], refs[NY:]
    other, refs = refs[:NY], refs[NY:]
    weights, outs, hidden = refs[0], refs[1:-1], refs[-1]
    mine, core = idx[2], idx[3]
    block = same[0].shape[0]
    half = block // 2
    for k in range(NY):
        y = lax.rem(mine - k + NY, NY)
        for g, i in enumerate(groups):
            at = (g * NY + y) * block
            hidden[rows_at(at + core * half, half), :] = same[k][pl.ds(i * half, half), :]
            hidden[rows_at(at + (1 - core) * half, half), :] = other[k][pl.ds(i * half, half), :]

    @pl.loop(0, weights.shape[1] // 256)
    def _(t):
        cols = pl.ds(pl.multiple_of(t * 256, 256), 256)
        some = jnp.concatenate([hidden[pl.ds(at, size), :] for at, size in ranges], axis=0)
        terms = jnp.dot(some, weights[:, cols], preferred_element_type=jnp.float32).astype(jnp.bfloat16)
        for i, out in enumerate(outs):
            out[:, cols] = terms[i * half : (i + 1) * half]


def add(came, own, out):
    out[...] = (came[...].astype(jnp.float32) + own[...].astype(jnp.float32)).astype(jnp.bfloat16)


def z_sum(own, one, two, *outs):
    rows = outs[0].shape[0]
    for k, out in enumerate(outs):
        at = pl.ds(k * rows, rows)
        total = own[at, :].astype(jnp.float32) + one[at, :].astype(jnp.float32) + two[at, :].astype(jnp.float32)
        out[...] = total.astype(out.dtype)


def finish(stream, mine, one, two, three, out):
    total = stream[...] + mine[...]
    for ref in (one, two, three):
        total = total + ref[...].astype(jnp.float32)
    out[...] = total.astype(jnp.bfloat16)


def shards(
    hidden_rows,
    queries,
    cache_keys,
    cache_values,
    new_keys,
    new_values,
    lengths,
    norm_gain,
    w_gate,
    w_up,
    w_down,
):
    f32, bf16 = jnp.float32, jnp.bfloat16
    rows, feats = hidden_rows.shape
    width = w_gate.shape[1]
    piece = rows * NX
    total = piece * NZ
    block = total // (NY * NC)
    wide = 2 * width + MARKS
    per = feats // HEAD_DIM
    idx = jnp.stack([lax.axis_index(a) for a in ("x", "z", "y", "core")]).astype(jnp.int32)
    given = [lengths, hidden_rows, queries, cache_keys, cache_values, new_keys, new_values, norm_gain.reshape(per, HEAD_DIM)]
    stream, inv_gain2, scaled = call(
        functools.partial(start_rows, HEAD_DIM ** (-0.5)),
        [shape(rows, feats, kind=f32), shape(per, HEAD_DIM, kind=f32), shape(rows, feats)],
        given,
        "h" * 8,
        scratch=[pltpu.SMEM(lengths.shape, jnp.int32)]
        + [pltpu.VMEM(v.shape, v.dtype) for v in given[1:]]
        + [pltpu.VMEM((rows * per, HEAD_DIM), f32)] * 2
        + [pltpu.VMEM((rows * per, HEAD_DIM), bf16)]
        + [pltpu.SemaphoreType.DMA((8,))],
        moved=4 * cache_keys.size,
        limit=60 * MIB,
    )

    own, inv_gain2 = call(
        seat, [shape(piece, feats), shape(per, HEAD_DIM, kind=f32)], [scaled, inv_gain2], "vv", moved=2 * rows * feats
    )
    from_x = {k: shift(scaled, "x", k, NX) for k in AWAY}
    own = call(
        join,
        shape(piece, feats),
        [own] + [from_x[k] for k in range(1, NX)],
        "v" * NX,
        moved=4 * piece * feats,
        alias={0: 0},
    )
    pieces = {0: own}
    up = down = own
    for step in range(1, NZ // 2):
        up = shift(up, "z", 1, NZ)
        down = shift(down, "z", -1, NZ)
        pieces[-step], pieces[step] = up, down

    def gates(some, after):
        size = sum(v.shape[0] for v in some)
        return call(
            functools.partial(gate_matmul, width),
            [shape(size // 2, wide)] * 2 + [shape(size, feats), shape(8, 128, kind=f32)],
            [idx] + some + [after, inv_gain2, w_gate],
            "s" + "v" * len(some) + "hvv",
            flops=2 * size * feats * width,
            moved=2 * feats * width,
        )

    def ups(keep, send, part, after):
        return call(
            functools.partial(up_matmul, width),
            [shape(*keep.shape)] * 2,
            [after, part, w_up, keep, send],
            "hvvvv",
            flops=2 * part.size * width,
            moved=2 * feats * width,
            alias={3: 0, 4: 1},
        )

    keep, send, part, done = gates([pieces[j] for j in ORDER[:EARLY]], pieces[2])
    up, down = call(halves, [shape(piece // 2, feats)] * 2, [up, down, done], "vvh", moved=4 * piece * feats)
    late = [pieces[j] for j in ORDER[EARLY:-1]]
    size = (NZ - EARLY) * piece
    keep, send = ups(keep, send, part, up)
    later, send_later, send = call(
        functools.partial(middle_matmul, width),
        [shape(size // 2, wide)] * 2 + [shape(*send.shape)],
        [idx] + late + [send, inv_gain2, w_gate, w_up],
        "s" + "v" * (len(late) + 4),
        scratch=[pltpu.VMEM((size - piece, feats), bf16)],
        flops=4 * (size - piece) * feats * width,
        moved=4 * feats * width,
        alias={1 + len(late): 2},
    )
    up = shift(up, "z", 1, NZ)
    down = shift(down, "z", -1, NZ)

    def across(keep, send):
        came = shift(send, "core", 1, NC)
        own, *parts = call(
            functools.partial(core_sum, block // 2),
            [shape(block // 2, wide, kind=f32)] + [shape(block // 2, wide)] * (NY - 1),
            [idx, keep, came],
            "svv",
            moved=2 * total * wide,
        )
        got = {k: shift(parts[k - 1], "y", k, NY) for k in AWAY}
        return [own] + [got[k] for k in range(1, NY)]

    early = across(keep, send)
    later, send_later = call(
        functools.partial(last_matmul, width),
        [shape(size // 2, wide)] * 2,
        [idx, up, down, inv_gain2, w_gate, w_up, later, send_later],
        "svvvvvvv",
        scratch=[pltpu.VMEM((piece, feats), bf16)],
        flops=4 * piece * feats * width,
        moved=4 * feats * width,
        alias={6: 0, 7: 1},
    )
    late = across(later, send_later)
    hidden = call(functools.partial(activate, width), shape(block, width), early + late, "v" * 2 * NY, moved=10 * block * wide)
    same = {0: hidden, **{k: shift(hidden, "y", k, NY) for k in AWAY}}
    other = {k: shift(v, "core", 1, NC) for k, v in same.items()}
    same, other = ([v[k] for k in range(NY)] for v in (same, other))

    half = piece // 2

    def expand(groups, halves_of):
        starts = [(ORDER.index(j) - (groups[0] * NY)) * piece + h * half for j, h in halves_of]
        ranges = []
        for at in starts:
            if ranges and sum(ranges[-1]) == at:
                ranges[-1] = (ranges[-1][0], ranges[-1][1] + half)
            else:
                ranges.append((at, half))
        size = half * len(starts)
        got = call(
            functools.partial(second_matmul, groups, ranges),
            [shape(half, feats)] * len(starts),
            [idx] + same + other + [w_down],
            "s" + "v" * (2 * NY + 1),
            scratch=[pltpu.VMEM((len(groups) * NY * piece, width), bf16)],
            flops=2 * size * feats * width,
            moved=2 * feats * width,
        )
        return dict(zip(halves_of, got))

    terms = {
        **expand((1,), [(-3, 1), (3, 0), (4, 0), (4, 1)]),
        **expand((0, 1), [(-2, 0), (-2, 1), (2, 0), (2, 1), (-3, 0), (3, 1)]),
        **expand((0,), [(0, 0), (0, 1), (-1, 0), (-1, 1), (1, 0), (1, 1)]),
    }

    def chain(half, way, steps):
        got = terms[way * steps if steps < NZ // 2 else steps, half]
        for step in range(steps, 1, -1):
            got = shift(got, "z", way, NZ)
            own = terms[way * (step - 1), half]
            got = call(add, shape(piece // 2, feats), [got, own], "vv", moved=3 * piece * feats)
        return shift(got, "z", way, NZ)

    far = NZ // 2
    low = [chain(0, -1, far), chain(0, 1, far - 1)]
    high = [chain(1, 1, far), chain(1, -1, far - 1)]
    mine, one = call(
        z_sum, [shape(rows, feats, kind=f32), shape(rows, feats)], [terms[0, 0]] + low, "vvv", moved=4 * piece * feats
    )
    two, three = call(z_sum, [shape(rows, feats)] * 2, [terms[0, 1]] + high, "vvv", moved=4 * piece * feats)
    sent = {1: one, 2: two, 3: three}
    parts = {k: shift(sent[k], "x", -k, NX) for k in AWAY}
    return call(finish, shape(rows, feats), [stream, mine] + [parts[k] for k in range(1, NX)], "v" * 5, moved=20 * rows * feats)


def solution(mesh):
    fine = Mesh(mesh.devices.reshape(NX, NZ, NY, NC), ("x", "z", "y", "core"))
    pool = ("x", "z")
    placed = (
        P(pool, TP),
        P(pool, TP),
        P(pool, None, TP),
        P(pool, None, TP),
        P(pool, TP),
        P(pool, TP),
        P(pool),
        P(TP),
        P(TP, pool),
        P(TP, pool),
        P(pool, TP),
    )
    return jax.shard_map(shards, mesh=fine, in_specs=placed, out_specs=P(pool, TP), check_vma=False)
```

```python
import functools

import jax
import jax.numpy as jnp
from jax import lax
from jax.experimental import pallas as pl
from jax.experimental.pallas import tpu as pltpu
from jax.sharding import Mesh
from jax.sharding import PartitionSpec as P

D = 16384
HEAD_DIM = 128
NX, NZ, NY, NC = 4, 8, 4, 2
TP = ("y", "core")
MARKS = 128
MIB = 1 << 20
ORDER = (0, -1, 1, -2, 2, -3, 3, 4)
EARLY = 4
AWAY = (2, 1, 3)


def shift(v, axis, by, n):
    return lax.ppermute(v, axis, [(i, (i + by) % n) for i in range(n)])


def rows_at(start, count):
    return pl.ds(pl.multiple_of(start, count), count)


def call(kernel, outs, args, kinds, scratch=(), flops=0, moved=0, limit=16 * MIB, alias=None):
    spaces = {"s": pltpu.SMEM, "v": pltpu.VMEM, "h": pltpu.HBM}
    single = not isinstance(outs, (list, tuple))
    whole = [outs] if single else list(outs)
    got = pl.pallas_call(
        kernel,
        out_shape=whole,
        in_specs=[pl.BlockSpec(memory_space=spaces[k]) for k in kinds],
        out_specs=[pl.BlockSpec(memory_space=pltpu.VMEM)] * len(whole),
        scratch_shapes=list(scratch),
        input_output_aliases=alias or {},
        compiler_params=pltpu.CompilerParams(vmem_limit_bytes=limit),
        cost_estimate=pl.CostEstimate(flops=flops, bytes_accessed=moved, transcendentals=0),
    )(*args)
    return got[0] if single else got


def shape(*dims, kind=jnp.bfloat16):
    return jax.ShapeDtypeStruct(dims, kind)


def copy_in(pairs, sems):
    copies = [pltpu.make_async_copy(src, dst, sems.at[i]) for i, (src, dst) in enumerate(pairs)]
    for copy in copies:
        copy.start()
    for copy in copies:
        copy.wait()


def copy_in(pairs, sems):
    copies = [pltpu.make_async_copy(src, dst, sems.at[i]) for i, (src, dst) in enumerate(pairs)]
    for copy in copies:
        copy.start()
    for copy in copies:
        copy.wait()


def start_rows(scale, lengths_in, hidden_in, queries_in, keys_in, values_in, own_keys_in, own_values_in, gain_in, *rest):
    stream, inv_gain2, out, lengths, hidden, queries, keys, values, own_keys, own_values, gain, heads, work, low, sems = rest
    copy_in(
        [
            (queries_in, queries),
            (lengths_in, lengths),
            (keys_in, keys),
            (values_in, values),
            (own_keys_in, own_keys),
            (own_values_in, own_values),
            (hidden_in, hidden),
            (gain_in, gain),
        ],
        sems,
    )
    rows, feats = hidden.shape
    per = feats // HEAD_DIM
    ctx = keys.shape[1]
    f32, bf16 = jnp.float32, jnp.bfloat16
    wide = queries[...].astype(f32)
    for h in range(per):
        heads[pl.ds(h, rows, stride=per), :] = wide[:, h * HEAD_DIM : (h + 1) * HEAD_DIM]
    slot = lax.broadcasted_iota(jnp.int32, (per, ctx), 1)

    def spread(ref):
        each = ref[...].astype(f32)
        return jnp.concatenate(
            [jnp.broadcast_to(each[r : r + 1, :], (per, HEAD_DIM)) for r in range(rows)], axis=0
        )

    for r in range(rows):
        score = lax.dot_general(
            heads[pl.ds(r * per, per), :].astype(bf16),
            keys[r],
            (((1,), (1,)), ((), ())),
            preferred_element_type=f32,
        )
        work[pl.ds(r * per, per), :] = jnp.where(slot < lengths[r], score * scale, -1e30)
    own = jnp.sum(heads[...] * spread(own_keys), axis=1, keepdims=True) * scale
    score = work[...]
    top = jnp.maximum(jnp.max(score, axis=1, keepdims=True), own)
    weight = jnp.exp(score - top)
    own_weight = jnp.exp(own - top)
    total = jnp.sum(weight, axis=1, keepdims=True) + own_weight
    low[...] = weight.astype(bf16)
    for r in range(rows):
        work[pl.ds(r * per, per), :] = jnp.dot(low[pl.ds(r * per, per), :], values[r], preferred_element_type=f32)
    work[...] = (work[...] + own_weight.astype(bf16).astype(f32) * spread(own_values)) / total
    scales = gain[...].astype(f32)
    inv_gain2[...] = 1.0 / (scales * scales)
    for h in range(per):
        cols = slice(h * HEAD_DIM, (h + 1) * HEAD_DIM)
        got = hidden[:, cols].astype(f32) + work[pl.ds(h, rows, stride=per), :]
        stream[:, cols] = got
        out[:, cols] = (got * scales[h : h + 1, :]).astype(bf16)


def seat(own, inv_gain2, out, kept):
    out[pl.ds(0, own.shape[0]), :] = own[...]
    kept[...] = inv_gain2[...]


def join(first, *refs):
    parts, out = refs[:-1], refs[-1]
    size = parts[0].shape[0]
    for k, part in enumerate(parts, 1):
        out[pl.ds(k * size, size), :] = part[...]


def place(core, pieces, part):
    top = part.shape[0] // 2
    for i, piece in enumerate(pieces):
        half = piece.shape[0] // 2
        at = i * half
        part[pl.ds(at, half), :] = piece[rows_at(core * half, half), :]
        part[pl.ds(top + at, half), :] = piece[rows_at((1 - core) * half, half), :]


def squares(width, part, inv_gain2, keep, send, row):
    top = part.shape[0] // 2
    step = 32
    lane = lax.broadcasted_iota(jnp.int32, (step, MARKS), 1)
    for i in range(2 * top // step):
        sums = 0.0
        for h in range(part.shape[1] // HEAD_DIM):
            wide = part[pl.ds(i * step, step), pl.ds(h * HEAD_DIM, HEAD_DIM)].astype(jnp.float32)
            sums = sums + wide * wide * inv_gain2[pl.ds(h, 1), :]
        sums = jnp.sum(sums, axis=1, keepdims=True)
        high = sums.astype(jnp.bfloat16).astype(jnp.float32)
        marks = jnp.where(lane == 0, high, jnp.where(lane == 1, sums - high, 0.0))
        out = keep if i * step < top else send
        out[pl.ds(row + i * step % top, step), pl.ds(2 * width, MARKS)] = marks.astype(jnp.bfloat16)


def project(weights, base, part, keep, send, row):
    top, width = part.shape[0] // 2, weights.shape[1]
    to = pl.ds(row, top)

    def tile(start, size):
        terms = jnp.dot(part[...], weights[:, pl.ds(start, size)], preferred_element_type=jnp.float32)
        keep[to, pl.ds(base + start, size)] = terms[:top].astype(jnp.bfloat16)
        send[to, pl.ds(base + start, size)] = terms[top:].astype(jnp.bfloat16)

    pl.loop(0, width // 256)(lambda t: tile(pl.multiple_of(t * 256, 256), 256))
    if width % 256:
        tile(width // 256 * 256, width % 256)


def gate_matmul(width, idx, *refs):
    pieces, (_, inv_gain2, w_gate, keep, send, part, done) = refs[:-7], refs[-7:]
    place(idx[3], pieces, part)
    squares(width, part, inv_gain2, keep, send, 0)
    project(w_gate, 0, part, keep, send, 0)
    done[...] = jnp.zeros_like(done)


def up_matmul(width, _, part, w_up, keep_in, send_in, keep, send):
    project(w_up, width, part, keep, send, 0)


def middle_matmul(width, idx, *refs):
    pieces, (_, inv_gain2, w_gate, w_up, keep, send, _, part) = refs[:-8], refs[-8:]
    place(idx[3], pieces, part)
    squares(width, part, inv_gain2, keep, send, 0)
    project(w_gate, 0, part, keep, send, 0)
    project(w_up, width, part, keep, send, 0)


def last_matmul(width, idx, low, high, inv_gain2, w_gate, w_up, keep_in, send_in, keep, send, part):
    core = idx[3]
    half = low.shape[0]
    part[rows_at(core * half, half), :] = low[...]
    part[rows_at((1 - core) * half, half), :] = high[...]
    row = keep.shape[0] - half
    squares(width, part, inv_gain2, keep, send, row)
    project(w_gate, 0, part, keep, send, row)
    project(w_up, width, part, keep, send, row)


def halves(up, down, _, up_half, down_half):
    size = up_half.shape[0]
    up_half[...] = up[pl.ds(0, size), :]
    down_half[...] = down[pl.ds(size, size), :]


def core_sum(block, idx, keep, came, own, *outs):
    mine = idx[2]

    def summed(y):
        at = rows_at(y * block, block)
        return keep[at, :].astype(jnp.float32) + came[at, :].astype(jnp.float32)

    own[...] = summed(mine)
    for k, out in enumerate(outs, 1):
        out[...] = summed(lax.rem(mine + k, NY)).astype(jnp.bfloat16)


def activate(width, *refs):
    parts, hidden = refs[:-1], refs[-1]
    block = parts[0].shape[0]
    for i in range(2):
        own, one, two, three = parts[i * NY : (i + 1) * NY]
        sums = own[...] + one[...].astype(jnp.float32) + two[...].astype(jnp.float32) + three[...].astype(jnp.float32)
        meansq = jnp.sum(sums[:, 2 * width :], axis=1, keepdims=True) / D
        inv = lax.rsqrt(meansq + 1e-05)
        gate = sums[:, :width] * inv
        up = sums[:, width : 2 * width] * inv
        hidden[pl.ds(i * block, block), :] = (gate / (1.0 + jnp.exp(-gate)) * up).astype(jnp.bfloat16)


def second_matmul(idx, *refs):
    same, refs = refs[:NY], refs[NY:]
    other, refs = refs[:NY], refs[NY:]
    weights, outs, hidden = refs[0], refs[1:-1], refs[-1]
    mine, core = idx[2], idx[3]
    block = same[0].shape[0]
    half = block // 2
    for k in range(NY):
        y = lax.rem(mine - k + NY, NY)
        for i in range(2):
            at = (i * NY + y) * block
            hidden[rows_at(at + core * half, half), :] = same[k][pl.ds(i * half, half), :]
            hidden[rows_at(at + (1 - core) * half, half), :] = other[k][pl.ds(i * half, half), :]

    @pl.loop(0, weights.shape[1] // 256)
    def _(t):
        cols = pl.ds(pl.multiple_of(t * 256, 256), 256)
        terms = jnp.dot(hidden[...], weights[:, cols], preferred_element_type=jnp.float32).astype(jnp.bfloat16)
        for i, out in enumerate(outs):
            out[:, cols] = terms[i * half : (i + 1) * half]


def add(came, own, out):
    out[...] = (came[...].astype(jnp.float32) + own[...].astype(jnp.float32)).astype(jnp.bfloat16)


def z_sum(own, one, two, *outs):
    rows = outs[0].shape[0]
    for k, out in enumerate(outs):
        at = pl.ds(k * rows, rows)
        total = own[at, :].astype(jnp.float32) + one[at, :].astype(jnp.float32) + two[at, :].astype(jnp.float32)
        out[...] = total.astype(out.dtype)


def finish(stream, mine, one, two, three, out):
    total = stream[...] + mine[...]
    for ref in (one, two, three):
        total = total + ref[...].astype(jnp.float32)
    out[...] = total.astype(jnp.bfloat16)


def shards(
    hidden_rows,
    queries,
    cache_keys,
    cache_values,
    new_keys,
    new_values,
    lengths,
    norm_gain,
    w_gate,
    w_up,
    w_down,
):
    f32, bf16 = jnp.float32, jnp.bfloat16
    rows, feats = hidden_rows.shape
    width = w_gate.shape[1]
    piece = rows * NX
    total = piece * NZ
    block = total // (NY * NC)
    wide = 2 * width + MARKS
    per = feats // HEAD_DIM
    idx = jnp.stack([lax.axis_index(a) for a in ("x", "z", "y", "core")]).astype(jnp.int32)
    given = [lengths, hidden_rows, queries, cache_keys, cache_values, new_keys, new_values, norm_gain.reshape(per, HEAD_DIM)]
    stream, inv_gain2, scaled = call(
        functools.partial(start_rows, HEAD_DIM ** (-0.5)),
        [shape(rows, feats, kind=f32), shape(per, HEAD_DIM, kind=f32), shape(rows, feats)],
        given,
        "h" * 8,
        scratch=[pltpu.SMEM(lengths.shape, jnp.int32)]
        + [pltpu.VMEM(v.shape, v.dtype) for v in given[1:]]
        + [pltpu.VMEM((rows * per, HEAD_DIM), f32)] * 2
        + [pltpu.VMEM((rows * per, HEAD_DIM), bf16)]
        + [pltpu.SemaphoreType.DMA((8,))],
        moved=4 * cache_keys.size,
        limit=60 * MIB,
    )

    own, inv_gain2 = call(
        seat, [shape(piece, feats), shape(per, HEAD_DIM, kind=f32)], [scaled, inv_gain2], "vv", moved=2 * rows * feats
    )
    from_x = {k: shift(scaled, "x", k, NX) for k in AWAY}
    own = call(
        join,
        shape(piece, feats),
        [own] + [from_x[k] for k in range(1, NX)],
        "v" * NX,
        moved=4 * piece * feats,
        alias={0: 0},
    )
    pieces = {0: own}
    up = down = own
    for step in range(1, NZ // 2):
        up = shift(up, "z", 1, NZ)
        down = shift(down, "z", -1, NZ)
        pieces[-step], pieces[step] = up, down

    def gates(some, after):
        size = sum(v.shape[0] for v in some)
        return call(
            functools.partial(gate_matmul, width),
            [shape(size // 2, wide)] * 2 + [shape(size, feats), shape(8, 128, kind=f32)],
            [idx] + some + [after, inv_gain2, w_gate],
            "s" + "v" * len(some) + "hvv",
            flops=2 * size * feats * width,
            moved=2 * feats * width,
        )

    def ups(keep, send, part, after):
        return call(
            functools.partial(up_matmul, width),
            [shape(*keep.shape)] * 2,
            [after, part, w_up, keep, send],
            "hvvvv",
            flops=2 * part.size * width,
            moved=2 * feats * width,
            alias={3: 0, 4: 1},
        )

    keep, send, part, done = gates([pieces[j] for j in ORDER[:EARLY]], pieces[2])
    up, down = call(halves, [shape(piece // 2, feats)] * 2, [up, down, done], "vvh", moved=4 * piece * feats)
    late = [pieces[j] for j in ORDER[EARLY:-1]]
    size = (NZ - EARLY) * piece
    keep, send = ups(keep, send, part, up)
    later, send_later, send = call(
        functools.partial(middle_matmul, width),
        [shape(size // 2, wide)] * 2 + [shape(*send.shape)],
        [idx] + late + [send, inv_gain2, w_gate, w_up],
        "s" + "v" * (len(late) + 4),
        scratch=[pltpu.VMEM((size - piece, feats), bf16)],
        flops=4 * (size - piece) * feats * width,
        moved=4 * feats * width,
        alias={1 + len(late): 2},
    )
    up = shift(up, "z", 1, NZ)
    down = shift(down, "z", -1, NZ)

    def across(keep, send):
        came = shift(send, "core", 1, NC)
        own, *parts = call(
            functools.partial(core_sum, block // 2),
            [shape(block // 2, wide, kind=f32)] + [shape(block // 2, wide)] * (NY - 1),
            [idx, keep, came],
            "svv",
            moved=2 * total * wide,
        )
        got = {k: shift(parts[k - 1], "y", k, NY) for k in AWAY}
        return [own] + [got[k] for k in range(1, NY)]

    early = across(keep, send)
    later, send_later = call(
        functools.partial(last_matmul, width),
        [shape(size // 2, wide)] * 2,
        [idx, up, down, inv_gain2, w_gate, w_up, later, send_later],
        "svvvvvvv",
        scratch=[pltpu.VMEM((piece, feats), bf16)],
        flops=4 * piece * feats * width,
        moved=4 * feats * width,
        alias={6: 0, 7: 1},
    )
    late = across(later, send_later)
    hidden = call(functools.partial(activate, width), shape(block, width), early + late, "v" * 2 * NY, moved=10 * block * wide)
    same = {0: hidden, **{k: shift(hidden, "y", k, NY) for k in AWAY}}
    other = {k: shift(v, "core", 1, NC) for k, v in same.items()}
    same, other = ([v[k] for k in range(NY)] for v in (same, other))

    half = piece // 2

    keys = [(j, h) for j in ORDER for h in range(2)]
    got = call(
        second_matmul,
        [shape(half, feats)] * len(keys),
        [idx] + same + other + [w_down],
        "s" + "v" * (2 * NY + 1),
        scratch=[pltpu.VMEM((total, width), bf16)],
        flops=2 * total * feats * width,
        moved=2 * feats * width,
        limit=20 * MIB,
    )
    terms = dict(zip(keys, got))

    def chain(half, way, steps):
        got = terms[way * steps if steps < NZ // 2 else steps, half]
        for step in range(steps, 1, -1):
            got = shift(got, "z", way, NZ)
            own = terms[way * (step - 1), half]
            got = call(add, shape(piece // 2, feats), [got, own], "vv", moved=3 * piece * feats)
        return shift(got, "z", way, NZ)

    far = NZ // 2
    low = [chain(0, -1, far), chain(0, 1, far - 1)]
    high = [chain(1, 1, far), chain(1, -1, far - 1)]
    mine, one = call(
        z_sum, [shape(rows, feats, kind=f32), shape(rows, feats)], [terms[0, 0]] + low, "vvv", moved=4 * piece * feats
    )
    two, three = call(z_sum, [shape(rows, feats)] * 2, [terms[0, 1]] + high, "vvv", moved=4 * piece * feats)
    sent = {1: one, 2: two, 3: three}
    parts = {k: shift(sent[k], "x", -k, NX) for k in AWAY}
    return call(finish, shape(rows, feats), [stream, mine] + [parts[k] for k in range(1, NX)], "v" * 5, moved=20 * rows * feats)


def solution(mesh):
    fine = Mesh(mesh.devices.reshape(NX, NZ, NY, NC), ("x", "z", "y", "core"))
    pool = ("x", "z")
    placed = (
        P(pool, TP),
        P(pool, TP),
        P(pool, None, TP),
        P(pool, None, TP),
        P(pool, TP),
        P(pool, TP),
        P(pool),
        P(TP),
        P(TP, pool),
        P(TP, pool),
        P(pool, TP),
    )
    return jax.shard_map(shards, mesh=fine, in_specs=placed, out_specs=P(pool, TP), check_vma=False)
```

```python
import functools

import jax
import jax.numpy as jnp
from jax import lax
from jax.experimental import pallas as pl
from jax.experimental.pallas import tpu as pltpu
from jax.sharding import Mesh
from jax.sharding import PartitionSpec as P

D = 16384
HEAD_DIM = 128
NX, NZ, NY, NC = 4, 8, 4, 2
TP = ("y", "core")
MARKS = 128
MIB = 1 << 20
ORDER = (0, -1, 1, -2, 2, -3, 3, 4)
EARLY = 4
FAR = 5
AWAY = (2, 1, 3)
SLOTS = (0, 2, 1, 3)


def shift(v, axis, by, n):
    return lax.ppermute(v, axis, [(i, (i + by) % n) for i in range(n)])


def rows_at(start, count):
    return pl.ds(pl.multiple_of(start, count), count)


def call(kernel, outs, args, kinds, scratch=(), flops=0, moved=0, limit=16 * MIB, alias=None):
    spaces = {"s": pltpu.SMEM, "v": pltpu.VMEM, "h": pltpu.HBM}
    single = not isinstance(outs, (list, tuple))
    whole = [outs] if single else list(outs)
    got = pl.pallas_call(
        kernel,
        out_shape=whole,
        in_specs=[pl.BlockSpec(memory_space=spaces[k]) for k in kinds],
        out_specs=[pl.BlockSpec(memory_space=pltpu.VMEM)] * len(whole),
        scratch_shapes=list(scratch),
        input_output_aliases=alias or {},
        compiler_params=pltpu.CompilerParams(vmem_limit_bytes=limit),
        cost_estimate=pl.CostEstimate(flops=flops, bytes_accessed=moved, transcendentals=0),
    )(*args)
    return got[0] if single else got


def shape(*dims, kind=jnp.bfloat16):
    return jax.ShapeDtypeStruct(dims, kind)


def copy_in(pairs, sems):
    copies = [pltpu.make_async_copy(src, dst, sems.at[i]) for i, (src, dst) in enumerate(pairs)]
    for copy in copies:
        copy.start()
    for copy in copies:
        copy.wait()


def copy_in(pairs, sems):
    copies = [pltpu.make_async_copy(src, dst, sems.at[i]) for i, (src, dst) in enumerate(pairs)]
    for copy in copies:
        copy.start()
    for copy in copies:
        copy.wait()


def start_rows(scale, lengths_in, hidden_in, queries_in, keys_in, values_in, own_keys_in, own_values_in, gain_in, *rest):
    stream, inv_gain2, out, lengths, hidden, queries, keys, values, own_keys, own_values, gain, heads, work, low, sems = rest
    copy_in(
        [
            (queries_in, queries),
            (lengths_in, lengths),
            (keys_in, keys),
            (values_in, values),
            (own_keys_in, own_keys),
            (own_values_in, own_values),
            (hidden_in, hidden),
            (gain_in, gain),
        ],
        sems,
    )
    rows, feats = hidden.shape
    per = feats // HEAD_DIM
    ctx = keys.shape[1]
    f32, bf16 = jnp.float32, jnp.bfloat16
    wide = queries[...].astype(f32)
    for h in range(per):
        heads[pl.ds(h, rows, stride=per), :] = wide[:, h * HEAD_DIM : (h + 1) * HEAD_DIM]
    slot = lax.broadcasted_iota(jnp.int32, (per, ctx), 1)

    def spread(ref):
        each = ref[...].astype(f32)
        return jnp.concatenate(
            [jnp.broadcast_to(each[r : r + 1, :], (per, HEAD_DIM)) for r in range(rows)], axis=0
        )

    for r in range(rows):
        score = lax.dot_general(
            heads[pl.ds(r * per, per), :].astype(bf16),
            keys[r],
            (((1,), (1,)), ((), ())),
            preferred_element_type=f32,
        )
        work[pl.ds(r * per, per), :] = jnp.where(slot < lengths[r], score * scale, -1e30)
    own = jnp.sum(heads[...] * spread(own_keys), axis=1, keepdims=True) * scale
    score = work[...]
    top = jnp.maximum(jnp.max(score, axis=1, keepdims=True), own)
    weight = jnp.exp(score - top)
    own_weight = jnp.exp(own - top)
    total = jnp.sum(weight, axis=1, keepdims=True) + own_weight
    low[...] = weight.astype(bf16)
    for r in range(rows):
        work[pl.ds(r * per, per), :] = jnp.dot(low[pl.ds(r * per, per), :], values[r], preferred_element_type=f32)
    work[...] = (work[...] + own_weight.astype(bf16).astype(f32) * spread(own_values)) / total
    scales = gain[...].astype(f32)
    inv_gain2[...] = 1.0 / (scales * scales)
    for h in range(per):
        cols = slice(h * HEAD_DIM, (h + 1) * HEAD_DIM)
        got = hidden[:, cols].astype(f32) + work[pl.ds(h, rows, stride=per), :]
        stream[:, cols] = got
        out[:, cols] = (got * scales[h : h + 1, :]).astype(bf16)


def seat(own, inv_gain2, out, kept):
    out[pl.ds(0, own.shape[0]), :] = own[...]
    kept[...] = inv_gain2[...]


def join(first, *refs):
    parts, out = refs[:-1], refs[-1]
    size = parts[0].shape[0]
    for k, part in enumerate(parts, 1):
        out[pl.ds(k * size, size), :] = part[...]


def place(core, pieces, part):
    top = part.shape[0] // 2
    for i, piece in enumerate(pieces):
        half = piece.shape[0] // 2
        at = i * half
        part[pl.ds(at, half), :] = piece[rows_at(core * half, half), :]
        part[pl.ds(top + at, half), :] = piece[rows_at((1 - core) * half, half), :]


def squares(width, part, inv_gain2, keep, send, row):
    top = part.shape[0] // 2
    step = 32
    lane = lax.broadcasted_iota(jnp.int32, (step, MARKS), 1)
    for i in range(2 * top // step):
        sums = 0.0
        for h in range(part.shape[1] // HEAD_DIM):
            wide = part[pl.ds(i * step, step), pl.ds(h * HEAD_DIM, HEAD_DIM)].astype(jnp.float32)
            sums = sums + wide * wide * inv_gain2[pl.ds(h, 1), :]
        sums = jnp.sum(sums, axis=1, keepdims=True)
        high = sums.astype(jnp.bfloat16).astype(jnp.float32)
        marks = jnp.where(lane == 0, high, jnp.where(lane == 1, sums - high, 0.0))
        out = keep if i * step < top else send
        out[pl.ds(row + i * step % top, step), pl.ds(2 * width, MARKS)] = marks.astype(jnp.bfloat16)


def project(weights, base, part, keep, send, row):
    top, width = part.shape[0] // 2, weights.shape[1]
    to = pl.ds(row, top)

    def tile(start, size):
        terms = jnp.dot(part[...], weights[:, pl.ds(start, size)], preferred_element_type=jnp.float32)
        keep[to, pl.ds(base + start, size)] = terms[:top].astype(jnp.bfloat16)
        send[to, pl.ds(base + start, size)] = terms[top:].astype(jnp.bfloat16)

    pl.loop(0, width // 256)(lambda t: tile(pl.multiple_of(t * 256, 256), 256))
    if width % 256:
        tile(width // 256 * 256, width % 256)


def gate_matmul(width, idx, *refs):
    pieces, (_, inv_gain2, w_gate, keep, send, part, done) = refs[:-7], refs[-7:]
    place(idx[3], pieces, part)
    squares(width, part, inv_gain2, keep, send, 0)
    project(w_gate, 0, part, keep, send, 0)
    done[...] = jnp.zeros_like(done)


def up_matmul(width, _, part, w_up, keep_in, send_in, keep, send):
    project(w_up, width, part, keep, send, 0)


def middle_matmul(width, idx, *refs):
    pieces, (_, inv_gain2, w_gate, w_up, keep, send, _, part) = refs[:-8], refs[-8:]
    place(idx[3], pieces, part)
    squares(width, part, inv_gain2, keep, send, 0)
    project(w_gate, 0, part, keep, send, 0)
    project(w_up, width, part, keep, send, 0)


def last_matmul(width, idx, low, high, inv_gain2, w_gate, w_up, keep_in, send_in, keep, send, part):
    core = idx[3]
    half = low.shape[0]
    part[rows_at(core * half, half), :] = low[...]
    part[rows_at((1 - core) * half, half), :] = high[...]
    row = keep.shape[0] - half
    squares(width, part, inv_gain2, keep, send, row)
    project(w_gate, 0, part, keep, send, row)
    project(w_up, width, part, keep, send, row)


def halves(up, down, _, up_half, down_half):
    size = up_half.shape[0]
    up_half[...] = up[pl.ds(0, size), :]
    down_half[...] = down[pl.ds(size, size), :]


def core_sum(block, idx, keep, came, own, *outs):
    mine = idx[2]

    def summed(y):
        at = rows_at(y * block, block)
        return keep[at, :].astype(jnp.float32) + came[at, :].astype(jnp.float32)

    own[...] = summed(mine)
    for k, out in enumerate(outs, 1):
        out[...] = summed(lax.rem(mine + k, NY)).astype(jnp.bfloat16)


def activate(width, *refs):
    parts, hidden = refs[:-1], refs[-1]
    block = parts[0].shape[0]
    for i in range(2):
        own, one, two, three = parts[i * NY : (i + 1) * NY]
        sums = own[...] + one[...].astype(jnp.float32) + two[...].astype(jnp.float32) + three[...].astype(jnp.float32)
        meansq = jnp.sum(sums[:, 2 * width :], axis=1, keepdims=True) / D
        inv = lax.rsqrt(meansq + 1e-05)
        gate = sums[:, :width] * inv
        up = sums[:, width : 2 * width] * inv
        hidden[pl.ds(i * block, block), :] = (gate / (1.0 + jnp.exp(-gate)) * up).astype(jnp.bfloat16)


def second_matmul(first, last, idx, *refs):
    same, refs = refs[:NY], refs[NY:]
    other, refs = refs[:NY], refs[NY:]
    weights, outs, hidden = refs[0], refs[1:-1], refs[-1]
    mine, core = idx[2], idx[3]
    block = same[0].shape[0]
    half = block // 2
    groups = range(first // NY, 2)
    for k in range(NY):
        y = lax.rem(mine - k + NY, NY)
        for i in groups:
            at = ((i - groups[0]) * NY + y) * block
            hidden[rows_at(at + core * half, half), :] = same[k][pl.ds(i * half, half), :]
            hidden[rows_at(at + (1 - core) * half, half), :] = other[k][pl.ds(i * half, half), :]
    some = pl.ds((first - groups[0] * NY) * block, (last - first) * block)

    @pl.loop(0, weights.shape[1] // 256)
    def _(t):
        cols = pl.ds(pl.multiple_of(t * 256, 256), 256)
        terms = jnp.dot(hidden[some, :], weights[:, cols], preferred_element_type=jnp.float32).astype(jnp.bfloat16)
        for i, out in enumerate(outs):
            out[:, cols] = terms[i * half : (i + 1) * half]


def add(came, own, *refs):
    out = refs[-1]
    out[...] = (came[...].astype(jnp.float32) + own[...].astype(jnp.float32)).astype(jnp.bfloat16)


def z_sum(own, one, two, *outs):
    rows = outs[0].shape[0]
    for k, out in enumerate(outs):
        at = pl.ds(k * rows, rows)
        total = own[at, :].astype(jnp.float32) + one[at, :].astype(jnp.float32) + two[at, :].astype(jnp.float32)
        out[...] = total.astype(out.dtype)


def finish(stream, mine, one, two, three, out):
    total = stream[...] + mine[...]
    for ref in (one, two, three):
        total = total + ref[...].astype(jnp.float32)
    out[...] = total.astype(jnp.bfloat16)


def shards(
    hidden_rows,
    queries,
    cache_keys,
    cache_values,
    new_keys,
    new_values,
    lengths,
    norm_gain,
    w_gate,
    w_up,
    w_down,
):
    f32, bf16 = jnp.float32, jnp.bfloat16
    rows, feats = hidden_rows.shape
    width = w_gate.shape[1]
    piece = rows * NX
    total = piece * NZ
    block = total // (NY * NC)
    wide = 2 * width + MARKS
    per = feats // HEAD_DIM
    idx = jnp.stack([lax.axis_index(a) for a in ("x", "z", "y", "core")]).astype(jnp.int32)
    given = [lengths, hidden_rows, queries, cache_keys, cache_values, new_keys, new_values, norm_gain.reshape(per, HEAD_DIM)]
    stream, inv_gain2, scaled = call(
        functools.partial(start_rows, HEAD_DIM ** (-0.5)),
        [shape(rows, feats, kind=f32), shape(per, HEAD_DIM, kind=f32), shape(rows, feats)],
        given,
        "h" * 8,
        scratch=[pltpu.SMEM(lengths.shape, jnp.int32)]
        + [pltpu.VMEM(v.shape, v.dtype) for v in given[1:]]
        + [pltpu.VMEM((rows * per, HEAD_DIM), f32)] * 2
        + [pltpu.VMEM((rows * per, HEAD_DIM), bf16)]
        + [pltpu.SemaphoreType.DMA((8,))],
        moved=4 * cache_keys.size,
        limit=60 * MIB,
    )

    own, inv_gain2 = call(
        seat, [shape(piece, feats), shape(per, HEAD_DIM, kind=f32)], [scaled, inv_gain2], "vv", moved=2 * rows * feats
    )
    from_x = {k: shift(scaled, "x", k, NX) for k in AWAY}
    own = call(
        join,
        shape(piece, feats),
        [own] + [from_x[k] for k in SLOTS[1:]],
        "v" * NX,
        moved=4 * piece * feats,
        alias={0: 0},
    )
    pieces = {0: own}
    up = down = own
    for step in range(1, NZ // 2):
        up = shift(up, "z", 1, NZ)
        down = shift(down, "z", -1, NZ)
        pieces[-step], pieces[step] = up, down

    def gates(some, after):
        size = sum(v.shape[0] for v in some)
        return call(
            functools.partial(gate_matmul, width),
            [shape(size // 2, wide)] * 2 + [shape(size, feats), shape(8, 128, kind=f32)],
            [idx] + some + [after, inv_gain2, w_gate],
            "s" + "v" * len(some) + "hvv",
            flops=2 * size * feats * width,
            moved=2 * feats * width,
        )

    def ups(keep, send, part, after):
        return call(
            functools.partial(up_matmul, width),
            [shape(*keep.shape)] * 2,
            [after, part, w_up, keep, send],
            "hvvvv",
            flops=2 * part.size * width,
            moved=2 * feats * width,
            alias={3: 0, 4: 1},
        )

    keep, send, part, done = gates([pieces[j] for j in ORDER[:EARLY]], pieces[2])
    up, down = call(halves, [shape(piece // 2, feats)] * 2, [up, down, done], "vvh", moved=4 * piece * feats)
    late = [pieces[j] for j in ORDER[EARLY:-1]]
    size = (NZ - EARLY) * piece
    keep, send = ups(keep, send, part, up)
    later, send_later, send = call(
        functools.partial(middle_matmul, width),
        [shape(size // 2, wide)] * 2 + [shape(*send.shape)],
        [idx] + late + [send, inv_gain2, w_gate, w_up],
        "s" + "v" * (len(late) + 4),
        scratch=[pltpu.VMEM((size - piece, feats), bf16)],
        flops=4 * (size - piece) * feats * width,
        moved=4 * feats * width,
        alias={1 + len(late): 2},
    )
    up = shift(up, "z", 1, NZ)
    down = shift(down, "z", -1, NZ)

    def across(keep, send):
        came = shift(send, "core", 1, NC)
        own, *parts = call(
            functools.partial(core_sum, block // 2),
            [shape(block // 2, wide, kind=f32)] + [shape(block // 2, wide)] * (NY - 1),
            [idx, keep, came],
            "svv",
            moved=2 * total * wide,
        )
        got = {k: shift(parts[k - 1], "y", k, NY) for k in AWAY}
        return [own] + [got[k] for k in range(1, NY)]

    early = across(keep, send)
    later, send_later = call(
        functools.partial(last_matmul, width),
        [shape(size // 2, wide)] * 2,
        [idx, up, down, inv_gain2, w_gate, w_up, later, send_later],
        "svvvvvvv",
        scratch=[pltpu.VMEM((piece, feats), bf16)],
        flops=4 * piece * feats * width,
        moved=4 * feats * width,
        alias={6: 0, 7: 1},
    )
    late = across(later, send_later)
    hidden = call(functools.partial(activate, width), shape(block, width), early + late, "v" * 2 * NY, moved=10 * block * wide)
    same = {0: hidden, **{k: shift(hidden, "y", k, NY) for k in AWAY}}
    other = {k: shift(v, "core", 1, NC) for k, v in same.items()}
    same, other = ([v[k] for k in range(NY)] for v in (same, other))

    def expand(first, last):
        got = call(
            functools.partial(second_matmul, first, last),
            [shape(piece // 2, feats)] * (2 * (last - first)),
            [idx] + same + other + [w_down],
            "s" + "v" * (2 * NY + 1),
            scratch=[pltpu.VMEM((total - first // NY * NY * piece, width), bf16)],
            flops=2 * (last - first) * piece * feats * width,
            moved=2 * feats * width,
        )
        return {j: got[2 * i : 2 * i + 2] for i, j in enumerate(ORDER[first:last])}

    terms = {**expand(FAR, NZ), **expand(0, FAR)}

    def chain(half, way, steps):
        got = terms[way * steps if steps < NZ // 2 else steps][half]
        for step in range(steps, 1, -1):
            got = shift(got, "z", way, NZ)
            own = terms[way * (step - 1)][half]
            after = [terms[0][0]] if step == steps else []
            got = call(add, shape(piece // 2, feats), [got, own] + after, "vvh"[: 2 + len(after)], moved=3 * piece * feats)
        return shift(got, "z", way, NZ)

    far = NZ // 2
    low = [chain(0, -1, far), chain(0, 1, far - 1)]
    high = [chain(1, 1, far), chain(1, -1, far - 1)]
    mine, two = call(
        z_sum, [shape(rows, feats, kind=f32), shape(rows, feats)], [terms[0][0]] + low, "vvv", moved=4 * piece * feats
    )
    one, three = call(z_sum, [shape(rows, feats)] * 2, [terms[0][1]] + high, "vvv", moved=4 * piece * feats)
    sent = {1: one, 2: two, 3: three}
    parts = {k: shift(sent[k], "x", -k, NX) for k in AWAY}
    return call(finish, shape(rows, feats), [stream, mine] + [parts[k] for k in range(1, NX)], "v" * 5, moved=20 * rows * feats)


def solution(mesh):
    fine = Mesh(mesh.devices.reshape(NX, NZ, NY, NC), ("x", "z", "y", "core"))
    pool = ("x", "z")
    placed = (
        P(pool, TP),
        P(pool, TP),
        P(pool, None, TP),
        P(pool, None, TP),
        P(pool, TP),
        P(pool, TP),
        P(pool),
        P(TP),
        P(TP, pool),
        P(TP, pool),
        P(pool, TP),
    )
    return jax.shard_map(shards, mesh=fine, in_specs=placed, out_specs=P(pool, TP), check_vma=False)
```

```python
import functools

import jax
import jax.numpy as jnp
from jax import lax
from jax.experimental import pallas as pl
from jax.experimental.pallas import tpu as pltpu
from jax.sharding import Mesh
from jax.sharding import PartitionSpec as P

D = 16384
HEAD_DIM = 128
NX, NZ, NY, NC = 4, 8, 4, 2
TP = ("y", "core")
MARKS = 128
MIB = 1 << 20
ORDER = (0, -1, 1, -2, 2, -3, 3, 4)
EARLY = 4
FAR = 5
AWAY = (2, 1, 3)
SLOTS = (0, 2, 1, 3)


def shift(v, axis, by, n):
    return lax.ppermute(v, axis, [(i, (i + by) % n) for i in range(n)])


def rows_at(start, count):
    return pl.ds(pl.multiple_of(start, count), count)


def call(kernel, outs, args, kinds, scratch=(), flops=0, moved=0, limit=16 * MIB, alias=None):
    spaces = {"s": pltpu.SMEM, "v": pltpu.VMEM, "h": pltpu.HBM}
    single = not isinstance(outs, (list, tuple))
    whole = [outs] if single else list(outs)
    got = pl.pallas_call(
        kernel,
        out_shape=whole,
        in_specs=[pl.BlockSpec(memory_space=spaces[k]) for k in kinds],
        out_specs=[pl.BlockSpec(memory_space=pltpu.VMEM)] * len(whole),
        scratch_shapes=list(scratch),
        input_output_aliases=alias or {},
        compiler_params=pltpu.CompilerParams(vmem_limit_bytes=limit),
        cost_estimate=pl.CostEstimate(flops=flops, bytes_accessed=moved, transcendentals=0),
    )(*args)
    return got[0] if single else got


def shape(*dims, kind=jnp.bfloat16):
    return jax.ShapeDtypeStruct(dims, kind)


def copy_in(pairs, sems):
    copies = [pltpu.make_async_copy(src, dst, sems.at[i]) for i, (src, dst) in enumerate(pairs)]
    for copy in copies:
        copy.start()
    for copy in copies:
        copy.wait()


def copy_in(pairs, sems):
    copies = [pltpu.make_async_copy(src, dst, sems.at[i]) for i, (src, dst) in enumerate(pairs)]
    for copy in copies:
        copy.start()
    for copy in copies:
        copy.wait()


def start_rows(scale, lengths_in, hidden_in, queries_in, keys_in, values_in, own_keys_in, own_values_in, gain_in, *rest):
    stream, inv_gain2, out, lengths, hidden, queries, keys, values, own_keys, own_values, gain, heads, work, low, sems = rest
    copy_in(
        [
            (queries_in, queries),
            (lengths_in, lengths),
            (keys_in, keys),
            (values_in, values),
            (own_keys_in, own_keys),
            (own_values_in, own_values),
            (hidden_in, hidden),
            (gain_in, gain),
        ],
        sems,
    )
    rows, feats = hidden.shape
    per = feats // HEAD_DIM
    ctx = keys.shape[1]
    f32, bf16 = jnp.float32, jnp.bfloat16
    wide = queries[...].astype(f32)
    for h in range(per):
        heads[pl.ds(h, rows, stride=per), :] = wide[:, h * HEAD_DIM : (h + 1) * HEAD_DIM]
    slot = lax.broadcasted_iota(jnp.int32, (per, ctx), 1)

    def spread(ref):
        each = ref[...].astype(f32)
        return jnp.concatenate(
            [jnp.broadcast_to(each[r : r + 1, :], (per, HEAD_DIM)) for r in range(rows)], axis=0
        )

    for r in range(rows):
        score = lax.dot_general(
            heads[pl.ds(r * per, per), :].astype(bf16),
            keys[r],
            (((1,), (1,)), ((), ())),
            preferred_element_type=f32,
        )
        work[pl.ds(r * per, per), :] = jnp.where(slot < lengths[r], score * scale, -1e30)
    own = jnp.sum(heads[...] * spread(own_keys), axis=1, keepdims=True) * scale
    score = work[...]
    top = jnp.maximum(jnp.max(score, axis=1, keepdims=True), own)
    weight = jnp.exp(score - top)
    own_weight = jnp.exp(own - top)
    total = jnp.sum(weight, axis=1, keepdims=True) + own_weight
    low[...] = weight.astype(bf16)
    for r in range(rows):
        work[pl.ds(r * per, per), :] = jnp.dot(low[pl.ds(r * per, per), :], values[r], preferred_element_type=f32)
    work[...] = (work[...] + own_weight.astype(bf16).astype(f32) * spread(own_values)) / total
    scales = gain[...].astype(f32)
    inv_gain2[...] = 1.0 / (scales * scales)
    for h in range(per):
        cols = slice(h * HEAD_DIM, (h + 1) * HEAD_DIM)
        got = hidden[:, cols].astype(f32) + work[pl.ds(h, rows, stride=per), :]
        stream[:, cols] = got
        out[:, cols] = (got * scales[h : h + 1, :]).astype(bf16)


def seat(own, out):
    out[pl.ds(0, own.shape[0]), :] = own[...]


def join(first, *refs):
    parts, out = refs[:-1], refs[-1]
    size = parts[0].shape[0]
    for k, part in enumerate(parts, 1):
        out[pl.ds(k * size, size), :] = part[...]


def place(core, pieces, part):
    top = part.shape[0] // 2
    for i, piece in enumerate(pieces):
        half = piece.shape[0] // 2
        at = i * half
        part[pl.ds(at, half), :] = piece[rows_at(core * half, half), :]
        part[pl.ds(top + at, half), :] = piece[rows_at((1 - core) * half, half), :]


def squares(width, part, inv_gain2, keep, send, row):
    top = part.shape[0] // 2
    step = 32
    lane = lax.broadcasted_iota(jnp.int32, (step, MARKS), 1)

    def some(start, out, i):
        at = rows_at(start + i * step, step)
        sums = 0.0
        for h in range(part.shape[1] // HEAD_DIM):
            wide = part[at, pl.ds(h * HEAD_DIM, HEAD_DIM)].astype(jnp.float32)
            sums = sums + wide * wide * inv_gain2[pl.ds(h, 1), :]
        sums = jnp.sum(sums, axis=1, keepdims=True)
        high = sums.astype(jnp.bfloat16).astype(jnp.float32)
        marks = jnp.where(lane == 0, high, jnp.where(lane == 1, sums - high, 0.0))
        out[rows_at(row + i * step, step), pl.ds(2 * width, MARKS)] = marks.astype(jnp.bfloat16)

    pl.loop(0, top // step)(lambda i: some(0, keep, i))
    pl.loop(0, top // step)(lambda i: some(top, send, i))


def project(weights, base, part, keep, send, row, wide=256):
    top, width = part.shape[0] // 2, weights.shape[1]
    to = pl.ds(row, top)

    def tile(start, size):
        terms = jnp.dot(part[...], weights[:, pl.ds(start, size)], preferred_element_type=jnp.float32)
        keep[to, pl.ds(base + start, size)] = terms[:top].astype(jnp.bfloat16)
        send[to, pl.ds(base + start, size)] = terms[top:].astype(jnp.bfloat16)

    if width > wide:
        pl.loop(0, width // wide)(lambda t: tile(pl.multiple_of(t * wide, wide), wide))
    if width % wide or width == wide:
        tile((width - 1) // wide * wide, (width - 1) % wide + 1)


def gate_matmul(width, idx, *refs):
    pieces, (_, inv_gain2, w_gate, keep, send, part, done) = refs[:-7], refs[-7:]
    place(idx[3], pieces, part)
    squares(width, part, inv_gain2, keep, send, 0)
    project(w_gate, 0, part, keep, send, 0)
    done[...] = jnp.zeros_like(done)


def up_matmul(width, _, part, w_up, keep_in, send_in, keep, send):
    project(w_up, width, part, keep, send, 0)


def middle_matmul(width, idx, *refs):
    pieces, (_, inv_gain2, w_gate, w_up, keep, send, _, part) = refs[:-8], refs[-8:]
    place(idx[3], pieces, part)
    squares(width, part, inv_gain2, keep, send, 0)
    project(w_gate, 0, part, keep, send, 0)
    project(w_up, width, part, keep, send, 0)


def last_matmul(width, idx, low, high, inv_gain2, w_gate, w_up, keep_in, send_in, keep, send, part):
    core = idx[3]
    half = low.shape[0]
    part[rows_at(core * half, half), :] = low[...]
    part[rows_at((1 - core) * half, half), :] = high[...]
    row = keep.shape[0] - half
    squares(width, part, inv_gain2, keep, send, row)
    project(w_gate, 0, part, keep, send, row, width)
    project(w_up, width, part, keep, send, row, width)


def halves(up, down, _, up_half, down_half):
    size = up_half.shape[0]
    up_half[...] = up[pl.ds(0, size), :]
    down_half[...] = down[pl.ds(size, size), :]


def core_sum(block, idx, keep, came, own, *outs):
    mine = idx[2]

    def summed(y):
        at = rows_at(y * block, block)
        return keep[at, :].astype(jnp.float32) + came[at, :].astype(jnp.float32)

    own[...] = summed(mine)
    for k, out in enumerate(outs, 1):
        out[...] = summed(lax.rem(mine + k, NY)).astype(jnp.bfloat16)


def activate(width, *refs):
    parts, hidden = refs[:-1], refs[-1]
    block = parts[0].shape[0]
    for i in range(2):
        own, one, two, three = parts[i * NY : (i + 1) * NY]
        sums = own[...] + one[...].astype(jnp.float32) + two[...].astype(jnp.float32) + three[...].astype(jnp.float32)
        meansq = jnp.sum(sums[:, 2 * width :], axis=1, keepdims=True) / D
        inv = lax.rsqrt(meansq + 1e-05)
        gate = sums[:, :width] * inv
        up = sums[:, width : 2 * width] * inv
        hidden[pl.ds(i * block, block), :] = (gate / (1.0 + jnp.exp(-gate)) * up).astype(jnp.bfloat16)


def second_matmul(first, last, idx, *refs):
    same, refs = refs[:NY], refs[NY:]
    other, refs = refs[:NY], refs[NY:]
    weights, outs, hidden = refs[0], refs[1:-1], refs[-1]
    mine, core = idx[2], idx[3]
    block = same[0].shape[0]
    half = block // 2
    groups = range(first // NY, 2)
    for k in range(NY):
        y = lax.rem(mine - k + NY, NY)
        for i in groups:
            at = ((i - groups[0]) * NY + y) * block
            hidden[rows_at(at + core * half, half), :] = same[k][pl.ds(i * half, half), :]
            hidden[rows_at(at + (1 - core) * half, half), :] = other[k][pl.ds(i * half, half), :]
    some = pl.ds((first - groups[0] * NY) * block, (last - first) * block)

    @pl.loop(0, weights.shape[1] // 512)
    def _(t):
        cols = pl.ds(pl.multiple_of(t * 512, 512), 512)
        terms = jnp.dot(hidden[some, :], weights[:, cols], preferred_element_type=jnp.float32).astype(jnp.bfloat16)
        for i, out in enumerate(outs):
            out[:, cols] = terms[i * half : (i + 1) * half]


def add(came, own, *refs):
    out = refs[-1]
    out[...] = (came[...].astype(jnp.float32) + own[...].astype(jnp.float32)).astype(jnp.bfloat16)


def z_sum(own, one, two, *outs):
    rows = outs[0].shape[0]
    for k, out in enumerate(outs):
        at = pl.ds(k * rows, rows)
        total = own[at, :].astype(jnp.float32) + one[at, :].astype(jnp.float32) + two[at, :].astype(jnp.float32)
        out[...] = total.astype(out.dtype)


def finish(stream, mine, one, two, three, out):
    total = stream[...] + mine[...]
    for ref in (one, two, three):
        total = total + ref[...].astype(jnp.float32)
    out[...] = total.astype(jnp.bfloat16)


def shards(
    hidden_rows,
    queries,
    cache_keys,
    cache_values,
    new_keys,
    new_values,
    lengths,
    norm_gain,
    w_gate,
    w_up,
    w_down,
):
    f32, bf16 = jnp.float32, jnp.bfloat16
    rows, feats = hidden_rows.shape
    width = w_gate.shape[1]
    piece = rows * NX
    total = piece * NZ
    block = total // (NY * NC)
    wide = 2 * width + MARKS
    per = feats // HEAD_DIM
    idx = jnp.stack([lax.axis_index(a) for a in ("x", "z", "y", "core")]).astype(jnp.int32)
    given = [lengths, hidden_rows, queries, cache_keys, cache_values, new_keys, new_values, norm_gain.reshape(per, HEAD_DIM)]
    stream, inv_gain2, scaled = call(
        functools.partial(start_rows, HEAD_DIM ** (-0.5)),
        [shape(rows, feats, kind=f32), shape(per, HEAD_DIM, kind=f32), shape(rows, feats)],
        given,
        "h" * 8,
        scratch=[pltpu.SMEM(lengths.shape, jnp.int32)]
        + [pltpu.VMEM(v.shape, v.dtype) for v in given[1:]]
        + [pltpu.VMEM((rows * per, HEAD_DIM), f32)] * 2
        + [pltpu.VMEM((rows * per, HEAD_DIM), bf16)]
        + [pltpu.SemaphoreType.DMA((8,))],
        moved=4 * cache_keys.size,
        limit=60 * MIB,
    )

    own = call(seat, shape(piece, feats), [scaled], "v", moved=2 * rows * feats)
    from_x = {k: shift(scaled, "x", k, NX) for k in AWAY}
    own = call(
        join,
        shape(piece, feats),
        [own] + [from_x[k] for k in SLOTS[1:]],
        "v" * NX,
        moved=4 * piece * feats,
        alias={0: 0},
    )
    pieces = {0: own}
    up = down = own
    for step in range(1, NZ // 2):
        up = shift(up, "z", 1, NZ)
        down = shift(down, "z", -1, NZ)
        pieces[-step], pieces[step] = up, down

    def gates(some, after):
        size = sum(v.shape[0] for v in some)
        return call(
            functools.partial(gate_matmul, width),
            [shape(size // 2, wide)] * 2 + [shape(size, feats), shape(8, 128, kind=f32)],
            [idx] + some + [after, inv_gain2, w_gate],
            "s" + "v" * len(some) + "hvv",
            flops=2 * size * feats * width,
            moved=2 * feats * width,
        )

    def ups(keep, send, part, after):
        return call(
            functools.partial(up_matmul, width),
            [shape(*keep.shape)] * 2,
            [after, part, w_up, keep, send],
            "hvvvv",
            flops=2 * part.size * width,
            moved=2 * feats * width,
            alias={3: 0, 4: 1},
        )

    keep, send, part, done = gates([pieces[j] for j in ORDER[:EARLY]], pieces[2])
    up, down = call(halves, [shape(piece // 2, feats)] * 2, [up, down, done], "vvh", moved=4 * piece * feats)
    late = [pieces[j] for j in ORDER[EARLY:-1]]
    size = (NZ - EARLY) * piece
    keep, send = ups(keep, send, part, up)
    later, send_later, send = call(
        functools.partial(middle_matmul, width),
        [shape(size // 2, wide)] * 2 + [shape(*send.shape)],
        [idx] + late + [send, inv_gain2, w_gate, w_up],
        "s" + "v" * (len(late) + 4),
        scratch=[pltpu.VMEM((size - piece, feats), bf16)],
        flops=4 * (size - piece) * feats * width,
        moved=4 * feats * width,
        alias={1 + len(late): 2},
    )
    up = shift(up, "z", 1, NZ)
    down = shift(down, "z", -1, NZ)

    def across(keep, send):
        came = shift(send, "core", 1, NC)
        own, *parts = call(
            functools.partial(core_sum, block // 2),
            [shape(block // 2, wide, kind=f32)] + [shape(block // 2, wide)] * (NY - 1),
            [idx, keep, came],
            "svv",
            moved=2 * total * wide,
        )
        got = {k: shift(parts[k - 1], "y", k, NY) for k in AWAY}
        return [own] + [got[k] for k in range(1, NY)]

    early = across(keep, send)
    later, send_later = call(
        functools.partial(last_matmul, width),
        [shape(size // 2, wide)] * 2,
        [idx, up, down, inv_gain2, w_gate, w_up, later, send_later],
        "svvvvvvv",
        scratch=[pltpu.VMEM((piece, feats), bf16)],
        flops=4 * piece * feats * width,
        moved=4 * feats * width,
        alias={6: 0, 7: 1},
    )
    late = across(later, send_later)
    hidden = call(functools.partial(activate, width), shape(block, width), early + late, "v" * 2 * NY, moved=10 * block * wide)
    same = {0: hidden, **{k: shift(hidden, "y", k, NY) for k in AWAY}}
    other = {k: shift(v, "core", 1, NC) for k, v in same.items()}
    same, other = ([v[k] for k in range(NY)] for v in (same, other))

    def expand(first, last):
        got = call(
            functools.partial(second_matmul, first, last),
            [shape(piece // 2, feats)] * (2 * (last - first)),
            [idx] + same + other + [w_down],
            "s" + "v" * (2 * NY + 1),
            scratch=[pltpu.VMEM((total - first // NY * NY * piece, width), bf16)],
            flops=2 * (last - first) * piece * feats * width,
            moved=2 * feats * width,
        )
        return {j: got[2 * i : 2 * i + 2] for i, j in enumerate(ORDER[first:last])}

    terms = {**expand(FAR, NZ), **expand(0, FAR)}

    def chain(half, way, steps):
        got = terms[way * steps if steps < NZ // 2 else steps][half]
        for step in range(steps, 1, -1):
            got = shift(got, "z", way, NZ)
            own = terms[way * (step - 1)][half]
            after = [terms[0][0]] if step == steps else []
            got = call(add, shape(piece // 2, feats), [got, own] + after, "vvh"[: 2 + len(after)], moved=3 * piece * feats)
        return shift(got, "z", way, NZ)

    far = NZ // 2
    low = [chain(0, -1, far), chain(0, 1, far - 1)]
    high = [chain(1, 1, far), chain(1, -1, far - 1)]
    mine, two = call(
        z_sum, [shape(rows, feats, kind=f32), shape(rows, feats)], [terms[0][0]] + low, "vvv", moved=4 * piece * feats
    )
    one, three = call(z_sum, [shape(rows, feats)] * 2, [terms[0][1]] + high, "vvv", moved=4 * piece * feats)
    sent = {1: one, 2: two, 3: three}
    parts = {k: shift(sent[k], "x", -k, NX) for k in AWAY}
    return call(finish, shape(rows, feats), [stream, mine] + [parts[k] for k in range(1, NX)], "v" * 5, moved=20 * rows * feats)


def solution(mesh):
    fine = Mesh(mesh.devices.reshape(NX, NZ, NY, NC), ("x", "z", "y", "core"))
    pool = ("x", "z")
    placed = (
        P(pool, TP),
        P(pool, TP),
        P(pool, None, TP),
        P(pool, None, TP),
        P(pool, TP),
        P(pool, TP),
        P(pool),
        P(TP),
        P(TP, pool),
        P(TP, pool),
        P(pool, TP),
    )
    return jax.shard_map(shards, mesh=fine, in_specs=placed, out_specs=P(pool, TP), check_vma=False)
```

```python
import functools

import jax
import jax.numpy as jnp
from jax import lax
from jax.experimental import pallas as pl
from jax.experimental.pallas import tpu as pltpu
from jax.sharding import Mesh
from jax.sharding import PartitionSpec as P

D = 16384
HEAD_DIM = 128
NX, NZ, NY, NC = 4, 8, 4, 2
TP = ("y", "core")
MARKS = 128
MIB = 1 << 20
ORDER = (0, -1, 1, -2, 2, -3, 3, 4)
EARLY = 4
FAR = 5
AWAY = (2, 1, 3)


def shift(v, axis, by, n):
    return lax.ppermute(v, axis, [(i, (i + by) % n) for i in range(n)])


def rows_at(start, count):
    return pl.ds(pl.multiple_of(start, count), count)


def call(kernel, outs, args, kinds, scratch=(), flops=0, moved=0, limit=16 * MIB, alias=None):
    spaces = {"s": pltpu.SMEM, "v": pltpu.VMEM, "h": pltpu.HBM}
    single = not isinstance(outs, (list, tuple))
    whole = [outs] if single else list(outs)
    got = pl.pallas_call(
        kernel,
        out_shape=whole,
        in_specs=[pl.BlockSpec(memory_space=spaces[k]) for k in kinds],
        out_specs=[pl.BlockSpec(memory_space=pltpu.VMEM)] * len(whole),
        scratch_shapes=list(scratch),
        input_output_aliases=alias or {},
        compiler_params=pltpu.CompilerParams(vmem_limit_bytes=limit),
        cost_estimate=pl.CostEstimate(flops=flops, bytes_accessed=moved, transcendentals=0),
    )(*args)
    return got[0] if single else got


def shape(*dims, kind=jnp.bfloat16):
    return jax.ShapeDtypeStruct(dims, kind)


def copy_in(pairs, sems):
    copies = [pltpu.make_async_copy(src, dst, sems.at[i]) for i, (src, dst) in enumerate(pairs)]
    for copy in copies:
        copy.start()
    for copy in copies:
        copy.wait()


def copy_in(pairs, sems):
    copies = [pltpu.make_async_copy(src, dst, sems.at[i]) for i, (src, dst) in enumerate(pairs)]
    for copy in copies:
        copy.start()
    for copy in copies:
        copy.wait()


def start_rows(scale, lengths_in, hidden_in, queries_in, keys_in, values_in, own_keys_in, own_values_in, gain_in, *rest):
    stream, inv_gain2, out, lengths, hidden, queries, keys, values, own_keys, own_values, gain, heads, work, low, sems = rest
    copy_in(
        [
            (queries_in, queries),
            (lengths_in, lengths),
            (keys_in, keys),
            (values_in, values),
            (own_keys_in, own_keys),
            (own_values_in, own_values),
            (hidden_in, hidden),
            (gain_in, gain),
        ],
        sems,
    )
    rows, feats = hidden.shape
    per = feats // HEAD_DIM
    ctx = keys.shape[1]
    f32, bf16 = jnp.float32, jnp.bfloat16
    wide = queries[...].astype(f32)
    for h in range(per):
        heads[pl.ds(h, rows, stride=per), :] = wide[:, h * HEAD_DIM : (h + 1) * HEAD_DIM]
    slot = lax.broadcasted_iota(jnp.int32, (per, ctx), 1)

    def spread(ref):
        each = ref[...].astype(f32)
        return jnp.concatenate(
            [jnp.broadcast_to(each[r : r + 1, :], (per, HEAD_DIM)) for r in range(rows)], axis=0
        )

    for r in range(rows):
        score = lax.dot_general(
            heads[pl.ds(r * per, per), :].astype(bf16),
            keys[r],
            (((1,), (1,)), ((), ())),
            preferred_element_type=f32,
        )
        work[pl.ds(r * per, per), :] = jnp.where(slot < lengths[r], score * scale, -1e30)
    own = jnp.sum(heads[...] * spread(own_keys), axis=1, keepdims=True) * scale
    score = work[...]
    top = jnp.maximum(jnp.max(score, axis=1, keepdims=True), own)
    weight = jnp.exp(score - top)
    own_weight = jnp.exp(own - top)
    total = jnp.sum(weight, axis=1, keepdims=True) + own_weight
    low[...] = weight.astype(bf16)
    for r in range(rows):
        work[pl.ds(r * per, per), :] = jnp.dot(low[pl.ds(r * per, per), :], values[r], preferred_element_type=f32)
    work[...] = (work[...] + own_weight.astype(bf16).astype(f32) * spread(own_values)) / total
    scales = gain[...].astype(f32)
    inv_gain2[...] = 1.0 / (scales * scales)
    for h in range(per):
        cols = slice(h * HEAD_DIM, (h + 1) * HEAD_DIM)
        got = hidden[:, cols].astype(f32) + work[pl.ds(h, rows, stride=per), :]
        stream[:, cols] = got
        out[:, cols] = (got * scales[h : h + 1, :]).astype(bf16)


def seat(own, out):
    out[pl.ds(0, own.shape[0]), :] = own[...]


def join(first, *refs):
    parts, out = refs[:-1], refs[-1]
    size = parts[0].shape[0]
    for k, part in enumerate(parts, 1):
        out[pl.ds(k * size, size), :] = part[...]


def place(core, pieces, part):
    top = part.shape[0] // 2
    for i, piece in enumerate(pieces):
        half = piece.shape[0] // 2
        at = i * half
        part[pl.ds(at, half), :] = piece[rows_at(core * half, half), :]
        part[pl.ds(top + at, half), :] = piece[rows_at((1 - core) * half, half), :]


def squares(width, part, inv_gain2, keep, send, row):
    top = part.shape[0] // 2
    step = next(n for n in (64, 48, 32) if top % n == 0)
    lane = lax.broadcasted_iota(jnp.int32, (step, MARKS), 1)

    def some(start, out, i):
        at = pl.ds(pl.multiple_of(start + i * step, 16), step)
        sums = 0.0
        for h in range(part.shape[1] // HEAD_DIM):
            wide = part[at, pl.ds(h * HEAD_DIM, HEAD_DIM)].astype(jnp.float32)
            sums = sums + wide * wide * inv_gain2[pl.ds(h, 1), :]
        sums = jnp.sum(sums, axis=1, keepdims=True)
        high = sums.astype(jnp.bfloat16).astype(jnp.float32)
        marks = jnp.where(lane == 0, high, jnp.where(lane == 1, sums - high, 0.0))
        out[pl.ds(pl.multiple_of(row + i * step, 16), step), pl.ds(2 * width, MARKS)] = marks.astype(jnp.bfloat16)

    pl.loop(0, top // step)(lambda i: some(0, keep, i))
    pl.loop(0, top // step)(lambda i: some(top, send, i))


def project(weights, base, part, keep, send, row, wide=256):
    top, width = part.shape[0] // 2, weights.shape[1]
    to = pl.ds(row, top)

    def tile(start, size):
        terms = jnp.dot(part[...], weights[:, pl.ds(start, size)], preferred_element_type=jnp.float32)
        keep[to, pl.ds(base + start, size)] = terms[:top].astype(jnp.bfloat16)
        send[to, pl.ds(base + start, size)] = terms[top:].astype(jnp.bfloat16)

    if width > wide:
        pl.loop(0, width // wide)(lambda t: tile(pl.multiple_of(t * wide, wide), wide))
    if width % wide or width == wide:
        tile((width - 1) // wide * wide, (width - 1) % wide + 1)


def gate_matmul(width, idx, *refs):
    pieces, (_, inv_gain2, w_gate, keep, send, part, done) = refs[:-7], refs[-7:]
    place(idx[3], pieces, part)
    squares(width, part, inv_gain2, keep, send, 0)
    project(w_gate, 0, part, keep, send, 0)
    done[...] = jnp.zeros_like(done)


def up_matmul(width, _, part, w_up, keep_in, send_in, keep, send):
    project(w_up, width, part, keep, send, 0)


def middle_matmul(width, idx, *refs):
    pieces, (_, inv_gain2, w_gate, w_up, keep, send, _, part) = refs[:-8], refs[-8:]
    place(idx[3], pieces, part)
    squares(width, part, inv_gain2, keep, send, 0)
    project(w_gate, 0, part, keep, send, 0)
    project(w_up, width, part, keep, send, 0)


def last_matmul(width, idx, low, high, inv_gain2, w_gate, w_up, keep_in, send_in, keep, send, part):
    core = idx[3]
    half = low.shape[0]
    part[rows_at(core * half, half), :] = low[...]
    part[rows_at((1 - core) * half, half), :] = high[...]
    row = keep.shape[0] - half
    squares(width, part, inv_gain2, keep, send, row)
    project(w_gate, 0, part, keep, send, row, width)
    project(w_up, width, part, keep, send, row, width)


def halves(up, down, _, up_half, down_half):
    size = up_half.shape[0]
    up_half[...] = up[pl.ds(0, size), :]
    down_half[...] = down[pl.ds(size, size), :]


def core_sum(block, idx, keep, came, own, *outs):
    mine = idx[2]

    def summed(y):
        at = rows_at(y * block, block)
        return keep[at, :].astype(jnp.float32) + came[at, :].astype(jnp.float32)

    own[...] = summed(mine)
    for k, out in enumerate(outs, 1):
        out[...] = summed(lax.rem(mine + k, NY)).astype(jnp.bfloat16)


def activate(width, *refs):
    parts, hidden = refs[:-1], refs[-1]
    block = parts[0].shape[0]
    for i in range(2):
        own, one, two, three = parts[i * NY : (i + 1) * NY]
        sums = own[...] + one[...].astype(jnp.float32) + two[...].astype(jnp.float32) + three[...].astype(jnp.float32)
        meansq = jnp.sum(sums[:, 2 * width :], axis=1, keepdims=True) / D
        inv = lax.rsqrt(meansq + 1e-05)
        gate = sums[:, :width] * inv
        up = sums[:, width : 2 * width] * inv
        hidden[pl.ds(i * block, block), :] = (gate / (1.0 + jnp.exp(-gate)) * up).astype(jnp.bfloat16)


def second_matmul(first, last, idx, *refs):
    same, refs = refs[:NY], refs[NY:]
    other, refs = refs[:NY], refs[NY:]
    weights, outs, hidden = refs[0], refs[1:-1], refs[-1]
    mine, core = idx[2], idx[3]
    block = same[0].shape[0]
    half = block // 2
    groups = range(first // NY, 2)
    for k in range(NY):
        y = lax.rem(mine - k + NY, NY)
        for i in groups:
            at = ((i - groups[0]) * NY + y) * block
            hidden[rows_at(at + core * half, half), :] = same[k][pl.ds(i * half, half), :]
            hidden[rows_at(at + (1 - core) * half, half), :] = other[k][pl.ds(i * half, half), :]
    some = pl.ds((first - groups[0] * NY) * block, (last - first) * block)

    @pl.loop(0, weights.shape[1] // 512)
    def _(t):
        cols = pl.ds(pl.multiple_of(t * 512, 512), 512)
        terms = jnp.dot(hidden[some, :], weights[:, cols], preferred_element_type=jnp.float32).astype(jnp.bfloat16)
        for i, out in enumerate(outs):
            out[:, cols] = terms[i * half : (i + 1) * half]


def add(came, own, *refs):
    out = refs[-1]
    out[...] = (came[...].astype(jnp.float32) + own[...].astype(jnp.float32)).astype(jnp.bfloat16)


def z_sum(own, one, two, *outs):
    rows = outs[0].shape[0]
    for k, out in enumerate(outs):
        at = pl.ds(k * rows, rows)
        total = own[at, :].astype(jnp.float32) + one[at, :].astype(jnp.float32) + two[at, :].astype(jnp.float32)
        out[...] = total.astype(out.dtype)


def finish(stream, mine, one, two, three, out):
    total = stream[...] + mine[...]
    for ref in (one, two, three):
        total = total + ref[...].astype(jnp.float32)
    out[...] = total.astype(jnp.bfloat16)


def shards(
    hidden_rows,
    queries,
    cache_keys,
    cache_values,
    new_keys,
    new_values,
    lengths,
    norm_gain,
    w_gate,
    w_up,
    w_down,
):
    f32, bf16 = jnp.float32, jnp.bfloat16
    rows, feats = hidden_rows.shape
    width = w_gate.shape[1]
    piece = rows * NX
    total = piece * NZ
    block = total // (NY * NC)
    wide = 2 * width + MARKS
    per = feats // HEAD_DIM
    idx = jnp.stack([lax.axis_index(a) for a in ("x", "z", "y", "core")]).astype(jnp.int32)
    given = [lengths, hidden_rows, queries, cache_keys, cache_values, new_keys, new_values, norm_gain.reshape(per, HEAD_DIM)]
    stream, inv_gain2, scaled = call(
        functools.partial(start_rows, HEAD_DIM ** (-0.5)),
        [shape(rows, feats, kind=f32), shape(per, HEAD_DIM, kind=f32), shape(rows, feats)],
        given,
        "h" * 8,
        scratch=[pltpu.SMEM(lengths.shape, jnp.int32)]
        + [pltpu.VMEM(v.shape, v.dtype) for v in given[1:]]
        + [pltpu.VMEM((rows * per, HEAD_DIM), f32)] * 2
        + [pltpu.VMEM((rows * per, HEAD_DIM), bf16)]
        + [pltpu.SemaphoreType.DMA((8,))],
        moved=4 * cache_keys.size,
        limit=60 * MIB,
    )

    own = call(seat, shape(piece, feats), [scaled], "v", moved=2 * rows * feats)
    from_x = {k: shift(scaled, "x", k, NX) for k in AWAY}
    own = call(
        join,
        shape(piece, feats),
        [own] + [from_x[k] for k in range(1, NX)],
        "v" * NX,
        moved=4 * piece * feats,
        alias={0: 0},
    )
    pieces = {0: own}
    up = down = own
    for step in range(1, NZ // 2):
        up = shift(up, "z", 1, NZ)
        down = shift(down, "z", -1, NZ)
        pieces[-step], pieces[step] = up, down

    def gates(some, after):
        size = sum(v.shape[0] for v in some)
        return call(
            functools.partial(gate_matmul, width),
            [shape(size // 2, wide)] * 2 + [shape(size, feats), shape(8, 128, kind=f32)],
            [idx] + some + [after, inv_gain2, w_gate],
            "s" + "v" * len(some) + "hvv",
            flops=2 * size * feats * width,
            moved=2 * feats * width,
        )

    def ups(keep, send, part, after):
        return call(
            functools.partial(up_matmul, width),
            [shape(*keep.shape)] * 2,
            [after, part, w_up, keep, send],
            "hvvvv",
            flops=2 * part.size * width,
            moved=2 * feats * width,
            alias={3: 0, 4: 1},
        )

    keep, send, part, done = gates([pieces[j] for j in ORDER[:EARLY]], pieces[2])
    up, down = call(halves, [shape(piece // 2, feats)] * 2, [up, down, done], "vvh", moved=4 * piece * feats)
    late = [pieces[j] for j in ORDER[EARLY:-1]]
    size = (NZ - EARLY) * piece
    keep, send = ups(keep, send, part, up)
    later, send_later, send = call(
        functools.partial(middle_matmul, width),
        [shape(size // 2, wide)] * 2 + [shape(*send.shape)],
        [idx] + late + [send, inv_gain2, w_gate, w_up],
        "s" + "v" * (len(late) + 4),
        scratch=[pltpu.VMEM((size - piece, feats), bf16)],
        flops=4 * (size - piece) * feats * width,
        moved=4 * feats * width,
        alias={1 + len(late): 2},
    )
    up = shift(up, "z", 1, NZ)
    down = shift(down, "z", -1, NZ)

    def across(keep, send):
        came = shift(send, "core", 1, NC)
        own, *parts = call(
            functools.partial(core_sum, block // 2),
            [shape(block // 2, wide, kind=f32)] + [shape(block // 2, wide)] * (NY - 1),
            [idx, keep, came],
            "svv",
            moved=2 * total * wide,
        )
        got = {k: shift(parts[k - 1], "y", k, NY) for k in AWAY}
        return [own] + [got[k] for k in range(1, NY)]

    early = across(keep, send)
    later, send_later = call(
        functools.partial(last_matmul, width),
        [shape(size // 2, wide)] * 2,
        [idx, up, down, inv_gain2, w_gate, w_up, later, send_later],
        "svvvvvvv",
        scratch=[pltpu.VMEM((piece, feats), bf16)],
        flops=4 * piece * feats * width,
        moved=4 * feats * width,
        alias={6: 0, 7: 1},
    )
    late = across(later, send_later)
    hidden = call(functools.partial(activate, width), shape(block, width), early + late, "v" * 2 * NY, moved=10 * block * wide)
    same = {0: hidden, **{k: shift(hidden, "y", k, NY) for k in AWAY}}
    other = {k: shift(v, "core", 1, NC) for k, v in same.items()}
    same, other = ([v[k] for k in range(NY)] for v in (same, other))

    def expand(first, last):
        got = call(
            functools.partial(second_matmul, first, last),
            [shape(piece // 2, feats)] * (2 * (last - first)),
            [idx] + same + other + [w_down],
            "s" + "v" * (2 * NY + 1),
            scratch=[pltpu.VMEM((total - first // NY * NY * piece, width), bf16)],
            flops=2 * (last - first) * piece * feats * width,
            moved=2 * feats * width,
        )
        return {j: got[2 * i : 2 * i + 2] for i, j in enumerate(ORDER[first:last])}

    terms = {**expand(FAR, NZ), **expand(0, FAR)}

    def chain(half, way, steps):
        got = terms[way * steps if steps < NZ // 2 else steps][half]
        for step in range(steps, 1, -1):
            got = shift(got, "z", way, NZ)
            own = terms[way * (step - 1)][half]
            after = [terms[0][0]] if step == steps else []
            got = call(add, shape(piece // 2, feats), [got, own] + after, "vvh"[: 2 + len(after)], moved=3 * piece * feats)
        return shift(got, "z", way, NZ)

    far = NZ // 2
    low = [chain(0, -1, far), chain(0, 1, far - 1)]
    high = [chain(1, 1, far), chain(1, -1, far - 1)]
    mine, one = call(
        z_sum, [shape(rows, feats, kind=f32), shape(rows, feats)], [terms[0][0]] + low, "vvv", moved=4 * piece * feats
    )
    two, three = call(z_sum, [shape(rows, feats)] * 2, [terms[0][1]] + high, "vvv", moved=4 * piece * feats)
    sent = {1: one, 2: two, 3: three}
    parts = {k: shift(sent[k], "x", -k, NX) for k in AWAY}
    return call(finish, shape(rows, feats), [stream, mine] + [parts[k] for k in range(1, NX)], "v" * 5, moved=20 * rows * feats)


def solution(mesh):
    fine = Mesh(mesh.devices.reshape(NX, NZ, NY, NC), ("x", "z", "y", "core"))
    pool = ("x", "z")
    placed = (
        P(pool, TP),
        P(pool, TP),
        P(pool, None, TP),
        P(pool, None, TP),
        P(pool, TP),
        P(pool, TP),
        P(pool),
        P(TP),
        P(TP, pool),
        P(TP, pool),
        P(pool, TP),
    )
    return jax.shard_map(shards, mesh=fine, in_specs=placed, out_specs=P(pool, TP), check_vma=False)
```

```python
import functools

import jax
import jax.numpy as jnp
from jax import lax
from jax.experimental import pallas as pl
from jax.experimental.pallas import tpu as pltpu
from jax.sharding import Mesh
from jax.sharding import PartitionSpec as P

D = 16384
HEAD_DIM = 128
NX, NZ, NY, NC = 4, 8, 4, 2
TP = ("y", "core")
MARKS = 128
MIB = 1 << 20
ORDER = (0, -1, 1, -2, 2, -3, 3, 4)
EARLY = 4
FAR = 5
AWAY = (2, 1, 3)
SLOTS = (0, 2, 1, 3)


def shift(v, axis, by, n):
    return lax.ppermute(v, axis, [(i, (i + by) % n) for i in range(n)])


def rows_at(start, count):
    return pl.ds(pl.multiple_of(start, count), count)


def call(kernel, outs, args, kinds, scratch=(), flops=0, moved=0, limit=16 * MIB, alias=None):
    spaces = {"s": pltpu.SMEM, "v": pltpu.VMEM, "h": pltpu.HBM}
    single = not isinstance(outs, (list, tuple))
    whole = [outs] if single else list(outs)
    got = pl.pallas_call(
        kernel,
        out_shape=whole,
        in_specs=[pl.BlockSpec(memory_space=spaces[k]) for k in kinds],
        out_specs=[pl.BlockSpec(memory_space=pltpu.VMEM)] * len(whole),
        scratch_shapes=list(scratch),
        input_output_aliases=alias or {},
        compiler_params=pltpu.CompilerParams(vmem_limit_bytes=limit),
        cost_estimate=pl.CostEstimate(flops=flops, bytes_accessed=moved, transcendentals=0),
    )(*args)
    return got[0] if single else got


def shape(*dims, kind=jnp.bfloat16):
    return jax.ShapeDtypeStruct(dims, kind)


def copy_in(pairs, sems):
    copies = [pltpu.make_async_copy(src, dst, sems.at[i]) for i, (src, dst) in enumerate(pairs)]
    for copy in copies:
        copy.start()
    for copy in copies:
        copy.wait()


def copy_in(pairs, sems):
    copies = [pltpu.make_async_copy(src, dst, sems.at[i]) for i, (src, dst) in enumerate(pairs)]
    for copy in copies:
        copy.start()
    for copy in copies:
        copy.wait()


def start_rows(scale, lengths_in, hidden_in, queries_in, keys_in, values_in, own_keys_in, own_values_in, gain_in, *rest):
    stream, inv_gain2, out, lengths, hidden, queries, keys, values, own_keys, own_values, gain, heads, work, low, sems = rest
    copy_in(
        [
            (queries_in, queries),
            (lengths_in, lengths),
            (keys_in, keys),
            (values_in, values),
            (own_keys_in, own_keys),
            (own_values_in, own_values),
            (hidden_in, hidden),
            (gain_in, gain),
        ],
        sems,
    )
    rows, feats = hidden.shape
    per = feats // HEAD_DIM
    ctx = keys.shape[1]
    f32, bf16 = jnp.float32, jnp.bfloat16
    wide = queries[...].astype(f32)
    for h in range(per):
        heads[pl.ds(h, rows, stride=per), :] = wide[:, h * HEAD_DIM : (h + 1) * HEAD_DIM]
    slot = lax.broadcasted_iota(jnp.int32, (per, ctx), 1)

    def spread(ref):
        each = ref[...].astype(f32)
        return jnp.concatenate(
            [jnp.broadcast_to(each[r : r + 1, :], (per, HEAD_DIM)) for r in range(rows)], axis=0
        )

    for r in range(rows):
        score = lax.dot_general(
            heads[pl.ds(r * per, per), :].astype(bf16),
            keys[r],
            (((1,), (1,)), ((), ())),
            preferred_element_type=f32,
        )
        work[pl.ds(r * per, per), :] = jnp.where(slot < lengths[r], score * scale, -1e30)
    own = jnp.sum(heads[...] * spread(own_keys), axis=1, keepdims=True) * scale
    score = work[...]
    top = jnp.maximum(jnp.max(score, axis=1, keepdims=True), own)
    weight = jnp.exp(score - top)
    own_weight = jnp.exp(own - top)
    total = jnp.sum(weight, axis=1, keepdims=True) + own_weight
    low[...] = weight.astype(bf16)
    for r in range(rows):
        work[pl.ds(r * per, per), :] = jnp.dot(low[pl.ds(r * per, per), :], values[r], preferred_element_type=f32)
    work[...] = (work[...] + own_weight.astype(bf16).astype(f32) * spread(own_values)) / total
    scales = gain[...].astype(f32)
    inv_gain2[...] = 1.0 / (scales * scales)
    for h in range(per):
        cols = slice(h * HEAD_DIM, (h + 1) * HEAD_DIM)
        got = hidden[:, cols].astype(f32) + work[pl.ds(h, rows, stride=per), :]
        stream[:, cols] = got
        out[:, cols] = (got * scales[h : h + 1, :]).astype(bf16)


def seat(own, out):
    out[pl.ds(0, own.shape[0]), :] = own[...]


def join(first, *refs):
    parts, out = refs[:-1], refs[-1]
    size = parts[0].shape[0]
    for k, part in enumerate(parts, 1):
        out[pl.ds(SLOTS[k] * size, size), :] = part[...]


def place(core, pieces, part):
    top = part.shape[0] // 2
    for i, piece in enumerate(pieces):
        half = piece.shape[0] // 2
        at = i * half
        part[pl.ds(at, half), :] = piece[rows_at(core * half, half), :]
        part[pl.ds(top + at, half), :] = piece[rows_at((1 - core) * half, half), :]


def squares(width, part, inv_gain2, keep, send, row):
    top = part.shape[0] // 2
    step = next(n for n in (64, 48, 32) if top % n == 0)
    lane = lax.broadcasted_iota(jnp.int32, (step, MARKS), 1)

    def some(start, out, i):
        at = pl.ds(pl.multiple_of(start + i * step, 16), step)
        sums = 0.0
        for h in range(part.shape[1] // HEAD_DIM):
            wide = part[at, pl.ds(h * HEAD_DIM, HEAD_DIM)].astype(jnp.float32)
            sums = sums + wide * wide * inv_gain2[pl.ds(h, 1), :]
        sums = jnp.sum(sums, axis=1, keepdims=True)
        high = sums.astype(jnp.bfloat16).astype(jnp.float32)
        marks = jnp.where(lane == 0, high, jnp.where(lane == 1, sums - high, 0.0))
        out[pl.ds(pl.multiple_of(row + i * step, 16), step), pl.ds(2 * width, MARKS)] = marks.astype(jnp.bfloat16)

    pl.loop(0, top // step)(lambda i: some(0, keep, i))
    pl.loop(0, top // step)(lambda i: some(top, send, i))


def project(weights, base, part, keep, send, row, wide=256):
    top, width = part.shape[0] // 2, weights.shape[1]
    to = pl.ds(row, top)

    def tile(start, size):
        terms = jnp.dot(part[...], weights[:, pl.ds(start, size)], preferred_element_type=jnp.float32)
        keep[to, pl.ds(base + start, size)] = terms[:top].astype(jnp.bfloat16)
        send[to, pl.ds(base + start, size)] = terms[top:].astype(jnp.bfloat16)

    if width > wide:
        pl.loop(0, width // wide)(lambda t: tile(pl.multiple_of(t * wide, wide), wide))
    if width % wide or width == wide:
        tile((width - 1) // wide * wide, (width - 1) % wide + 1)


def gate_matmul(width, idx, *refs):
    pieces, (_, inv_gain2, w_gate, keep, send, part, done) = refs[:-7], refs[-7:]
    place(idx[3], pieces, part)
    squares(width, part, inv_gain2, keep, send, 0)
    project(w_gate, 0, part, keep, send, 0)
    done[...] = jnp.zeros_like(done)


def up_matmul(width, _, part, w_up, keep_in, send_in, keep, send):
    project(w_up, width, part, keep, send, 0)


def middle_matmul(width, idx, *refs):
    pieces, (_, inv_gain2, w_gate, w_up, keep, send, _, part) = refs[:-8], refs[-8:]
    place(idx[3], pieces, part)
    squares(width, part, inv_gain2, keep, send, 0)
    project(w_gate, 0, part, keep, send, 0)
    project(w_up, width, part, keep, send, 0)


def last_matmul(width, idx, low, high, inv_gain2, w_gate, w_up, keep_in, send_in, keep, send, part):
    core = idx[3]
    half = low.shape[0]
    part[rows_at(core * half, half), :] = low[...]
    part[rows_at((1 - core) * half, half), :] = high[...]
    row = keep.shape[0] - half
    squares(width, part, inv_gain2, keep, send, row)
    project(w_gate, 0, part, keep, send, row, width)
    project(w_up, width, part, keep, send, row, width)


def halves(up, down, _, up_half, down_half):
    size = up_half.shape[0]
    up_half[...] = up[pl.ds(0, size), :]
    down_half[...] = down[pl.ds(size, size), :]


def core_sum(block, idx, keep, came, own, *outs):
    mine = idx[2]

    def summed(y):
        at = rows_at(y * block, block)
        return keep[at, :].astype(jnp.float32) + came[at, :].astype(jnp.float32)

    own[...] = summed(mine)
    for k, out in enumerate(outs, 1):
        out[...] = summed(lax.rem(mine + k, NY)).astype(jnp.bfloat16)


def activate(width, *refs):
    parts, hidden = refs[:-1], refs[-1]
    block = parts[0].shape[0]
    for i in range(2):
        own, one, two, three = parts[i * NY : (i + 1) * NY]
        sums = own[...] + one[...].astype(jnp.float32) + two[...].astype(jnp.float32) + three[...].astype(jnp.float32)
        meansq = jnp.sum(sums[:, 2 * width :], axis=1, keepdims=True) / D
        inv = lax.rsqrt(meansq + 1e-05)
        gate = sums[:, :width] * inv
        up = sums[:, width : 2 * width] * inv
        hidden[pl.ds(i * block, block), :] = (gate / (1.0 + jnp.exp(-gate)) * up).astype(jnp.bfloat16)


def second_matmul(first, last, idx, *refs):
    same, refs = refs[:NY], refs[NY:]
    other, refs = refs[:NY], refs[NY:]
    weights, outs, hidden = refs[0], refs[1:-1], refs[-1]
    mine, core = idx[2], idx[3]
    block = same[0].shape[0]
    half = block // 2
    groups = range(first // NY, 2)
    for k in range(NY):
        y = lax.rem(mine - k + NY, NY)
        for i in groups:
            at = ((i - groups[0]) * NY + y) * block
            hidden[rows_at(at + core * half, half), :] = same[k][pl.ds(i * half, half), :]
            hidden[rows_at(at + (1 - core) * half, half), :] = other[k][pl.ds(i * half, half), :]
    some = pl.ds((first - groups[0] * NY) * block, (last - first) * block)

    @pl.loop(0, weights.shape[1] // 512)
    def _(t):
        cols = pl.ds(pl.multiple_of(t * 512, 512), 512)
        terms = jnp.dot(hidden[some, :], weights[:, cols], preferred_element_type=jnp.float32).astype(jnp.bfloat16)
        for i, out in enumerate(outs):
            out[:, cols] = terms[i * half : (i + 1) * half]


def add(came, own, *refs):
    out = refs[-1]
    out[...] = (came[...].astype(jnp.float32) + own[...].astype(jnp.float32)).astype(jnp.bfloat16)


def z_sum(own, one, two, *outs):
    rows = outs[0].shape[0]
    for k, out in enumerate(outs):
        at = pl.ds(k * rows, rows)
        total = own[at, :].astype(jnp.float32) + one[at, :].astype(jnp.float32) + two[at, :].astype(jnp.float32)
        out[...] = total.astype(out.dtype)


def finish(stream, mine, one, two, three, out):
    total = stream[...] + mine[...]
    for ref in (one, two, three):
        total = total + ref[...].astype(jnp.float32)
    out[...] = total.astype(jnp.bfloat16)


def shards(
    hidden_rows,
    queries,
    cache_keys,
    cache_values,
    new_keys,
    new_values,
    lengths,
    norm_gain,
    w_gate,
    w_up,
    w_down,
):
    f32, bf16 = jnp.float32, jnp.bfloat16
    rows, feats = hidden_rows.shape
    width = w_gate.shape[1]
    piece = rows * NX
    total = piece * NZ
    block = total // (NY * NC)
    wide = 2 * width + MARKS
    per = feats // HEAD_DIM
    idx = jnp.stack([lax.axis_index(a) for a in ("x", "z", "y", "core")]).astype(jnp.int32)
    given = [lengths, hidden_rows, queries, cache_keys, cache_values, new_keys, new_values, norm_gain.reshape(per, HEAD_DIM)]
    stream, inv_gain2, scaled = call(
        functools.partial(start_rows, HEAD_DIM ** (-0.5)),
        [shape(rows, feats, kind=f32), shape(per, HEAD_DIM, kind=f32), shape(rows, feats)],
        given,
        "h" * 8,
        scratch=[pltpu.SMEM(lengths.shape, jnp.int32)]
        + [pltpu.VMEM(v.shape, v.dtype) for v in given[1:]]
        + [pltpu.VMEM((rows * per, HEAD_DIM), f32)] * 2
        + [pltpu.VMEM((rows * per, HEAD_DIM), bf16)]
        + [pltpu.SemaphoreType.DMA((8,))],
        moved=4 * cache_keys.size,
        limit=60 * MIB,
    )

    own = call(seat, shape(piece, feats), [scaled], "v", moved=2 * rows * feats)
    from_x = {k: shift(scaled, "x", k, NX) for k in AWAY}
    own = call(
        join,
        shape(piece, feats),
        [own] + [from_x[k] for k in range(1, NX)],
        "v" * NX,
        moved=4 * piece * feats,
        alias={0: 0},
    )
    pieces = {0: own}
    up = down = own
    for step in range(1, NZ // 2):
        up = shift(up, "z", 1, NZ)
        down = shift(down, "z", -1, NZ)
        pieces[-step], pieces[step] = up, down

    def gates(some, after):
        size = sum(v.shape[0] for v in some)
        return call(
            functools.partial(gate_matmul, width),
            [shape(size // 2, wide)] * 2 + [shape(size, feats), shape(8, 128, kind=f32)],
            [idx] + some + [after, inv_gain2, w_gate],
            "s" + "v" * len(some) + "hvv",
            flops=2 * size * feats * width,
            moved=2 * feats * width,
        )

    def ups(keep, send, part, after):
        return call(
            functools.partial(up_matmul, width),
            [shape(*keep.shape)] * 2,
            [after, part, w_up, keep, send],
            "hvvvv",
            flops=2 * part.size * width,
            moved=2 * feats * width,
            alias={3: 0, 4: 1},
        )

    keep, send, part, done = gates([pieces[j] for j in ORDER[:EARLY]], pieces[2])
    up, down = call(halves, [shape(piece // 2, feats)] * 2, [up, down, done], "vvh", moved=4 * piece * feats)
    late = [pieces[j] for j in ORDER[EARLY:-1]]
    size = (NZ - EARLY) * piece
    keep, send = ups(keep, send, part, up)
    later, send_later, send = call(
        functools.partial(middle_matmul, width),
        [shape(size // 2, wide)] * 2 + [shape(*send.shape)],
        [idx] + late + [send, inv_gain2, w_gate, w_up],
        "s" + "v" * (len(late) + 4),
        scratch=[pltpu.VMEM((size - piece, feats), bf16)],
        flops=4 * (size - piece) * feats * width,
        moved=4 * feats * width,
        alias={1 + len(late): 2},
    )
    up = shift(up, "z", 1, NZ)
    down = shift(down, "z", -1, NZ)

    def across(keep, send):
        came = shift(send, "core", 1, NC)
        own, *parts = call(
            functools.partial(core_sum, block // 2),
            [shape(block // 2, wide, kind=f32)] + [shape(block // 2, wide)] * (NY - 1),
            [idx, keep, came],
            "svv",
            moved=2 * total * wide,
        )
        got = {k: shift(parts[k - 1], "y", k, NY) for k in AWAY}
        return [own] + [got[k] for k in range(1, NY)]

    early = across(keep, send)
    later, send_later = call(
        functools.partial(last_matmul, width),
        [shape(size // 2, wide)] * 2,
        [idx, up, down, inv_gain2, w_gate, w_up, later, send_later],
        "svvvvvvv",
        scratch=[pltpu.VMEM((piece, feats), bf16)],
        flops=4 * piece * feats * width,
        moved=4 * feats * width,
        alias={6: 0, 7: 1},
    )
    late = across(later, send_later)
    hidden = call(functools.partial(activate, width), shape(block, width), early + late, "v" * 2 * NY, moved=10 * block * wide)
    same = {0: hidden, **{k: shift(hidden, "y", k, NY) for k in AWAY}}
    other = {k: shift(v, "core", 1, NC) for k, v in same.items()}
    same, other = ([v[k] for k in range(NY)] for v in (same, other))

    def expand(first, last):
        got = call(
            functools.partial(second_matmul, first, last),
            [shape(piece // 2, feats)] * (2 * (last - first)),
            [idx] + same + other + [w_down],
            "s" + "v" * (2 * NY + 1),
            scratch=[pltpu.VMEM((total - first // NY * NY * piece, width), bf16)],
            flops=2 * (last - first) * piece * feats * width,
            moved=2 * feats * width,
        )
        return {j: got[2 * i : 2 * i + 2] for i, j in enumerate(ORDER[first:last])}

    terms = {**expand(FAR, NZ), **expand(0, FAR)}

    def chain(half, way, steps):
        got = terms[way * steps if steps < NZ // 2 else steps][half]
        for step in range(steps, 1, -1):
            got = shift(got, "z", way, NZ)
            own = terms[way * (step - 1)][half]
            after = [terms[0][0]] if step == steps else []
            got = call(add, shape(piece // 2, feats), [got, own] + after, "vvh"[: 2 + len(after)], moved=3 * piece * feats)
        return shift(got, "z", way, NZ)

    far = NZ // 2
    low = [chain(0, -1, far), chain(0, 1, far - 1)]
    high = [chain(1, 1, far), chain(1, -1, far - 1)]
    mine, two = call(
        z_sum, [shape(rows, feats, kind=f32), shape(rows, feats)], [terms[0][0]] + low, "vvv", moved=4 * piece * feats
    )
    one, three = call(z_sum, [shape(rows, feats)] * 2, [terms[0][1]] + high, "vvv", moved=4 * piece * feats)
    sent = {1: one, 2: two, 3: three}
    parts = {k: shift(sent[k], "x", -k, NX) for k in AWAY}
    return call(finish, shape(rows, feats), [stream, mine] + [parts[k] for k in range(1, NX)], "v" * 5, moved=20 * rows * feats)


def solution(mesh):
    fine = Mesh(mesh.devices.reshape(NX, NZ, NY, NC), ("x", "z", "y", "core"))
    pool = ("x", "z")
    placed = (
        P(pool, TP),
        P(pool, TP),
        P(pool, None, TP),
        P(pool, None, TP),
        P(pool, TP),
        P(pool, TP),
        P(pool),
        P(TP),
        P(TP, pool),
        P(TP, pool),
        P(pool, TP),
    )
    return jax.shard_map(shards, mesh=fine, in_specs=placed, out_specs=P(pool, TP), check_vma=False)
```
